32 devices in a mesh: tensor: 4 (over y, core), dp: 8 (over z, x).
Axes of the slice: x: 2, y: 2, z: 4, core: 2. Of those that a mesh axis runs over, the one named last changes fastest.
Arguments:
- hidden: bfloat16 [8192, 1536], P('dp'), may hold values from -6 to 6
- segments: int32 [8192], P('dp'), may hold values from 0 to 31, never falling along the last dimension, each value on 1 to 512 neighbouring positions
- norm_gain: float32 [2, 1536], replicated, may hold values from 0.5 to 1.5
- w_z: bfloat16 [2, 1536, 3072], P(None, 'dp', 'tensor'), may hold values from -0.15625 to 0.15625
- w_x: bfloat16 [2, 1536, 3072], P(None, 'dp', 'tensor'), may hold values from -0.15625 to 0.15625
- w_bc: bfloat16 [2, 1536, 256], P(None, 'dp'), may hold values from -0.15625 to 0.15625
- w_dt: bfloat16 [2, 1536, 48], P(None, 'dp', 'tensor'), may hold values from -0.15625 to 0.15625
- conv_x_w: float32 [2, 4, 3072], P(None, None, 'tensor'), may hold values from -3 to 3
- conv_x_b: float32 [2, 3072], P(None, 'tensor'), may hold values from -3 to 3
- conv_bc_w: float32 [2, 4, 256], replicated, may hold values from -3 to 3
- conv_bc_b: float32 [2, 256], replicated, may hold values from -3 to 3
- dt_bias: float32 [2, 48], P(None, 'tensor'), may hold values from -6 to -2
- a_log: float32 [2, 48], P(None, 'tensor'), may hold values from 0 to 2.77
- d_skip: float32 [2, 48], P(None, 'tensor'), may hold values from 0.5 to 1.5
- gated_gain: float32 [2, 3072], P(None, 'tensor'), may hold values from 0.5 to 1.5
- w_out: bfloat16 [2, 1536, 3072], P(None, 'dp', 'tensor'), may hold values from -0.109375 to 0.109375
- cotangent: bfloat16 [8192, 1536], P('dp'), may hold values from -6 to 6
Outputs:
- mixed: bfloat16 [8192, 1536], P('dp')
- d_hidden: float32 [8192, 1536], P('dp')
- d_norm_gain: float32 [2, 1536], replicated
- d_w_z: float32 [2, 1536, 3072], P(None, 'dp', 'tensor')
- d_w_x: float32 [2, 1536, 3072], P(None, 'dp', 'tensor')
- d_w_bc: float32 [2, 1536, 256], P(None, 'dp', 'tensor')
- d_w_dt: float32 [2, 1536, 48], P(None, 'dp', 'tensor')
- d_conv_x_w: float32 [2, 4, 3072], P(None, None, 'tensor')
- d_conv_x_b: float32 [2, 3072], P(None, 'tensor')
- d_conv_bc_w: float32 [2, 4, 256], replicated
- d_conv_bc_b: float32 [2, 256], replicated
- d_dt_bias: float32 [2, 48], P(None, 'tensor')
- d_a_log: float32 [2, 48], P(None, 'tensor')
- d_d_skip: float32 [2, 48], P(None, 'tensor')
- d_gated_gain: float32 [2, 3072], P(None, 'tensor')
- d_w_out: float32 [2, 1536, 3072], P(None, 'dp', 'tensor')
The draws below stay inside these ranges and needn't reach their ends.
Inputs may be any that keep to these rules, and one draw needn't show every extreme that they name: `segments`: segment numbers never fall along the tokens; a segment holds 1 to 512 tokens.
All inputs are finite; a program needn't handle non-finite values.
Results may differ from the reference program's by a relative error of at most 0.02.
Values may be sent and summed in bfloat16 or wider, within the bound.
No kernel may reach another device: no remote copies, remote signals or barrier semaphores. Data moves between devices by JAX's collectives and lax.ppermute only.
A program may use at most 256 MiB of HBM per device.

```python
import math
import jax
import jax.numpy as jnp
import numpy as np
from jax import lax

D = 1536
HEADS = 48
HEAD_DIM = 64
STATE = 128
CONV = 4
PACK = 1024
LAYERS = 2
INNER = 3072
TOKENS = 8192


def steps_of(rng, dims, cuts, least, largest):
    def one(dim, parts):
        draws = jax.random.uniform(jax.random.fold_in(jax.random.fold_in(rng, 6), dim), (parts,), jnp.float32, least / len(cuts), largest / len(cuts))
        return jnp.repeat(jnp.exp(draws), dims[dim] // parts).reshape((-1,) + (1,) * (len(dims) - dim - 1))

    loudness = one(*cuts[0])
    for cut in cuts[1:]:
        loudness = loudness * one(*cut)
    return loudness


def length_profile(number_of, total, bound, skew):
    loads = [(1 << 20) // math.isqrt(grade ** skew) + 1 for grade in range(2, number_of + 1)]
    spare, given = total - bound - (number_of - 1), [1] * (number_of - 1)
    while spare > 0:
        movable = [i for i in range(number_of - 1) if given[i] < bound]
        pool, remaining = sum([loads[i] for i in movable]), spare
        for i in movable:
            addition = min(bound - given[i], max(1, remaining * loads[i] // pool), spare)
            given[i] = given[i] + addition
            spare = spare - addition
    return np.array([bound] + given)


def ragged_sizes(own_key, amount, total, bound, skew):
    if amount == 2:
        one = jax.random.randint(own_key, (), max(1, total - bound), min(bound, total - 1) + 1)
        return jnp.stack([one, total - one])
    tallies = jnp.asarray(length_profile(amount, total, bound, skew), jnp.int32)
    pairs = (amount - 1) // 2
    donor, receiver = tallies[1:1 + 2 * pairs:2], tallies[2:2 + 2 * pairs:2]
    slack = jnp.minimum(donor - 1, bound - receiver)
    passed = jax.random.randint(jax.random.fold_in(own_key, 1), (pairs,), 0, 1 << 20) % (slack + 1)
    tallies = tallies.at[1:1 + 2 * pairs:2].set(donor - passed).at[2:2 + 2 * pairs:2].set(receiver + passed)
    return tallies[jax.random.permutation(jax.random.fold_in(own_key, 2), amount)]


def normal_values(stream_key, dims, deviation, limit, cuts=(), kind=jnp.bfloat16):
    values = deviation * jax.random.normal(stream_key, dims, jnp.float32)
    if cuts:
        values = values * steps_of(stream_key, dims, cuts, -0.22, 0.18)
    return jnp.clip(values, -limit, limit).astype(kind)


def setup_inputs(seed: int = 0) -> dict:
    key_of = jax.random.split(jax.random.key(seed), 18)
    hidden = normal_values(key_of[0], (TOKENS, D), 1.0, 6.0, ((0, 8),))
    segments = jnp.searchsorted(jnp.cumsum(ragged_sizes(key_of[1], TOKENS // (PACK // 4), TOKENS, PACK // 2, 0)), jnp.arange(TOKENS), side="right").astype(jnp.int32)
    norm_gain = jnp.clip(1.0 + 0.1 * jax.random.normal(key_of[2], (LAYERS, D), jnp.float32), 0.5, 1.5)
    w_z = normal_values(key_of[3], (LAYERS, D, INNER), D ** -0.5, 0.15625, ((1, 8), (2, 4)))
    w_x = normal_values(key_of[4], (LAYERS, D, INNER), D ** -0.5, 0.15625, ((1, 8), (2, 4)))
    w_bc = normal_values(key_of[5], (LAYERS, D, 2 * STATE), D ** -0.5, 0.15625, ((1, 8),))
    w_dt = normal_values(key_of[6], (LAYERS, D, HEADS), D ** -0.5, 0.15625, ((1, 8), (2, 4)))
    conv_x_w = normal_values(key_of[7], (LAYERS, CONV, INNER), CONV ** -0.5, 3.0, ((2, 4),), jnp.float32)
    conv_x_b = normal_values(key_of[8], (LAYERS, INNER), 0.5, 3.0, ((1, 4),), jnp.float32)
    conv_bc_w = normal_values(key_of[9], (LAYERS, CONV, 2 * STATE), CONV ** -0.5, 3.0, (), jnp.float32)
    conv_bc_b = normal_values(key_of[10], (LAYERS, 2 * STATE), 0.5, 3.0, (), jnp.float32)
    dt_bias = jnp.clip(-6.0 + 4.0 * jax.random.uniform(key_of[11], (LAYERS, HEADS), jnp.float32) ** steps_of(key_of[11], (LAYERS, HEADS), ((1, 4),), -0.2, 0.2), -6.0, -2.0)
    a_log = jnp.clip(2.77 * jax.random.uniform(key_of[12], (LAYERS, HEADS), jnp.float32) ** steps_of(key_of[12], (LAYERS, HEADS), ((1, 4),), -0.2, 0.2), 0.0, 2.77)
    d_skip = jnp.clip(0.5 + 1.0 * jax.random.uniform(key_of[13], (LAYERS, HEADS), jnp.float32) ** steps_of(key_of[13], (LAYERS, HEADS), ((1, 4),), -0.2, 0.2), 0.5, 1.5)
    gated_gain = jnp.clip(1.0 + 0.1 * jax.random.normal(key_of[14], (LAYERS, INNER), jnp.float32), 0.5, 1.5)
    w_out = normal_values(key_of[15], (LAYERS, D, INNER), INNER ** -0.5, 0.109375, ((1, 8), (2, 4)))
    cotangent = normal_values(key_of[16], (TOKENS, D), 1.0, 6.0, ((0, 8),))
    return dict(hidden=hidden, segments=segments, norm_gain=norm_gain, w_z=w_z, w_x=w_x, w_bc=w_bc, w_dt=w_dt, conv_x_w=conv_x_w, conv_x_b=conv_x_b, conv_bc_w=conv_bc_w, conv_bc_b=conv_bc_b, dt_bias=dt_bias, a_log=a_log, d_skip=d_skip, gated_gain=gated_gain, w_out=w_out, cotangent=cotangent)


EPSILON = 1e-05
PRECISE = lax.Precision.HIGHEST

@jax.custom_vjp
def low(v):
    return lax.optimization_barrier(v.astype(jnp.bfloat16)).astype(jnp.float32)

@jax.custom_vjp
def low_back(v):
    return v

def low_keep(v):
    return (low(v), None)

def low_pass(kept, grad):
    return (grad,)

def back_keep(v):
    return (v, None)

def back_low(kept, grad):
    return (low(grad),)
low.defvjp(low_keep, low_pass)
low_back.defvjp(back_keep, back_low)

def matmul(lhs_mat, rhs_mat):
    return jnp.dot(lhs_mat, rhs_mat, precision=PRECISE, preferred_element_type=jnp.float32)

def rms_scale(values, gain):
    return values * lax.rsqrt(lax.optimization_barrier(jnp.mean(values * values, -1, keepdims=True)) + EPSILON) * gain

def causal_conv(values, weight, bias_row, doc_ids):
    length = values.shape[0]
    summed = bias_row + weight[0] * values
    for offset in range(1, weight.shape[0]):
        moved_rows = jnp.concatenate([jnp.zeros((offset, values.shape[1]), values.dtype), values[:length - offset]], 0)
        moved_doc = jnp.concatenate([jnp.full((offset,), -1, jnp.int32), doc_ids[:length - offset]], 0)
        kept_mask = (moved_doc == doc_ids).astype(values.dtype)
        summed = summed + weight[offset] * moved_rows * kept_mask[:, None]
    return summed

def ssd_reference(heads_x, dt_vals, decay_rates, b_matrix, c_matrix, doc_ids):

    def one_pack(pieces):
        pack_x, pack_dt, pack_b, pack_c, pack_doc = pieces
        log_decay = jnp.cumsum(pack_dt * decay_rates, 0)
        order_idx = jnp.arange(pack_doc.shape[0])
        visible = (pack_doc[:, None] == pack_doc[None, :]) & (order_idx[:, None] >= order_idx[None, :])
        log_gap = log_decay[:, None, :] - log_decay[None, :, :]
        weights = jnp.exp(jnp.where(visible[:, :, None], log_gap, -10000.0))
        intersection = matmul(pack_c, pack_b.T)
        return jnp.einsum('tsh,shp->thp', weights * intersection[:, :, None], pack_x * pack_dt[:, :, None], precision=PRECISE)
    pack_count = heads_x.shape[0] // PACK
    shaped = (heads_x.reshape(pack_count, PACK, heads_x.shape[1], heads_x.shape[2]), dt_vals.reshape(pack_count, PACK, dt_vals.shape[1]), b_matrix.reshape(pack_count, PACK, b_matrix.shape[1]), c_matrix.reshape(pack_count, PACK, c_matrix.shape[1]), doc_ids.reshape(pack_count, PACK))
    return lax.map(jax.checkpoint(one_pack), shaped).reshape(heads_x.shape)

def mamba_layer(stream, doc_ids, params):
    gain_now, weight_z, weight_x, weight_bc, weight_dt, conv_xw, conv_xb, conv_bcw, conv_bcb, bias_dt, log_rate, skip_now, gain_gated, weight_out = params
    length = stream.shape[0]
    normed = low(rms_scale(stream, gain_now))
    gate_pre = low_back(matmul(normed, weight_z))
    x_pre = low_back(matmul(normed, weight_x))
    bc_pre = low_back(matmul(normed, weight_bc))
    dt_pre = low_back(matmul(normed, weight_dt))
    x_conv = jax.nn.silu(causal_conv(x_pre, conv_xw, conv_xb, doc_ids))
    bc_conv = jax.nn.silu(causal_conv(bc_pre, conv_bcw, conv_bcb, doc_ids))
    dt_vals = jax.nn.softplus(dt_pre + bias_dt)
    decay_rates = -jnp.exp(log_rate)
    heads_x = x_conv.reshape(length, HEADS, HEAD_DIM)
    scanned = ssd_reference(heads_x, dt_vals, decay_rates, bc_conv[:, :STATE], bc_conv[:, STATE:], doc_ids)
    scanned = scanned + skip_now[None, :, None] * heads_x
    gated = scanned.reshape(length, INNER) * jax.nn.silu(gate_pre)
    scaled = low(rms_scale(gated, gain_gated))
    branch = low_back(matmul(scaled, weight_out.T))
    return stream + branch

def reference(hidden, segments, norm_gain, w_z, w_x, w_bc, w_dt, conv_x_w, conv_x_b, conv_bc_w, conv_bc_b, dt_bias, a_log, d_skip, gated_gain, w_out, cotangent):
    length = segments.shape[0]
    position = jnp.arange(length, dtype=jnp.int32)
    previous = jnp.concatenate([jnp.full((1,), -1, jnp.int32), segments[:-1]], 0)
    starts = (position % PACK == 0) | (segments != previous)
    doc_ids = jnp.cumsum(starts.astype(jnp.int32)).astype(jnp.int32)
    params = tuple((param.astype(jnp.float32) for param in (norm_gain, w_z, w_x, w_bc, w_dt, conv_x_w, conv_x_b, conv_bc_w, conv_bc_b, dt_bias, a_log, d_skip, gated_gain, w_out)))

    def forward(stream, *layer_params):
        for layer_idx in range(LAYERS):
            stream = mamba_layer(stream, doc_ids, tuple((param[layer_idx] for param in layer_params)))
        return stream
    result, pullback = jax.vjp(forward, hidden.astype(jnp.float32), *params)
    gradients = pullback(cotangent.astype(jnp.float32))
    return (result.astype(jnp.bfloat16), gradients[0], gradients[1], gradients[2], gradients[3], gradients[4], gradients[5], gradients[6], gradients[7], gradients[8], gradients[9], gradients[10], gradients[11], gradients[12], gradients[13], gradients[14])
```

```python
import jax
import jax.numpy as jnp
from jax import lax
from jax.sharding import PartitionSpec as P
from jax.experimental import pallas as pl
from jax.experimental.pallas import tpu as pltpu

HEAD_DIM = 64
STATE = 128
PACK = 1024
LAYERS = 2
INNER = 3072
EPSILON = 1e-05
CHUNK = 128
LANES = 128
GROUP = 16
TAIL = 8
FAR = -10000.0
PRECISE = lax.Precision.HIGHEST
BF16 = jnp.bfloat16
F32 = jnp.float32
VMEM_BYTES = 48 * 1024 * 1024


def mm(lhs, rhs, precision=None):
    return lax.dot_general(
        lhs, rhs, (((1,), (0,)), ((), ())), precision=precision, preferred_element_type=F32
    )


def mm_t(lhs, rhs):
    return lax.dot_general(lhs, rhs, (((1,), (1,)), ((), ())), preferred_element_type=F32)


def t_mm(lhs, rhs):
    return lax.dot_general(lhs, rhs, (((0,), (0,)), ((), ())), preferred_element_type=F32)


def iota(shape, dim):
    return lax.broadcasted_iota(jnp.int32, shape, dim)


def expand(values, spread):
    lane = iota(values.shape, 1)
    high = values.astype(BF16).astype(F32)
    parts = jnp.where(lane < GROUP, high, jnp.where(lane < 2 * GROUP, values - high, 0.0))
    return mm(parts.astype(BF16), spread)


def shifted_back(joined, offset):
    return joined[TAIL - offset : TAIL - offset + CHUNK]


def conv_pre(joined, taps, bias_row, aux):
    summed = bias_row + taps[0:1] * joined[TAIL:]
    for offset in range(1, 4):
        summed = summed + taps[offset : offset + 1] * (
            shifted_back(joined, offset) * aux[:, offset : offset + 1]
        )
    return summed


def halves_rows(tile, low_lanes):
    zero = jnp.zeros_like(tile)
    return jnp.concatenate(
        [jnp.where(low_lanes, tile, zero), jnp.where(low_lanes, zero, tile)], 0
    )


def step_values(dt_ref, head_ref):
    raw = dt_ref + head_ref[0:1]
    dt = jnp.maximum(raw, 0.0) + jnp.log1p(jnp.exp(-jnp.abs(raw)))
    row = iota((CHUNK, CHUNK), 0)
    col = iota((CHUNK, CHUNK), 1)
    lower = (row >= col).astype(F32)
    log_decay = mm(lower, dt * head_ref[1:2], PRECISE)
    return raw, dt, log_decay, row, col


def scan_fwd_kernel(
    with_cross,
    x_ref,
    bcdt_ref,
    gate_ref,
    aux_ref,
    seg_ref,
    taps_ref,
    bias_ref,
    bc_taps_ref,
    bc_bias_ref,
    head_ref,
    skip_ref,
    gain_ref,
    spread_ref,
    *rest,
):
    if with_cross:
        gs_ref, u_ref, y_ref, sq_ref, kept_ref, state, tail_x, tail_bc = rest
    else:
        u_ref, y_ref, sq_ref, kept_ref, state, tail_x, tail_bc = rest
    width = x_ref.shape[1]

    @pl.when(pl.program_id(0) == 0)
    def _():
        state[...] = jnp.zeros_like(state)
        tail_x[...] = jnp.zeros_like(tail_x)
        tail_bc[...] = jnp.zeros_like(tail_bc)

    aux = aux_ref[...]
    bc_now = bcdt_ref[:, : 2 * STATE]
    joined_bc = jnp.concatenate([tail_bc[...], bc_now], 0)
    tail_bc[...] = bc_now[CHUNK - TAIL :]
    bc_pre = conv_pre(joined_bc, bc_taps_ref[...], bc_bias_ref[...], aux)
    bc = bc_pre * jax.nn.sigmoid(bc_pre)
    b_low = bc[:, :STATE].astype(BF16)
    c_low = bc[:, STATE:].astype(BF16)
    b_turned = bc[:, :STATE].T.astype(BF16)
    _, dt, log_decay, row, col = step_values(bcdt_ref[:, 2 * STATE :], head_ref)
    log_turned = log_decay.T
    meet = mm_t(c_low, b_low)
    visible = (aux[:, 0:1] == seg_ref[0]) & (row >= col)
    spread = spread_ref[...]
    dt_wide = expand(dt, spread)
    reach = expand(jnp.exp(log_decay) * aux[:, 4:5], spread)
    to_end = expand(jnp.exp(log_decay[CHUNK - 1 :] - log_decay) * aux[:, 5:6], spread)
    state_low = state[...].astype(BF16)
    kept_ref[0] = state_low
    carried = mm(c_low, state_low)
    low_lanes = iota((CHUNK, LANES), 1) < HEAD_DIM
    squares = jnp.zeros((CHUNK, LANES), F32)
    crosses = jnp.zeros((CHUNK, LANES), F32)
    for pair in range(width // LANES):
        at = slice(pair * LANES, (pair + 1) * LANES)
        now = x_ref[:, at]
        joined = jnp.concatenate([tail_x[:, at], now], 0)
        tail_x[:, at] = now[CHUNK - TAIL :]
        pre = conv_pre(joined, taps_ref[:, at], bias_ref[:, at], aux)
        x_conv = pre * jax.nn.sigmoid(pre)
        inputs = x_conv * dt_wide[:, at]
        mats = []
        for head in (2 * pair, 2 * pair + 1):
            gap = log_decay[:, head : head + 1] - log_turned[head : head + 1, :]
            mats.append((jnp.exp(jnp.where(visible, gap, FAR)) * meet).astype(BF16))
        local = mm(jnp.concatenate(mats, 1), halves_rows(inputs.astype(BF16), low_lanes))
        y = local + carried[:, at] * reach[:, at] + skip_ref[:, at] * x_conv
        y_ref[:, at] = y.astype(y_ref.dtype)
        ending = (inputs * to_end[:, at]).astype(BF16)
        state[:, at] = state[:, at] * reach[CHUNK - 1 :, at] + mm(b_turned, ending)
        gate = gate_ref[:, at].astype(F32)
        gated = y * (gate * jax.nn.sigmoid(gate))
        grown = gated * gain_ref[:, at]
        u_ref[:, at] = grown.astype(BF16)
        squares = squares + gated * gated
        if with_cross:
            crosses = crosses + grown * gs_ref[:, at].astype(F32)
    ones = jnp.ones((8, LANES), F32)
    sums = lax.dot_general(
        ones, squares, (((1,), (1,)), ((), ())), precision=PRECISE, preferred_element_type=F32
    )
    if with_cross:
        more = lax.dot_general(
            ones, crosses, (((1,), (1,)), ((), ())), precision=PRECISE, preferred_element_type=F32
        )
        sums = jnp.where(iota((8, CHUNK), 0) == 0, sums, more)
    sq_ref[...] = sums


def whole(shape):
    return pl.BlockSpec(shape, lambda c: (0,) * len(shape))


def scan_fwd(x_pre, bcdt_pre, gate_pre, side, weights, gs=None, y_dtype=F32):
    length, width = x_pre.shape
    chunks = length // CHUNK
    aux, seg_rows = side
    taps, bias, bc_taps, bc_bias, head, skip, gain, spread = weights
    tile = lambda columns: pl.BlockSpec((CHUNK, columns), lambda c: (c, 0))
    in_specs = [
        tile(width),
        tile(bcdt_pre.shape[1]),
        tile(width),
        tile(LANES),
        pl.BlockSpec((1, 1, CHUNK), lambda c: (c, 0, 0)),
    ] + [whole(w.shape) for w in weights]
    args = [x_pre, bcdt_pre, gate_pre, aux, seg_rows, *weights]
    if gs is not None:
        in_specs.append(tile(width))
        args.append(gs)

    def kernel(*refs):
        scan_fwd_kernel(gs is not None, *refs)

    return pl.pallas_call(
        kernel,
        grid=(chunks,),
        in_specs=in_specs,
        out_specs=[
            tile(width),
            tile(width),
            pl.BlockSpec((8, CHUNK), lambda c: (0, c)),
            pl.BlockSpec((1, STATE, width), lambda c: (c, 0, 0)),
        ],
        out_shape=[
            jax.ShapeDtypeStruct((length, width), BF16),
            jax.ShapeDtypeStruct((length, width), y_dtype),
            jax.ShapeDtypeStruct((8, length), F32),
            jax.ShapeDtypeStruct((chunks, STATE, width), BF16),
        ],
        scratch_shapes=[
            pltpu.VMEM((STATE, width), F32),
            pltpu.VMEM((TAIL, width), F32),
            pltpu.VMEM((TAIL, 2 * STATE), F32),
        ],
        compiler_params=pltpu.CompilerParams(vmem_limit_bytes=VMEM_BYTES),
        cost_estimate=pl.CostEstimate(
            flops=16 * length * width * LANES, bytes_accessed=16 * length * width, transcendentals=0
        ),
        name="scan_fwd",
    )(*args)


def gate_bwd_kernel(
    gs_ref, y_ref, gate_ref, col_ref, gain_ref, g_gate_ref, g_y_ref, scaled_ref, d_gain_ref
):
    @pl.when(pl.program_id(0) == 0)
    def _():
        d_gain_ref[...] = jnp.zeros_like(d_gain_ref)

    inv = col_ref[:, 0:1]
    pull = col_ref[:, 1:2]
    for pair in range(gs_ref.shape[1] // LANES):
        at = slice(pair * LANES, (pair + 1) * LANES)
        gs = gs_ref[:, at].astype(F32)
        y = y_ref[:, at].astype(F32)
        gate = gate_ref[:, at].astype(F32)
        sig = jax.nn.sigmoid(gate)
        act = gate * sig
        gated = y * act
        normal = gated * inv
        gain = gain_ref[:, at]
        d_gain_ref[:, at] += jnp.sum(gs * normal, 0, keepdims=True)
        g_gated = inv * (gs * gain) - gated * pull
        scaled_ref[:, at] = (normal * gain).astype(BF16)
        g_y_ref[:, at] = (g_gated * act).astype(BF16)
        g_gate_ref[:, at] = (g_gated * y * sig * (1.0 + gate * (1.0 - sig))).astype(BF16)


def gate_bwd(gs, y, gate_pre, columns, gain, rows=256):
    length, width = gs.shape
    tile = pl.BlockSpec((rows, width), lambda c: (c, 0))
    return pl.pallas_call(
        gate_bwd_kernel,
        grid=(length // rows,),
        in_specs=[
            tile,
            tile,
            tile,
            pl.BlockSpec((rows, columns.shape[1]), lambda c: (c, 0)),
            whole(gain.shape),
        ],
        out_specs=[tile, tile, tile, whole((1, width))],
        out_shape=[jax.ShapeDtypeStruct((length, width), BF16)] * 3
        + [jax.ShapeDtypeStruct((1, width), F32)],
        compiler_params=pltpu.CompilerParams(vmem_limit_bytes=VMEM_BYTES),
        cost_estimate=pl.CostEstimate(
            flops=20 * length * width, bytes_accessed=18 * length * width, transcendentals=0
        ),
        name="gate_bwd",
    )(gs, y, gate_pre, columns, gain)


def conv_bwd(joined, joined_grad, grad, taps, aux, acc_ref, at):
    acc_ref[4:5, at] += jnp.sum(grad, 0, keepdims=True)
    acc_ref[0:1, at] += jnp.sum(grad * joined[TAIL:], 0, keepdims=True)
    result = taps[0:1] * grad
    for offset in range(1, 4):
        moved = shifted_back(joined, offset) * aux[:, offset : offset + 1]
        acc_ref[offset : offset + 1, at] += jnp.sum(grad * moved, 0, keepdims=True)
        later = joined_grad[offset : offset + CHUNK] * aux[:, 5 + offset : 6 + offset]
        result = result + taps[offset : offset + 1] * later
    return result


def scan_bwd_kernel(
    g_ref,
    x_ref,
    x_tail_ref,
    bcdt_ref,
    bc_tail_ref,
    kept_ref,
    aux_ref,
    seg_ref,
    taps_ref,
    bias_ref,
    bc_taps_ref,
    bc_bias_ref,
    head_ref,
    skip_ref,
    gain_ref,
    spread_ref,
    gx_ref,
    gbc_ref,
    gdt_ref,
    accx_ref,
    accbc_ref,
    acch_ref,
    grad_state,
    next_x,
    next_bc,
):
    width = x_ref.shape[1]

    @pl.when(pl.program_id(0) == 0)
    def _():
        grad_state[...] = jnp.zeros_like(grad_state)
        next_x[...] = jnp.zeros_like(next_x)
        next_bc[...] = jnp.zeros_like(next_bc)
        accx_ref[...] = jnp.zeros_like(accx_ref)
        accbc_ref[...] = jnp.zeros_like(accbc_ref)
        acch_ref[...] = jnp.zeros_like(acch_ref)

    aux = aux_ref[...]
    joined_bc = jnp.concatenate([bc_tail_ref[:, : 2 * STATE], bcdt_ref[:, : 2 * STATE]], 0)
    bc_pre = conv_pre(joined_bc, bc_taps_ref[...], bc_bias_ref[...], aux)
    bc_sig = jax.nn.sigmoid(bc_pre)
    bc = bc_pre * bc_sig
    b_low = bc[:, :STATE].astype(BF16)
    c_low = bc[:, STATE:].astype(BF16)
    c_turned = bc[:, STATE:].T.astype(BF16)
    raw, dt, log_decay, row, col = step_values(bcdt_ref[:, 2 * STATE :], head_ref)
    log_turned = log_decay.T
    meet = mm_t(b_low, c_low)
    visible = (aux[:, 0:1] == seg_ref[0]) & (row <= col)
    spread = spread_ref[...]
    dt_wide = expand(dt, spread)
    reach = expand(jnp.exp(log_decay) * aux[:, 4:5], spread)
    to_end = expand(jnp.exp(log_decay[CHUNK - 1 :] - log_decay) * aux[:, 5:6], spread)
    low_lanes = iota((CHUNK, LANES), 1) < HEAD_DIM
    lane = iota((CHUNK, LANES), 1)
    grad_meet = jnp.zeros((CHUNK, CHUNK), F32)
    grad_b = jnp.zeros((CHUNK, STATE), F32)
    grad_c = jnp.zeros((CHUNK, STATE), F32)
    col_sums = jnp.zeros((CHUNK, LANES), F32)
    row_sums = jnp.zeros((LANES, CHUNK), F32)
    head_sums = jnp.zeros((3 * CHUNK, LANES), F32)
    through = jnp.zeros((8, LANES), F32)
    head_row = iota((LANES, CHUNK), 0)
    for pair in range(width // LANES):
        at = slice(pair * LANES, (pair + 1) * LANES)
        joined = jnp.concatenate([x_tail_ref[:, at], x_ref[:, at]], 0)
        pre = conv_pre(joined, taps_ref[:, at], bias_ref[:, at], aux)
        sig = jax.nn.sigmoid(pre)
        x_conv = pre * sig
        inputs = x_conv * dt_wide[:, at]
        g_low = g_ref[:, at]
        g = g_low.astype(F32)
        grad_mats = mm_t(halves_rows(inputs.astype(BF16), low_lanes), g_low)
        mats = []
        for member in range(2):
            head = 2 * pair + member
            gap = log_turned[head : head + 1, :] - log_decay[:, head : head + 1]
            weight = jnp.exp(jnp.where(visible, gap, FAR))
            mats.append((weight * meet).astype(BF16))
            part = weight * grad_mats[member * CHUNK : (member + 1) * CHUNK]
            grad_meet = grad_meet + part
            product = part * meet
            col_sums = jnp.where(lane == head, jnp.sum(product, 1, keepdims=True), col_sums)
            row_sums = jnp.where(head_row == head, jnp.sum(product, 0, keepdims=True), row_sums)
        local = mm(jnp.concatenate(mats, 1), halves_rows(g_low, low_lanes))
        reach_now = reach[:, at]
        to_end_now = to_end[:, at]
        state_low = kept_ref[0, :, at]
        coming = g * reach_now
        coming_low = coming.astype(BF16)
        carried = mm(c_low, state_low)
        grad_c = grad_c + mm_t(coming_low, state_low)
        grad_state_now = grad_state[:, at]
        grad_state_low = grad_state_now.astype(BF16)
        leaving = mm(b_low, grad_state_low)
        ending = inputs * to_end_now
        grad_b = grad_b + mm_t(ending.astype(BF16), grad_state_low)
        last = reach_now[CHUNK - 1 :]
        passed = jnp.sum(grad_state_now * state_low.astype(F32), 0, keepdims=True) * last
        through = through + mm_t(
            jnp.broadcast_to(passed, (8, LANES)).astype(BF16), spread[:, at]
        )
        grad_state[:, at] = grad_state_now * last + mm(c_turned, coming_low)
        grad_inputs = local + leaving * to_end_now
        stacked = jnp.concatenate([coming * carried, ending * leaving, grad_inputs * x_conv], 0)
        head_sums = head_sums + mm_t(stacked.astype(BF16), spread[:, at])
        acch_ref[0:1, at] += jnp.sum(g * x_conv, 0, keepdims=True)
        grad_conv = (grad_inputs * dt_wide[:, at] + g * skip_ref[:, at]) * (
            sig * (1.0 + pre * (1.0 - sig))
        )
        joined_grad = jnp.concatenate([grad_conv, next_x[:, at]], 0)
        next_x[:, at] = grad_conv[:TAIL]
        gx_ref[:, at] = conv_bwd(
            joined, joined_grad, grad_conv, taps_ref[:, at], aux, accx_ref, at
        ).astype(BF16)
    upper = (row <= col).astype(F32)
    strict = (row > col).astype(F32)
    straddle = (
        mm(upper, row_sums.T - col_sums + head_sums[:CHUNK], PRECISE)
        + mm(strict, head_sums[CHUNK : 2 * CHUNK], PRECISE)
        + through[0:1]
    )
    grad_dt = head_sums[2 * CHUNK :] + head_ref[1:2] * straddle
    grad_raw = jnp.where(lane < GROUP, grad_dt * jax.nn.sigmoid(raw), 0.0)
    gdt_ref[...] = grad_raw.astype(BF16)
    acch_ref[1:2, :LANES] += jnp.sum(grad_raw, 0, keepdims=True)
    acch_ref[2:3, :LANES] += jnp.sum(dt * straddle, 0, keepdims=True)
    grad_meet_low = grad_meet.astype(BF16)
    grad_b = grad_b + mm(grad_meet_low, c_low)
    grad_c = grad_c + t_mm(grad_meet_low, b_low)
    grad_bc = jnp.concatenate([grad_b, grad_c], 1) * (bc_sig * (1.0 + bc_pre * (1.0 - bc_sig)))
    joined_grad = jnp.concatenate([grad_bc, next_bc[...]], 0)
    next_bc[...] = grad_bc[:TAIL]
    gbc_ref[...] = conv_bwd(
        joined_bc, joined_grad, grad_bc, bc_taps_ref[...], aux, accbc_ref, slice(None)
    ).astype(BF16)


def scan_bwd(g_y, x_pre, bcdt_pre, kept, side, weights):
    length, width = x_pre.shape
    chunks = length // CHUNK
    aux, seg_rows = side
    back = lambda c: chunks - 1 - c
    tile = lambda columns: pl.BlockSpec((CHUNK, columns), lambda c: (back(c), 0))
    tail = lambda columns: pl.BlockSpec(
        (TAIL, columns), lambda c: (jnp.maximum(back(c) * (CHUNK // TAIL) - 1, 0), 0)
    )
    wide = bcdt_pre.shape[1]
    in_specs = [
        tile(width),
        tile(width),
        tail(width),
        tile(wide),
        tail(wide),
        pl.BlockSpec((1, STATE, width), lambda c: (back(c), 0, 0)),
        tile(LANES),
        pl.BlockSpec((1, 1, CHUNK), lambda c: (back(c), 0, 0)),
    ] + [whole(w.shape) for w in weights]
    return pl.pallas_call(
        scan_bwd_kernel,
        grid=(chunks,),
        in_specs=in_specs,
        out_specs=[
            tile(width),
            tile(2 * STATE),
            tile(LANES),
            whole((8, width)),
            whole((8, 2 * STATE)),
            whole((8, width)),
        ],
        out_shape=[
            jax.ShapeDtypeStruct((length, width), BF16),
            jax.ShapeDtypeStruct((length, 2 * STATE), BF16),
            jax.ShapeDtypeStruct((length, LANES), BF16),
            jax.ShapeDtypeStruct((8, width), F32),
            jax.ShapeDtypeStruct((8, 2 * STATE), F32),
            jax.ShapeDtypeStruct((8, width), F32),
        ],
        scratch_shapes=[
            pltpu.VMEM((STATE, width), F32),
            pltpu.VMEM((TAIL, width), F32),
            pltpu.VMEM((TAIL, 2 * STATE), F32),
        ],
        compiler_params=pltpu.CompilerParams(vmem_limit_bytes=VMEM_BYTES),
        cost_estimate=pl.CostEstimate(
            flops=40 * length * width * LANES, bytes_accessed=16 * length * width, transcendentals=0
        ),
        name="scan_bwd",
    )(g_y, x_pre, x_pre, bcdt_pre, bcdt_pre, kept, aux, seg_rows, *weights)


def side_arrays(segments):
    length = segments.shape[0]
    seg = segments.astype(F32)
    columns = [seg]
    nothing = lambda count: jnp.full((count,), -1.0, F32)
    for offset in range(1, 4):
        moved = jnp.concatenate([nothing(offset), seg[: length - offset]], 0)
        columns.append((moved == seg).astype(F32))
    blocks = seg.reshape(-1, CHUNK)
    ends = blocks[:, -1]
    before = jnp.concatenate([nothing(1), ends[:-1]], 0)
    columns.append((blocks == before[:, None]).astype(F32).reshape(-1))
    columns.append((blocks == ends[:, None]).astype(F32).reshape(-1))
    for offset in range(1, 4):
        moved = jnp.concatenate([seg[offset:], nothing(offset)], 0)
        columns.append((moved == seg).astype(F32))
    stacked = jnp.stack(columns, 1)
    aux = jnp.pad(stacked, ((0, 0), (0, LANES - stacked.shape[1])))
    return aux, blocks.reshape(-1, 1, CHUNK)


def in_groups(values):
    padded = jnp.pad(values, [(0, 0)] * (values.ndim - 1) + [(0, GROUP - values.shape[-1])])
    return jnp.tile(padded, (1,) * (values.ndim - 1) + (LANES // GROUP,))


def spread_matrix(width):
    head = lax.broadcasted_iota(jnp.int32, (LANES, width), 0) % GROUP
    owner = lax.broadcasted_iota(jnp.int32, (LANES, width), 1) // HEAD_DIM
    return (head == owner).astype(BF16)


def scan_weights(taps, bias, bc_taps, bc_bias, dt_bias, a_log, d_skip, gain, spread):
    rates = -jnp.exp(a_log)
    rows = jnp.stack([in_groups(dt_bias), in_groups(rates)])
    head = jnp.pad(rows, ((0, 6), (0, 0)))
    return (
        taps,
        bias[None],
        bc_taps,
        bc_bias[None],
        head,
        jnp.repeat(d_skip, HEAD_DIM)[None],
        gain[None],
        spread,
    )


def partners(count, step):
    return [(index, index ^ step) for index in range(count)]


def swap(values, axis, step):
    return lax.ppermute(values, axis, partners(lax.axis_size(axis), step))


def turn(values, blocks, ahead):
    perm = [
        (2 * block + side, 2 * ((block + ahead) % blocks) + side)
        for block in range(blocks)
        for side in range(2)
    ]
    return lax.ppermute(values, "dp", perm)


def after(values, *earlier):
    return lax.optimization_barrier((values, *earlier))[0]


def gather_rows(own, blocks):
    slots = [own] + [turn(own, blocks, ahead) for ahead in range(1, blocks)]
    across = [swap(slot, "dp", 1) for slot in slots]
    return jnp.concatenate(slots + across, 0), slots[-1]


def scatter_rows(left_part, right_part, blocks):
    height = left_part.shape[0] // blocks
    mine = right_part.astype(F32) + swap(left_part, "dp", 1).astype(F32)
    total = mine[:height]
    low = mine.astype(BF16)
    for ahead in range(1, blocks):
        piece = low[ahead * height : (ahead + 1) * height]
        total = total + turn(piece, blocks, blocks - ahead).astype(F32)
    return total


def weight_grad(rows, grads, blocks):
    width = rows.shape[1] // 2
    dims = (((0,), (0,)), ((), ()))
    sent = lax.dot_general(rows[:, width:], grads, dims, preferred_element_type=F32).astype(BF16)
    kept = lax.dot_general(rows[:, :width], grads, dims, preferred_element_type=F32)
    return scatter_rows(sent, kept, blocks)


class Quarters:
    def __init__(self, length):
        place = lax.axis_index("tensor")
        self.core = place % 2
        self.far = place // 2
        self.half = length // 2
        self.size = length // 4

    def own(self, values):
        start = self.core * self.half + self.far * self.size
        return lax.dynamic_slice_in_dim(values, start, self.size, 0)

    def reduce(self, make):
        sent = make((1 - self.core) * self.half).astype(BF16)
        got = swap(sent, "tensor", 1)
        mine = make(self.core * self.half) + got.astype(F32)
        away = lax.dynamic_slice_in_dim(mine, (1 - self.far) * self.size, self.size, 0)
        got = swap(away.astype(BF16), "tensor", 2)
        near = lax.dynamic_slice_in_dim(mine, self.far * self.size, self.size, 0)
        return near + got.astype(F32)

    def join(self, values):
        got = swap(values, "tensor", 2)
        first = self.far == 0
        half = jnp.concatenate([jnp.where(first, values, got), jnp.where(first, got, values)], 0)
        got = swap(half, "tensor", 1)
        first = self.core == 0
        return jnp.concatenate([jnp.where(first, half, got), jnp.where(first, got, half)], 0)


def tensor_sum(values):
    values = values + swap(values, "tensor", 1)
    return values + swap(values, "tensor", 2)


def dp_sum(values):
    step = 1
    while step < lax.axis_size("dp"):
        values = values + swap(values, "dp", step)
        step = 2 * step
    return values


def dot(lhs, rhs):
    return lax.dot_general(lhs, rhs, (((1,), (0,)), ((), ())), preferred_element_type=F32)


def dot_t(lhs, rhs):
    return lax.dot_general(lhs, rhs, (((1,), (1,)), ((), ())), preferred_element_type=F32)


def turned_order(features, blocks):
    place = lax.axis_index("dp")
    block, side = place // 2, place % 2
    height = features // (2 * blocks)
    index = lax.broadcasted_iota(jnp.int32, (features, features), 1)
    part, within = index // height, index % height
    source_side = lax.rem(side + part // blocks, 2)
    source_block = lax.rem(block + blocks - part % blocks, blocks)
    source = (2 * source_block + source_side) * height + within
    return (lax.broadcasted_iota(jnp.int32, (features, features), 0) == source).astype(BF16)


def on_device(
    hidden,
    segments,
    norm_gain,
    w_z,
    w_x,
    w_bc,
    w_dt,
    conv_x_w,
    conv_x_b,
    conv_bc_w,
    conv_bc_b,
    dt_bias,
    a_log,
    d_skip,
    gated_gain,
    w_out,
    cotangent,
):
    length, features = hidden.shape
    width = w_x.shape[2]
    heads = dt_bias.shape[1]
    blocks = lax.axis_size("dp") // 2
    quarters = Quarters(length)
    order = turned_order(features, blocks)

    w_bcdt = jnp.concatenate([w_bc, in_groups(w_dt)], 2)
    gathered = []
    earlier = None
    for layer in range(LAYERS):
        row = []
        for group in (w_bcdt[layer], w_x[layer], w_z[layer], w_out[layer]):
            if earlier is not None:
                group = after(group, earlier)
            full, earlier = gather_rows(group, blocks)
            row.append(full)
        gathered.append(row)

    side = side_arrays(segments)
    spread = spread_matrix(width)
    weights = [
        scan_weights(
            conv_x_w[layer],
            conv_x_b[layer],
            conv_bc_w[layer],
            conv_bc_b[layer],
            dt_bias[layer],
            a_log[layer],
            d_skip[layer],
            gated_gain[layer],
            spread,
        )
        for layer in range(LAYERS)
    ]
    gains = mm(norm_gain, order.astype(F32), PRECISE)
    hidden_low = dot(hidden, order).astype(BF16)
    cotangent_low = dot(cotangent, order).astype(BF16)

    def rms_of(stream):
        return lax.rsqrt(jnp.mean(stream * stream, -1, keepdims=True) + EPSILON)

    def half_of(values, start):
        return lax.dynamic_slice_in_dim(values, start, quarters.half, 0)

    streams, totals, saved = [], [], []
    stream_full = hidden_low.astype(F32)
    normed = (stream_full * rms_of(stream_full) * gains[0]).astype(BF16)
    stream = quarters.own(hidden_low).astype(F32)
    for layer in range(LAYERS):
        wf_bcdt, wf_x, wf_z, wf_out = gathered[layer]
        bcdt_pre = dot(normed, wf_bcdt)
        x_pre = dot(normed, wf_x)
        gate_pre = dot(normed, wf_z)
        u, y, sq, kept = scan_fwd(x_pre, bcdt_pre, gate_pre, side, weights[layer])
        inv = lax.rsqrt(tensor_sum(sq[0:1]) / INNER + EPSILON)[0]
        total = quarters.reduce(lambda start: dot_t(half_of(u, start), wf_out))
        streams.append(stream)
        totals.append(total)
        saved.append((normed, x_pre, bcdt_pre, gate_pre, u, y, kept, inv))
        stream = stream + quarters.own(inv)[:, None] * total
        if layer + 1 < LAYERS:
            normed_own = (stream * rms_of(stream) * gains[layer + 1]).astype(BF16)
            normed = quarters.join(normed_own)
    mixed = quarters.join(dot_t(stream.astype(BF16), order).astype(BF16))

    grad_low = cotangent_low
    grad_stream = quarters.own(cotangent_low).astype(F32)
    weight_parts = [None] * LAYERS
    small_parts = [None] * LAYERS
    for layer in reversed(range(LAYERS)):
        wf_bcdt, wf_x, wf_z, wf_out = gathered[layer]
        normed, x_pre, bcdt_pre, gate_pre, u, y, kept, inv = saved[layer]
        grad_scaled = dot(grad_low, wf_out)
        if layer + 1 == LAYERS:
            cross = jnp.sum(grad_scaled * u.astype(F32), -1)
            cross = tensor_sum(cross[None])[0]
        else:
            cross = quarters.join(jnp.sum(grad_low_own.astype(F32) * totals[layer], -1))
        columns = jnp.stack([inv, inv * inv * inv * cross / INNER], 1)
        g_gate, g_y, scaled, d_gain = gate_bwd(
            grad_scaled, y, gate_pre, columns, gated_gain[layer][None]
        )
        d_out = weight_grad(grad_low, scaled, blocks)
        d_z = weight_grad(normed, g_gate, blocks)
        g_x, g_bc, g_dt, acc_x, acc_bc, acc_head = scan_bwd(
            g_y, x_pre, bcdt_pre, kept, side, weights[layer]
        )
        d_x = weight_grad(normed, g_x, blocks)
        g_bcdt = jnp.concatenate([g_bc, g_dt], 1)

        def partial_rows(start):
            return (
                dot_t(half_of(g_gate, start), wf_z)
                + dot_t(half_of(g_x, start), wf_x)
                + dot_t(half_of(g_bcdt, start), wf_bcdt)
            )

        grad_normed = quarters.reduce(partial_rows)
        stream = streams[layer]
        rms = rms_of(stream)
        normal = stream * rms
        d_norm = jnp.sum(grad_normed * normal, 0)
        grown = grad_normed * gains[layer]
        grad_stream = grad_stream + rms * (
            grown - normal * jnp.mean(grown * normal, -1, keepdims=True)
        )
        if layer > 0:
            grad_low_own = grad_stream.astype(BF16)
            grad_low = quarters.join(grad_low_own)
        far_cols = lax.dynamic_slice_in_dim(g_bc, (1 - quarters.far) * STATE, STATE, 1)
        near_cols = lax.dynamic_slice_in_dim(g_bc, quarters.far * STATE, STATE, 1)
        bc_sum = near_cols.astype(F32) + swap(far_cols, "tensor", 2).astype(F32)
        bc_sum = bc_sum + swap(bc_sum.astype(BF16), "tensor", 1).astype(F32)
        rolled = jnp.roll(bc_sum, STATE // 2, 1)
        own_bc = jnp.where(quarters.core == 0, bc_sum, rolled)[:, : STATE // 2].astype(BF16)
        own_bcdt = jnp.concatenate([own_bc, g_dt[:, : STATE // 2]], 1)
        d_bcdt = weight_grad(normed, own_bcdt, blocks)
        weight_parts[layer] = (d_z, d_x, d_bcdt, d_out)
        small_parts[layer] = (d_norm, acc_x, acc_bc, acc_head, d_gain)

    d_hidden = quarters.join(dot_t(grad_stream.astype(BF16), order).astype(BF16)).astype(F32)

    norm_part = mm(
        jnp.stack([part[0] for part in small_parts]), order.astype(F32).T, PRECISE
    )
    pieces = []
    for layer in range(LAYERS):
        _, acc_x, acc_bc, acc_head, d_gain = small_parts[layer]
        skips = acc_head[0].reshape(heads, HEAD_DIM).sum(1)
        rates = -jnp.exp(a_log[layer])
        pieces.append(
            (
                acc_x[:5].reshape(-1),
                d_gain.reshape(-1),
                jnp.concatenate([acc_head[1, :heads], acc_head[2, :heads] * rates, skips]),
            )
        )
    shared = jnp.concatenate(
        [norm_part.reshape(-1)] + [small_parts[layer][2][:5].reshape(-1) for layer in range(LAYERS)]
    )
    flat = jnp.concatenate([tensor_sum(shared[None])[0]] + [v for piece in pieces for v in piece])
    flat = dp_sum(flat[None])[0]

    at = 0

    def take(*shape):
        nonlocal at
        size = 1
        for extent in shape:
            size *= extent
        values = flat[at : at + size].reshape(shape)
        at += size
        return values

    d_norm_gain = take(LAYERS, features)
    bc_acc = take(LAYERS, 5, 2 * STATE)
    x_acc, gain_acc, head_acc = [], [], []
    for layer in range(LAYERS):
        x_acc.append(take(5, width))
        gain_acc.append(take(width))
        head_acc.append(take(3, heads))
    x_acc = jnp.stack(x_acc)
    head_acc = jnp.stack(head_acc)
    stacked = [jnp.stack([weight_parts[layer][m] for layer in range(LAYERS)]) for m in range(4)]
    own_width = STATE // 2
    return (
        mixed,
        d_hidden,
        d_norm_gain,
        stacked[0],
        stacked[1],
        stacked[2][:, :, :own_width],
        stacked[2][:, :, own_width : own_width + heads],
        x_acc[:, :4],
        x_acc[:, 4],
        bc_acc[:, :4],
        bc_acc[:, 4],
        head_acc[:, 0],
        head_acc[:, 1],
        head_acc[:, 2],
        jnp.stack(gain_acc),
        stacked[3],
    )


def solution(mesh):
    in_specs = (
        P("dp", None),
        P("dp"),
        P(),
        P(None, "dp", "tensor"),
        P(None, "dp", "tensor"),
        P(None, "dp", None),
        P(None, "dp", "tensor"),
        P(None, None, "tensor"),
        P(None, "tensor"),
        P(),
        P(),
        P(None, "tensor"),
        P(None, "tensor"),
        P(None, "tensor"),
        P(None, "tensor"),
        P(None, "dp", "tensor"),
        P("dp", None),
    )
    out_specs = (
        P("dp", None),
        P("dp", None),
        P(),
        P(None, "dp", "tensor"),
        P(None, "dp", "tensor"),
        P(None, "dp", "tensor"),
        P(None, "dp", "tensor"),
        P(None, None, "tensor"),
        P(None, "tensor"),
        P(),
        P(),
        P(None, "tensor"),
        P(None, "tensor"),
        P(None, "tensor"),
        P(None, "tensor"),
        P(None, "dp", "tensor"),
    )
    return jax.shard_map(
        on_device, mesh=mesh, in_specs=in_specs, out_specs=out_specs, check_vma=False
    )
```

```python
import jax
import jax.numpy as jnp
from jax import lax
from jax.sharding import PartitionSpec as P
from jax.experimental import pallas as pl
from jax.experimental.pallas import tpu as pltpu

HEAD_DIM = 64
STATE = 128
PACK = 1024
LAYERS = 2
INNER = 3072
EPSILON = 1e-05
CHUNK = 128
LANES = 128
GROUP = 16
TAIL = 8
FAR = -10000.0
PRECISE = lax.Precision.HIGHEST
BF16 = jnp.bfloat16
F32 = jnp.float32
VMEM_BYTES = 48 * 1024 * 1024


def mm(lhs, rhs, precision=None):
    return lax.dot_general(
        lhs, rhs, (((1,), (0,)), ((), ())), precision=precision, preferred_element_type=F32
    )


def mm_t(lhs, rhs):
    return lax.dot_general(lhs, rhs, (((1,), (1,)), ((), ())), preferred_element_type=F32)


def t_mm(lhs, rhs):
    return lax.dot_general(lhs, rhs, (((0,), (0,)), ((), ())), preferred_element_type=F32)


def iota(shape, dim):
    return lax.broadcasted_iota(jnp.int32, shape, dim)


def expand(values, spread):
    lane = iota(values.shape, 1)
    high = values.astype(BF16).astype(F32)
    parts = jnp.where(lane < GROUP, high, jnp.where(lane < 2 * GROUP, values - high, 0.0))
    return mm(parts.astype(BF16), spread)


def shifted_back(joined, offset):
    return joined[TAIL - offset : TAIL - offset + CHUNK]


def conv_pre(joined, taps, bias_row, aux):
    summed = bias_row + taps[0:1] * joined[TAIL:]
    for offset in range(1, 4):
        summed = summed + taps[offset : offset + 1] * (
            shifted_back(joined, offset) * aux[:, offset : offset + 1]
        )
    return summed


def halves_rows(tile, low_lanes):
    zero = jnp.zeros_like(tile)
    return jnp.concatenate(
        [jnp.where(low_lanes, tile, zero), jnp.where(low_lanes, zero, tile)], 0
    )


def step_values(dt_ref, head_ref):
    raw = dt_ref + head_ref[0:1]
    dt = jnp.maximum(raw, 0.0) + jnp.log1p(jnp.exp(-jnp.abs(raw)))
    row = iota((CHUNK, CHUNK), 0)
    col = iota((CHUNK, CHUNK), 1)
    lower = (row >= col).astype(F32)
    log_decay = mm(lower, dt * head_ref[1:2], PRECISE)
    return raw, dt, log_decay, row, col


def scan_fwd_kernel(
    me_ref,
    x_ref,
    bcdt_ref,
    gate_ref,
    aux_ref,
    seg_ref,
    taps_ref,
    bias_ref,
    bc_taps_ref,
    bc_bias_ref,
    head_ref,
    skip_ref,
    gain_ref,
    spread_ref,
    u_ref,
    y_ref,
    sq_ref,
    kept_ref,
    state,
    tail_x,
    tail_bc,
):
    width = x_ref.shape[1]

    @pl.when(pl.program_id(0) == 0)
    def _():
        state[...] = jnp.zeros_like(state)
        tail_x[...] = jnp.zeros_like(tail_x)
        tail_bc[...] = jnp.zeros_like(tail_bc)

    aux = aux_ref[...]
    bc_now = bcdt_ref[:, : 2 * STATE]
    joined_bc = jnp.concatenate([tail_bc[...], bc_now], 0)
    tail_bc[...] = bc_now[CHUNK - TAIL :]
    bc_pre = conv_pre(joined_bc, bc_taps_ref[...], bc_bias_ref[...], aux)
    bc = bc_pre * jax.nn.sigmoid(bc_pre)
    b_low = bc[:, :STATE].astype(BF16)
    c_low = bc[:, STATE:].astype(BF16)
    b_turned = bc[:, :STATE].T.astype(BF16)
    _, dt, log_decay, row, col = step_values(bcdt_ref[:, 2 * STATE :], head_ref)
    log_turned = log_decay.T
    meet = mm_t(c_low, b_low)
    visible = (aux[:, 0:1] == seg_ref[0]) & (row >= col)
    spread = spread_ref[...]
    dt_wide = expand(dt, spread)
    reach = expand(jnp.exp(log_decay) * aux[:, 4:5], spread)
    to_end = expand(jnp.exp(log_decay[CHUNK - 1 :] - log_decay) * aux[:, 5:6], spread)
    state_low = state[...].astype(BF16)
    kept_ref[0] = state_low
    carried = mm(c_low, state_low)
    low_lanes = iota((CHUNK, LANES), 1) < HEAD_DIM
    squares = jnp.zeros((CHUNK, LANES), F32)
    for pair in range(width // LANES):
        at = slice(pair * LANES, (pair + 1) * LANES)
        now = x_ref[:, at]
        joined = jnp.concatenate([tail_x[:, at], now], 0)
        tail_x[:, at] = now[CHUNK - TAIL :]
        pre = conv_pre(joined, taps_ref[:, at], bias_ref[:, at], aux)
        x_conv = pre * jax.nn.sigmoid(pre)
        inputs = x_conv * dt_wide[:, at]
        mats = []
        for head in (2 * pair, 2 * pair + 1):
            gap = log_decay[:, head : head + 1] - log_turned[head : head + 1, :]
            mats.append((jnp.exp(jnp.where(visible, gap, FAR)) * meet).astype(BF16))
        local = mm(jnp.concatenate(mats, 1), halves_rows(inputs.astype(BF16), low_lanes))
        y = local + carried[:, at] * reach[:, at] + skip_ref[:, at] * x_conv
        y_ref[:, at] = y.astype(y_ref.dtype)
        ending = (inputs * to_end[:, at]).astype(BF16)
        state[:, at] = state[:, at] * reach[CHUNK - 1 :, at] + mm(b_turned, ending)
        gate = gate_ref[:, at].astype(F32)
        gated = y * (gate * jax.nn.sigmoid(gate))
        grown = gated * gain_ref[:, at]
        u_ref[:, at] = grown.astype(BF16)
        squares = squares + gated * gated
    ones = jnp.ones((8, LANES), F32)
    sums = lax.dot_general(
        ones, squares, (((1,), (1,)), ((), ())), precision=PRECISE, preferred_element_type=F32
    )
    sq_ref[...] = sums


def whole(shape):
    return pl.BlockSpec(shape, lambda *_: (0,) * len(shape))


def place_of(chunk, chunks, me_ref):
    part = chunks // 4
    return (chunk // part ^ me_ref[0]) * part + chunk % part


def scan_fwd(me, x_pre, bcdt_pre, gate_pre, side, weights):
    length, width = x_pre.shape
    chunks = length // CHUNK
    aux, seg_rows = side
    at = lambda c, m: (place_of(c, chunks, m), 0)
    tile = lambda columns: pl.BlockSpec((CHUNK, columns), at)
    in_specs = [
        tile(width),
        tile(bcdt_pre.shape[1]),
        tile(width),
        pl.BlockSpec((CHUNK, LANES), lambda c, m: (c, 0)),
        pl.BlockSpec((1, 1, CHUNK), lambda c, m: (c, 0, 0)),
    ] + [whole(w.shape) for w in weights]
    return pl.pallas_call(
        scan_fwd_kernel,
        grid_spec=pltpu.PrefetchScalarGridSpec(
            num_scalar_prefetch=1,
            grid=(chunks,),
            in_specs=in_specs,
            out_specs=[
                tile(width),
                tile(width),
                pl.BlockSpec((8, CHUNK), lambda c, m: (0, c)),
                pl.BlockSpec((1, STATE, width), lambda c, m: (c, 0, 0)),
            ],
            scratch_shapes=[
                pltpu.VMEM((STATE, width), F32),
                pltpu.VMEM((TAIL, width), F32),
                pltpu.VMEM((TAIL, 2 * STATE), F32),
            ],
        ),
        out_shape=[
            jax.ShapeDtypeStruct((length, width), BF16),
            jax.ShapeDtypeStruct((length, width), F32),
            jax.ShapeDtypeStruct((8, length), F32),
            jax.ShapeDtypeStruct((chunks, STATE, width), BF16),
        ],
        compiler_params=pltpu.CompilerParams(vmem_limit_bytes=VMEM_BYTES),
        cost_estimate=pl.CostEstimate(
            flops=140 * length * width * LANES,
            bytes_accessed=20 * length * width,
            transcendentals=0,
        ),
        name="scan_fwd",
    )(me, x_pre, bcdt_pre, gate_pre, aux, seg_rows, *weights)


def gate_bwd_kernel(
    me_ref, gs_ref, y_ref, gate_ref, col_ref, gain_ref, g_gate_ref, g_y_ref, d_gain_ref
):
    @pl.when(pl.program_id(0) == 0)
    def _():
        d_gain_ref[...] = jnp.zeros_like(d_gain_ref)

    inv = col_ref[:, 0:1]
    pull = col_ref[:, 1:2]
    for pair in range(gs_ref.shape[1] // LANES):
        at = slice(pair * LANES, (pair + 1) * LANES)
        gs = gs_ref[:, at].astype(F32)
        y = y_ref[:, at].astype(F32)
        gate = gate_ref[:, at].astype(F32)
        sig = jax.nn.sigmoid(gate)
        act = gate * sig
        gated = y * act
        grown = gs * inv
        d_gain_ref[:, at] += jnp.sum(grown * gated, 0, keepdims=True)
        g_gated = grown * gain_ref[:, at] - gated * pull
        g_y_ref[:, at] = (g_gated * act).astype(BF16)
        g_gate_ref[:, at] = (g_gated * y * sig * (1.0 + gate * (1.0 - sig))).astype(BF16)


def gate_bwd(me, gs, y, gate_pre, columns, gain):
    length, width = gs.shape
    rows = length // 4
    tile = pl.BlockSpec((rows, width), lambda p, m: (p, 0))
    return pl.pallas_call(
        gate_bwd_kernel,
        grid_spec=pltpu.PrefetchScalarGridSpec(
            num_scalar_prefetch=1,
            grid=(4,),
            in_specs=[
                tile,
                tile,
                tile,
                pl.BlockSpec((rows, columns.shape[1]), lambda p, m: (p ^ m[0], 0)),
                whole(gain.shape),
            ],
            out_specs=[tile, tile, whole((1, width))],
        ),
        out_shape=[jax.ShapeDtypeStruct((length, width), BF16)] * 2
        + [jax.ShapeDtypeStruct((1, width), F32)],
        compiler_params=pltpu.CompilerParams(vmem_limit_bytes=VMEM_BYTES),
        cost_estimate=pl.CostEstimate(
            flops=50 * length * width * LANES,
            bytes_accessed=18 * length * width,
            transcendentals=0,
        ),
        name="gate_bwd",
    )(me, gs, y, gate_pre, columns, gain)


def conv_bwd(joined, joined_grad, grad, taps, aux, acc_ref, at):
    acc_ref[4:5, at] += jnp.sum(grad, 0, keepdims=True)
    acc_ref[0:1, at] += jnp.sum(grad * joined[TAIL:], 0, keepdims=True)
    result = taps[0:1] * grad
    for offset in range(1, 4):
        moved = shifted_back(joined, offset) * aux[:, offset : offset + 1]
        acc_ref[offset : offset + 1, at] += jnp.sum(grad * moved, 0, keepdims=True)
        later = joined_grad[offset : offset + CHUNK] * aux[:, 5 + offset : 6 + offset]
        result = result + taps[offset : offset + 1] * later
    return result


def scan_bwd_kernel(
    me_ref,
    g_ref,
    x_ref,
    x_tail_ref,
    bcdt_ref,
    bc_tail_ref,
    kept_ref,
    aux_ref,
    seg_ref,
    taps_ref,
    bias_ref,
    bc_taps_ref,
    bc_bias_ref,
    head_ref,
    skip_ref,
    gain_ref,
    spread_ref,
    gx_ref,
    gbc_ref,
    gdt_ref,
    accx_ref,
    accbc_ref,
    acch_ref,
    grad_state,
    next_x,
    next_bc,
):
    width = x_ref.shape[1]

    @pl.when(pl.program_id(0) == 0)
    def _():
        grad_state[...] = jnp.zeros_like(grad_state)
        next_x[...] = jnp.zeros_like(next_x)
        next_bc[...] = jnp.zeros_like(next_bc)
        accx_ref[...] = jnp.zeros_like(accx_ref)
        accbc_ref[...] = jnp.zeros_like(accbc_ref)
        acch_ref[...] = jnp.zeros_like(acch_ref)

    aux = aux_ref[...]
    joined_bc = jnp.concatenate([bc_tail_ref[:, : 2 * STATE], bcdt_ref[:, : 2 * STATE]], 0)
    bc_pre = conv_pre(joined_bc, bc_taps_ref[...], bc_bias_ref[...], aux)
    bc_sig = jax.nn.sigmoid(bc_pre)
    bc = bc_pre * bc_sig
    b_low = bc[:, :STATE].astype(BF16)
    c_low = bc[:, STATE:].astype(BF16)
    c_turned = bc[:, STATE:].T.astype(BF16)
    raw, dt, log_decay, row, col = step_values(bcdt_ref[:, 2 * STATE :], head_ref)
    log_turned = log_decay.T
    meet = mm_t(b_low, c_low)
    visible = (aux[:, 0:1] == seg_ref[0]) & (row <= col)
    spread = spread_ref[...]
    dt_wide = expand(dt, spread)
    reach = expand(jnp.exp(log_decay) * aux[:, 4:5], spread)
    to_end = expand(jnp.exp(log_decay[CHUNK - 1 :] - log_decay) * aux[:, 5:6], spread)
    low_lanes = iota((CHUNK, LANES), 1) < HEAD_DIM
    lane = iota((CHUNK, LANES), 1)
    grad_meet = jnp.zeros((CHUNK, CHUNK), F32)
    grad_b = jnp.zeros((CHUNK, STATE), F32)
    grad_c = jnp.zeros((CHUNK, STATE), F32)
    col_sums = jnp.zeros((CHUNK, LANES), F32)
    row_sums = jnp.zeros((LANES, CHUNK), F32)
    head_sums = jnp.zeros((3 * CHUNK, LANES), F32)
    through = jnp.zeros((8, LANES), F32)
    head_row = iota((LANES, CHUNK), 0)
    for pair in range(width // LANES):
        at = slice(pair * LANES, (pair + 1) * LANES)
        joined = jnp.concatenate([x_tail_ref[:, at], x_ref[:, at]], 0)
        pre = conv_pre(joined, taps_ref[:, at], bias_ref[:, at], aux)
        sig = jax.nn.sigmoid(pre)
        x_conv = pre * sig
        inputs = x_conv * dt_wide[:, at]
        g_low = g_ref[:, at]
        g = g_low.astype(F32)
        grad_mats = mm_t(halves_rows(inputs.astype(BF16), low_lanes), g_low)
        mats = []
        for member in range(2):
            head = 2 * pair + member
            gap = log_turned[head : head + 1, :] - log_decay[:, head : head + 1]
            weight = jnp.exp(jnp.where(visible, gap, FAR))
            mats.append((weight * meet).astype(BF16))
            part = weight * grad_mats[member * CHUNK : (member + 1) * CHUNK]
            grad_meet = grad_meet + part
            product = part * meet
            col_sums = jnp.where(lane == head, jnp.sum(product, 1, keepdims=True), col_sums)
            row_sums = jnp.where(head_row == head, jnp.sum(product, 0, keepdims=True), row_sums)
        local = mm(jnp.concatenate(mats, 1), halves_rows(g_low, low_lanes))
        reach_now = reach[:, at]
        to_end_now = to_end[:, at]
        state_low = kept_ref[0, :, at]
        coming = g * reach_now
        coming_low = coming.astype(BF16)
        carried = mm(c_low, state_low)
        grad_c = grad_c + mm_t(coming_low, state_low)
        grad_state_now = grad_state[:, at]
        grad_state_low = grad_state_now.astype(BF16)
        leaving = mm(b_low, grad_state_low)
        ending = inputs * to_end_now
        grad_b = grad_b + mm_t(ending.astype(BF16), grad_state_low)
        last = reach_now[CHUNK - 1 :]
        passed = jnp.sum(grad_state_now * state_low.astype(F32), 0, keepdims=True) * last
        through = through + mm_t(
            jnp.broadcast_to(passed, (8, LANES)).astype(BF16), spread[:, at]
        )
        grad_state[:, at] = grad_state_now * last + mm(c_turned, coming_low)
        grad_inputs = local + leaving * to_end_now
        stacked = jnp.concatenate([coming * carried, ending * leaving, grad_inputs * x_conv], 0)
        head_sums = head_sums + mm_t(stacked.astype(BF16), spread[:, at])
        acch_ref[0:1, at] += jnp.sum(g * x_conv, 0, keepdims=True)
        grad_conv = (grad_inputs * dt_wide[:, at] + g * skip_ref[:, at]) * (
            sig * (1.0 + pre * (1.0 - sig))
        )
        joined_grad = jnp.concatenate([grad_conv, next_x[:, at]], 0)
        next_x[:, at] = grad_conv[:TAIL]
        gx_ref[:, at] = conv_bwd(
            joined, joined_grad, grad_conv, taps_ref[:, at], aux, accx_ref, at
        ).astype(BF16)
    upper = (row <= col).astype(F32)
    strict = (row > col).astype(F32)
    straddle = (
        mm(upper, row_sums.T - col_sums + head_sums[:CHUNK], PRECISE)
        + mm(strict, head_sums[CHUNK : 2 * CHUNK], PRECISE)
        + through[0:1]
    )
    grad_dt = head_sums[2 * CHUNK :] + head_ref[1:2] * straddle
    grad_raw = jnp.where(lane < GROUP, grad_dt * jax.nn.sigmoid(raw), 0.0)
    gdt_ref[...] = grad_raw.astype(BF16)
    acch_ref[1:2, :LANES] += jnp.sum(grad_raw, 0, keepdims=True)
    acch_ref[2:3, :LANES] += jnp.sum(dt * straddle, 0, keepdims=True)
    grad_meet_low = grad_meet.astype(BF16)
    grad_b = grad_b + mm(grad_meet_low, c_low)
    grad_c = grad_c + t_mm(grad_meet_low, b_low)
    grad_bc = jnp.concatenate([grad_b, grad_c], 1) * (bc_sig * (1.0 + bc_pre * (1.0 - bc_sig)))
    joined_grad = jnp.concatenate([grad_bc, next_bc[...]], 0)
    next_bc[...] = grad_bc[:TAIL]
    gbc_ref[...] = conv_bwd(
        joined_bc, joined_grad, grad_bc, bc_taps_ref[...], aux, accbc_ref, slice(None)
    ).astype(BF16)


def scan_bwd(me, g_y, x_pre, bcdt_pre, kept, side, weights):
    length, width = x_pre.shape
    chunks = length // CHUNK
    aux, seg_rows = side
    back = lambda c: chunks - 1 - c
    place = lambda c, m: place_of(back(c), chunks, m)
    tile = lambda columns: pl.BlockSpec((CHUNK, columns), lambda c, m: (place(c, m), 0))

    def tail_at(c, m):
        before = place_of(jnp.maximum(back(c) - 1, 0), chunks, m)
        return (before * (CHUNK // TAIL) + CHUNK // TAIL - 1, 0)

    tail = lambda columns: pl.BlockSpec((TAIL, columns), tail_at)
    wide = bcdt_pre.shape[1]
    in_specs = [
        tile(width),
        tile(width),
        tail(width),
        tile(wide),
        tail(wide),
        pl.BlockSpec((1, STATE, width), lambda c, m: (back(c), 0, 0)),
        pl.BlockSpec((CHUNK, LANES), lambda c, m: (back(c), 0)),
        pl.BlockSpec((1, 1, CHUNK), lambda c, m: (back(c), 0, 0)),
    ] + [whole(w.shape) for w in weights]
    return pl.pallas_call(
        scan_bwd_kernel,
        grid_spec=pltpu.PrefetchScalarGridSpec(
            num_scalar_prefetch=1,
            grid=(chunks,),
            in_specs=in_specs,
            out_specs=[
                tile(width),
                tile(2 * STATE),
                tile(LANES),
                whole((8, width)),
                whole((8, 2 * STATE)),
                whole((8, width)),
            ],
            scratch_shapes=[
                pltpu.VMEM((STATE, width), F32),
                pltpu.VMEM((TAIL, width), F32),
                pltpu.VMEM((TAIL, 2 * STATE), F32),
            ],
        ),
        out_shape=[
            jax.ShapeDtypeStruct((length, width), BF16),
            jax.ShapeDtypeStruct((length, 2 * STATE), BF16),
            jax.ShapeDtypeStruct((length, LANES), BF16),
            jax.ShapeDtypeStruct((8, width), F32),
            jax.ShapeDtypeStruct((8, 2 * STATE), F32),
            jax.ShapeDtypeStruct((8, width), F32),
        ],
        compiler_params=pltpu.CompilerParams(vmem_limit_bytes=VMEM_BYTES),
        cost_estimate=pl.CostEstimate(
            flops=280 * length * width * LANES,
            bytes_accessed=20 * length * width,
            transcendentals=0,
        ),
        name="scan_bwd",
    )(me, g_y, x_pre, x_pre, bcdt_pre, bcdt_pre, kept, aux, seg_rows, *weights)


def side_arrays(segments):
    length = segments.shape[0]
    seg = segments.astype(F32)
    columns = [seg]
    nothing = lambda count: jnp.full((count,), -1.0, F32)
    for offset in range(1, 4):
        moved = jnp.concatenate([nothing(offset), seg[: length - offset]], 0)
        columns.append((moved == seg).astype(F32))
    blocks = seg.reshape(-1, CHUNK)
    ends = blocks[:, -1]
    before = jnp.concatenate([nothing(1), ends[:-1]], 0)
    columns.append((blocks == before[:, None]).astype(F32).reshape(-1))
    columns.append((blocks == ends[:, None]).astype(F32).reshape(-1))
    for offset in range(1, 4):
        moved = jnp.concatenate([seg[offset:], nothing(offset)], 0)
        columns.append((moved == seg).astype(F32))
    stacked = jnp.stack(columns, 1)
    aux = jnp.pad(stacked, ((0, 0), (0, LANES - stacked.shape[1])))
    return aux, blocks.reshape(-1, 1, CHUNK)


def in_groups(values):
    padded = jnp.pad(values, [(0, 0)] * (values.ndim - 1) + [(0, GROUP - values.shape[-1])])
    return jnp.tile(padded, (1,) * (values.ndim - 1) + (LANES // GROUP,))


def spread_matrix(width):
    head = lax.broadcasted_iota(jnp.int32, (LANES, width), 0) % GROUP
    owner = lax.broadcasted_iota(jnp.int32, (LANES, width), 1) // HEAD_DIM
    return (head == owner).astype(BF16)


def scan_weights(taps, bias, bc_taps, bc_bias, dt_bias, a_log, d_skip, gain, spread):
    rates = -jnp.exp(a_log)
    rows = jnp.stack([in_groups(dt_bias), in_groups(rates)])
    head = jnp.pad(rows, ((0, 6), (0, 0)))
    return (
        taps,
        bias[None],
        bc_taps,
        bc_bias[None],
        head,
        jnp.repeat(d_skip, HEAD_DIM)[None],
        gain[None],
        spread,
    )


def partners(count, step):
    return [(index, index ^ step) for index in range(count)]


def swap(values, axis, step):
    return lax.ppermute(values, axis, partners(lax.axis_size(axis), step))


def after(values, *earlier):
    return lax.optimization_barrier((values, *earlier))[0]


def dp_masks():
    masks = []
    step = lax.axis_size("dp") // 2
    while step > 0:
        masks.append(step)
        step = step // 2
    return masks


def offsets(masks):
    found = [0]
    for mask in masks:
        found = found + [offset ^ mask for offset in found]
    return found


def spread_stage(rows, mask):
    got = swap(rows, "dp", mask)
    return jnp.concatenate([rows, got], 0), got


def gather_rows(own, masks):
    stages = []
    rows = own
    for mask in masks:
        rows, got = spread_stage(rows, mask)
        stages.append(got)
    return rows, stages


def scatter_first(kept, got):
    total = kept + got.astype(F32)
    height = total.shape[0] // 2
    return total[:height], total[height:].astype(BF16)


def scatter_rest(kept, sent, masks):
    for mask in reversed(masks[1:-1]):
        kept, sent = scatter_first(kept, swap(sent, "dp", mask))
    return kept + swap(sent, "dp", masks[0]).astype(F32)


def grad_half(rows, grads, which):
    width = rows.shape[1] // 2
    dims = (((0,), (0,)), ((), ()))
    taken = rows[:, which * width : (which + 1) * width]
    return lax.dot_general(taken, grads, dims, preferred_element_type=F32)


def sent_half(rows, grads):
    return grad_half(rows, grads, 1).astype(BF16)


def reordered(values, me):
    size = values.shape[0] // 4
    return jnp.concatenate(
        [lax.dynamic_slice_in_dim(values, (part ^ me) * size, size, 0) for part in range(4)], 0
    )


def turned_over(values, size):
    shaped = values.reshape(-1, 2, size, values.shape[1])
    return shaped[:, ::-1].reshape(values.shape)


def own_quarter(values, me):
    size = values.shape[0] // 4
    return lax.dynamic_slice_in_dim(values, me * size, size, 0)


def tensor_sum(values):
    values = values + swap(values, "tensor", 1)
    return values + swap(values, "tensor", 2)


def dp_sum(values):
    step = 1
    while step < lax.axis_size("dp"):
        values = values + swap(values, "dp", step)
        step = 2 * step
    return values


def dot(lhs, rhs):
    return lax.dot_general(lhs, rhs, (((1,), (0,)), ((), ())), preferred_element_type=F32)


def dot_t(lhs, rhs):
    return lax.dot_general(lhs, rhs, (((1,), (1,)), ((), ())), preferred_element_type=F32)


def own_order(features, masks):
    place = lax.axis_index("dp")
    found = offsets(masks)
    height = features // len(found)
    index = lax.broadcasted_iota(jnp.int32, (1, features), 1)
    part, within = index // height, index % height
    away = jnp.zeros_like(part)
    for position, offset in enumerate(found):
        away = jnp.where(part == position, offset, away)
    source = (away ^ place) * height + within
    return (lax.broadcasted_iota(jnp.int32, (features, features), 0) == source).astype(BF16)


def rms_of(stream):
    return lax.rsqrt(jnp.mean(stream * stream, -1, keepdims=True) + EPSILON)


def on_device(
    hidden,
    segments,
    norm_gain,
    w_z,
    w_x,
    w_bc,
    w_dt,
    conv_x_w,
    conv_x_b,
    conv_bc_w,
    conv_bc_b,
    dt_bias,
    a_log,
    d_skip,
    gated_gain,
    w_out,
    cotangent,
):
    length, features = hidden.shape
    width = w_x.shape[2]
    heads = dt_bias.shape[1]
    masks = dp_masks()
    place = lax.axis_index("tensor")
    core, far = place % 2, place // 2
    me = 2 * core + far
    me_row = me.astype(jnp.int32)[None]
    half = length // 2
    quarter = length // 4

    side_first = masks[-1:] + masks[:-1]
    seated = [offsets(side_first).index(offset) for offset in offsets(masks)]
    height = w_x.shape[1]
    quart_bc = w_bc.shape[2] // 4
    own_bc = lax.dynamic_slice_in_dim(w_bc, place * quart_bc, quart_bc, 2)
    w_small = jnp.concatenate([own_bc[0], own_bc[1], w_dt[0], w_dt[1]], 1)
    w_small = jnp.pad(w_small, ((0, 0), (0, 2 * LANES - w_small.shape[1])))

    far_stage, near_stage = {}, {}

    def gathered(name, own, over):
        rows, stages = gather_rows(own, over)
        far_stage[name], near_stage[name] = stages[0], stages[-1 if over is not masks else -2]
        return rows

    early = swap(w_out[1], "dp", 1)
    x_rows = gathered("x0", w_x[0], masks)
    small_rows = gathered("small", after(w_small, near_stage["x0"]), masks)
    z_rows = gathered("z0", after(w_z[0], near_stage["x0"]), masks)
    out_rows = gathered("out0", after(w_out[0], far_stage["z0"]), masks)
    x_rows = [x_rows, gathered("x1", after(w_x[1], far_stage["out0"]), masks)]
    z_rows = [z_rows, gathered("z1", after(w_z[1], far_stage["x1"]), masks)]
    both_sides = after(jnp.concatenate([w_out[1], early], 0), far_stage["z1"])
    rows = gathered("out1", both_sides, masks[:-1])
    rows = [rows[seat * height : (seat + 1) * height] for seat in seated]
    out_rows = [out_rows, jnp.concatenate(rows, 0)]

    own_cols = small_rows[:, :LANES]
    across = swap(own_cols, "tensor", 2)
    beside = swap(jnp.concatenate([own_cols, across], 1), "tensor", 1)

    def small_columns(layer):
        low = layer * quart_bc
        parts = [
            own_cols[:, low : low + quart_bc],
            across[:, low : low + quart_bc],
            beside[:, low : low + quart_bc],
            beside[:, LANES + low : LANES + low + quart_bc],
        ]
        first = core == 0
        near = [jnp.where(first, parts[0], parts[2]), jnp.where(first, parts[2], parts[0])]
        away = [jnp.where(first, parts[1], parts[3]), jnp.where(first, parts[3], parts[1])]
        first = far == 0
        ordered = [jnp.where(first, n, a) for n, a in zip(near, away)]
        ordered += [jnp.where(first, a, n) for n, a in zip(near, away)]
        at = LANES + layer * heads
        return jnp.concatenate(ordered + [in_groups(small_rows[:, at : at + heads])], 1)

    bcdt_rows = [small_columns(layer) for layer in range(LAYERS)]

    order = lax.optimization_barrier(own_order(features, masks))
    side = side_arrays(segments)
    spread = spread_matrix(width)
    weights = [
        scan_weights(
            conv_x_w[layer],
            conv_x_b[layer],
            conv_bc_w[layer],
            conv_bc_b[layer],
            dt_bias[layer],
            a_log[layer],
            d_skip[layer],
            gated_gain[layer],
            spread,
        )
        for layer in range(LAYERS)
    ]
    order, side, weights = lax.optimization_barrier((order, side, weights))
    hidden_now = after(reordered(hidden, me), far_stage["x0"], early)
    hidden_low = dot(hidden_now, order).astype(BF16)
    cotangent_now = after(reordered(cotangent, me), near_stage["x0"], hidden_low)
    cotangent_low = dot(cotangent_now, order).astype(BF16)
    gains = mm(after(norm_gain, near_stage["x0"]), order.astype(F32), PRECISE)
    hidden_low, cotangent_low, gains, _, _ = lax.optimization_barrier(
        (hidden_low, cotangent_low, gains, far_stage["small"], far_stage["z0"])
    )

    def columns_of(values, which):
        return lax.dynamic_slice_in_dim(values, which * STATE, STATE, 1)

    stream = hidden_low.astype(F32)
    normed0 = (stream * rms_of(stream) * gains[0]).astype(BF16)
    stream0 = hidden_low[:quarter].astype(F32)
    x_pre0 = dot(after(normed0, near_stage["small"]), x_rows[0])
    bcdt_pre0 = dot(after(normed0, near_stage["z0"], far_stage["out0"]), bcdt_rows[0])
    gate_pre0 = dot(after(normed0, near_stage["out0"], far_stage["x1"]), z_rows[0])
    gate_pre0 = after(gate_pre0, near_stage["x1"], far_stage["z1"])
    u0, y0, sq, kept0 = scan_fwd(me_row, x_pre0, bcdt_pre0, gate_pre0, side, weights[0])
    u_now = after(u0, near_stage["z1"])
    sent = dot_t(u_now[half:], out_rows[0]).astype(BF16)
    sq = sq[0:1]
    sq = sq + swap(sq, "tensor", 1)
    u_now = after(u_now, sent, sq)
    mine = dot_t(u_now[:half], out_rows[0]) + swap(sent, "tensor", 1).astype(F32)
    sq = sq + swap(sq, "tensor", 2)
    away = after(mine[quarter:].astype(BF16), sq)
    got = swap(away, "tensor", 2)
    inv0 = lax.rsqrt(sq / INNER + EPSILON)[0]
    total0 = mine[:quarter] + got.astype(F32)
    stream1 = stream0 + own_quarter(inv0, me)[:, None] * total0
    normed_own = (stream1 * rms_of(stream1) * gains[1]).astype(BF16)
    normed_own = after(normed_own, far_stage["out1"])
    normed_half = jnp.concatenate([normed_own, swap(normed_own, "tensor", 2)], 0)
    normed1 = jnp.concatenate([normed_half, swap(normed_half, "tensor", 1)], 0)
    scaled0 = (u0.astype(F32) * reordered(inv0, me)[:, None]).astype(BF16)

    x_pre1 = dot(normed1, x_rows[1])
    bcdt_pre1 = dot(normed1, bcdt_rows[1])
    gate_pre1 = dot(after(normed1, near_stage["out1"]), z_rows[1])
    u1, y1, sq, kept1 = scan_fwd(me_row, x_pre1, bcdt_pre1, gate_pre1, side, weights[1])
    scaled_grad1 = dot(cotangent_low, out_rows[1])
    cross = reordered(jnp.sum(scaled_grad1 * u1.astype(F32), -1), me)
    both = tensor_sum(jnp.stack([sq[0], cross]))
    mixed_sent = dot_t(u1[half:], out_rows[1]).astype(BF16)
    mixed_mine = dot_t(u1[:half], out_rows[1])
    mixed_mine = mixed_mine + swap(mixed_sent, "tensor", 1).astype(F32)
    both = after(both, mixed_sent, mixed_mine)
    mixed_got = swap(mixed_mine[quarter:].astype(BF16), "tensor", 2)
    inv1 = lax.rsqrt(both[0] / INNER + EPSILON)

    columns = jnp.stack([inv1, inv1 * inv1 * inv1 * both[1] / INNER], 1)
    g_gate1, g_y, d_gain1 = gate_bwd(
        me_row, scaled_grad1, y1, gate_pre1, columns, gated_gain[1][None]
    )
    z_sent = sent_half(normed1, g_gate1)
    z_got = swap(z_sent, "dp", 1)
    scaled1 = (u1.astype(F32) * reordered(inv1, me)[:, None]).astype(BF16)
    out_sent = sent_half(cotangent_low, scaled1)
    out_got = swap(out_sent, "dp", 1)
    g_y = after(g_y, z_sent, out_sent)
    g_x1, g_bc1, g_dt1, acc_x1, acc_bc1, acc_head1 = scan_bwd(
        me_row, g_y, x_pre1, bcdt_pre1, kept1, side, weights[1]
    )
    g_x1 = after(g_x1, z_got, mixed_got)

    def grad_rows(rows, g_gate, g_x, g_bcdt, layer):
        return (
            dot_t(g_gate[rows], z_rows[layer])
            + dot_t(g_x[rows], x_rows[layer])
            + dot_t(g_bcdt[rows], bcdt_rows[layer])
        )

    g_bcdt = jnp.concatenate([g_bc1, g_dt1], 1)
    sent = grad_rows(slice(half, length), g_gate1, g_x1, g_bcdt, 1).astype(BF16)
    own = grad_rows(slice(0, half), after(g_gate1, sent), g_x1, g_bcdt, 1)
    mine = own + swap(sent, "tensor", 1).astype(F32)
    away = mine[quarter:].astype(BF16)
    got = swap(away, "tensor", 2)
    normed_now, cotangent_now, _ = lax.optimization_barrier((normed1, cotangent_low, away))
    z_kept, z_next = scatter_first(grad_half(normed_now, g_gate1, 0), z_got)
    x_got = swap(sent_half(normed_now, g_x1), "dp", 1)
    out_kept, out_next = scatter_first(grad_half(cotangent_now, scaled1, 0), out_got)
    x_kept_half = grad_half(normed_now, g_x1, 0)
    total = mine[:quarter] + got.astype(F32)
    rms = rms_of(stream1)
    normal = stream1 * rms
    d_norm1 = jnp.sum(total * normal, 0)
    grown = total * gains[1]
    grad_stream = cotangent_low[:quarter].astype(F32) + rms * (
        grown - normal * jnp.mean(grown * normal, -1, keepdims=True)
    )
    grad_own = grad_stream.astype(BF16)
    cross = jnp.sum(grad_own.astype(F32) * total0, -1)
    grad_half_rows = jnp.concatenate([grad_own, swap(grad_own, "tensor", 2)], 0)
    cross = jnp.concatenate([cross, swap(cross, "tensor", 2)], 0)
    grad_half_rows, cross = lax.optimization_barrier((grad_half_rows, cross))
    grad0 = jnp.concatenate([grad_half_rows, swap(grad_half_rows, "tensor", 1)], 0)
    cross = reordered(jnp.concatenate([cross, swap(cross, "tensor", 1)], 0), me)
    x_kept, x_next = scatter_first(x_kept_half, x_got)
    x_next = after(x_next, grad0)
    x_near = swap(x_next, "dp", masks[-2])

    out_sent0 = sent_half(grad0, scaled0)
    out_got0 = swap(out_sent0, "dp", 1)
    scaled_grad0 = dot(after(grad0, out_sent0), out_rows[0])
    columns = jnp.stack([inv0, inv0 * inv0 * inv0 * cross / INNER], 1)
    g_gate0, g_y, d_gain0 = gate_bwd(
        me_row, scaled_grad0, y0, gate_pre0, columns, gated_gain[0][None]
    )
    z_sent0 = sent_half(normed0, g_gate0)
    z_got0 = swap(z_sent0, "dp", 1)
    d_z1 = scatter_rest(z_kept, z_next, masks)
    mixed_total = mixed_mine[:quarter] + mixed_got.astype(F32)
    last = stream1 + own_quarter(inv1, me)[:, None] * mixed_total
    last = after(last, grad0)
    mixed_own = dot_t(last.astype(BF16), order).astype(BF16)
    mixed_half = jnp.concatenate([mixed_own, swap(mixed_own, "tensor", 2)], 0)
    g_y = after(g_y, z_sent0, mixed_own, x_near)
    g_x0, g_bc0, g_dt0, acc_x0, acc_bc0, acc_head0 = scan_bwd(
        me_row, g_y, x_pre0, bcdt_pre0, kept0, side, weights[0]
    )
    away1 = after(columns_of(g_bc1, 1 - far), grad0)
    away1 = swap(away1, "tensor", 2)
    away0 = swap(columns_of(g_bc0, 1 - far), "tensor", 2)
    g_x0 = after(g_x0, out_got0, mixed_half, away1)
    x_sent0 = sent_half(normed0, g_x0)
    x_got0 = swap(x_sent0, "dp", 1)
    g_x0 = after(g_x0, x_sent0)
    g_bcdt = jnp.concatenate([g_bc0, g_dt0], 1)
    sent = grad_rows(slice(half, length), g_gate0, g_x0, g_bcdt, 0).astype(BF16)
    own = grad_rows(slice(0, half), after(g_gate0, sent), g_x0, g_bcdt, 0)
    mine = own + swap(sent, "tensor", 1).astype(F32)
    away = mine[quarter:].astype(BF16)
    got = swap(away, "tensor", 2)
    normed_now, grad_now, _ = lax.optimization_barrier((normed0, grad0, away))
    z_kept0, z_next0 = scatter_first(grad_half(normed_now, g_gate0, 0), z_got0)
    out_kept0, out_next0 = scatter_first(grad_half(grad_now, scaled0, 0), out_got0)
    x_kept0, x_next0 = scatter_first(grad_half(normed_now, g_x0, 0), x_got0)
    total = mine[:quarter] + got.astype(F32)
    rms = rms_of(stream0)
    normal = stream0 * rms
    d_norm0 = jnp.sum(total * normal, 0)
    grown = total * gains[0]
    grad_stream = grad_stream + rms * (
        grown - normal * jnp.mean(grown * normal, -1, keepdims=True)
    )
    d_hidden = dot_t(grad_stream.astype(BF16), order).astype(BF16)
    d_hidden = jnp.concatenate([d_hidden, swap(d_hidden, "tensor", 2)], 0)
    d_hidden = jnp.concatenate([d_hidden, swap(d_hidden, "tensor", 1)], 0)
    d_hidden = reordered(d_hidden, me).astype(F32)
    mixed = jnp.concatenate([mixed_half, swap(mixed_half, "tensor", 1)], 0)
    mixed = reordered(mixed, me)

    d_out1 = scatter_rest(out_kept, out_next, masks)
    d_x1 = scatter_rest(*scatter_first(x_kept, x_near), masks[:1] + masks[2:])
    d_out0 = scatter_rest(out_kept0, out_next0, masks)
    d_z0 = scatter_rest(z_kept0, z_next0, masks)
    d_x0 = scatter_rest(x_kept0, x_next0, masks)

    near_cols = jnp.concatenate([columns_of(v, far) for v in (g_bc0, g_bc1)], 1)
    away_cols = jnp.concatenate([away0, away1], 1)
    bc_sum = near_cols.astype(F32) + turned_over(away_cols, quarter).astype(F32)
    across_sum = swap(after(bc_sum.astype(BF16), away), "tensor", 1)
    bc_sum = bc_sum + turned_over(across_sum, half).astype(F32)
    small_sent, small_kept = [], []
    for layer, (rows, g_dt) in enumerate(((normed0, g_dt0), (normed1, g_dt1))):
        summed = bc_sum[:, layer * STATE : (layer + 1) * STATE]
        rolled = jnp.roll(summed, STATE // 2, 1)
        own_cols = jnp.where(core == 0, summed, rolled)[:, : STATE // 2].astype(BF16)
        own_cols = jnp.concatenate([own_cols, g_dt[:, : STATE // 2]], 1)
        small_sent.append(sent_half(rows, own_cols))
        small_kept.append(grad_half(rows, own_cols, 0))
    small_sent = after(jnp.concatenate(small_sent, 1), x_got0)
    small_got = swap(small_sent, "dp", 1)
    small_kept, small_next = scatter_first(jnp.concatenate(small_kept, 1), small_got)
    d_small = scatter_rest(small_kept, small_next, masks)
    d_small = jnp.stack([d_small[:, layer * LANES : (layer + 1) * LANES] for layer in range(LAYERS)])
    small_parts = [
        (d_norm0, acc_x0, acc_bc0, acc_head0, d_gain0),
        (d_norm1, acc_x1, acc_bc1, acc_head1, d_gain1),
    ]

    norm_part = mm(
        jnp.stack([part[0] for part in small_parts]), order.astype(F32).T, PRECISE
    )
    pieces = []
    for layer in range(LAYERS):
        _, acc_x, acc_bc, acc_head, d_gain = small_parts[layer]
        skips = acc_head[0].reshape(heads, HEAD_DIM).sum(1)
        rates = -jnp.exp(a_log[layer])
        pieces.append(
            (
                acc_x[:5].reshape(-1),
                d_gain.reshape(-1),
                jnp.concatenate([acc_head[1, :heads], acc_head[2, :heads] * rates, skips]),
            )
        )
    shared = jnp.concatenate(
        [norm_part.reshape(-1)] + [small_parts[layer][2][:5].reshape(-1) for layer in range(LAYERS)]
    )
    flat = jnp.concatenate([tensor_sum(shared[None])[0]] + [v for piece in pieces for v in piece])
    flat = dp_sum(flat[None])[0]

    at = 0

    def take(*shape):
        nonlocal at
        size = 1
        for extent in shape:
            size *= extent
        values = flat[at : at + size].reshape(shape)
        at += size
        return values

    d_norm_gain = take(LAYERS, features)
    bc_acc = take(LAYERS, 5, 2 * STATE)
    x_acc, gain_acc, head_acc = [], [], []
    for layer in range(LAYERS):
        x_acc.append(take(5, width))
        gain_acc.append(take(width))
        head_acc.append(take(3, heads))
    x_acc = jnp.stack(x_acc)
    head_acc = jnp.stack(head_acc)
    own_width = STATE // 2
    return (
        mixed,
        d_hidden,
        d_norm_gain,
        jnp.stack([d_z0, d_z1]),
        jnp.stack([d_x0, d_x1]),
        d_small[:, :, :own_width],
        d_small[:, :, own_width : own_width + heads],
        x_acc[:, :4],
        x_acc[:, 4],
        bc_acc[:, :4],
        bc_acc[:, 4],
        head_acc[:, 0],
        head_acc[:, 1],
        head_acc[:, 2],
        jnp.stack(gain_acc),
        jnp.stack([d_out0, d_out1]),
    )


def solution(mesh):
    in_specs = (
        P("dp", None),
        P("dp"),
        P(),
        P(None, "dp", "tensor"),
        P(None, "dp", "tensor"),
        P(None, "dp", None),
        P(None, "dp", "tensor"),
        P(None, None, "tensor"),
        P(None, "tensor"),
        P(),
        P(),
        P(None, "tensor"),
        P(None, "tensor"),
        P(None, "tensor"),
        P(None, "tensor"),
        P(None, "dp", "tensor"),
        P("dp", None),
    )
    out_specs = (
        P("dp", None),
        P("dp", None),
        P(),
        P(None, "dp", "tensor"),
        P(None, "dp", "tensor"),
        P(None, "dp", "tensor"),
        P(None, "dp", "tensor"),
        P(None, None, "tensor"),
        P(None, "tensor"),
        P(),
        P(),
        P(None, "tensor"),
        P(None, "tensor"),
        P(None, "tensor"),
        P(None, "tensor"),
        P(None, "dp", "tensor"),
    )
    return jax.shard_map(
        on_device, mesh=mesh, in_specs=in_specs, out_specs=out_specs, check_vma=False
    )
```

```python
import jax
import jax.numpy as jnp
from jax import lax
from jax.sharding import PartitionSpec as P
from jax.experimental import pallas as pl
from jax.experimental.pallas import tpu as pltpu

HEAD_DIM = 64
STATE = 128
PACK = 1024
LAYERS = 2
INNER = 3072
EPSILON = 1e-05
CHUNK = 128
LANES = 128
GROUP = 16
TAIL = 8
FAR = -10000.0
PRECISE = lax.Precision.HIGHEST
BF16 = jnp.bfloat16
F32 = jnp.float32
VMEM_BYTES = 48 * 1024 * 1024


def mm(lhs, rhs, precision=None):
    return lax.dot_general(
        lhs, rhs, (((1,), (0,)), ((), ())), precision=precision, preferred_element_type=F32
    )


def mm_t(lhs, rhs):
    return lax.dot_general(lhs, rhs, (((1,), (1,)), ((), ())), preferred_element_type=F32)


def t_mm(lhs, rhs):
    return lax.dot_general(lhs, rhs, (((0,), (0,)), ((), ())), preferred_element_type=F32)


def iota(shape, dim):
    return lax.broadcasted_iota(jnp.int32, shape, dim)


def expand(values, spread):
    lane = iota(values.shape, 1)
    high = values.astype(BF16).astype(F32)
    parts = jnp.where(lane < GROUP, high, jnp.where(lane < 2 * GROUP, values - high, 0.0))
    return mm(parts.astype(BF16), spread)


def shifted_back(joined, offset):
    return joined[TAIL - offset : TAIL - offset + CHUNK]


def conv_pre(joined, taps, bias_row, aux):
    summed = bias_row + taps[0:1] * joined[TAIL:]
    for offset in range(1, 4):
        summed = summed + taps[offset : offset + 1] * (
            shifted_back(joined, offset) * aux[:, offset : offset + 1]
        )
    return summed


def halves_rows(tile, low_lanes):
    zero = jnp.zeros_like(tile)
    return jnp.concatenate(
        [jnp.where(low_lanes, tile, zero), jnp.where(low_lanes, zero, tile)], 0
    )


def step_values(dt_ref, head_ref):
    raw = dt_ref + head_ref[0:1]
    dt = jnp.maximum(raw, 0.0) + jnp.log1p(jnp.exp(-jnp.abs(raw)))
    row = iota((CHUNK, CHUNK), 0)
    col = iota((CHUNK, CHUNK), 1)
    lower = (row >= col).astype(F32)
    log_decay = mm(lower, dt * head_ref[1:2], PRECISE)
    return raw, dt, log_decay, row, col


def scan_fwd_kernel(
    me_ref,
    x_ref,
    bcdt_ref,
    gate_ref,
    aux_ref,
    seg_ref,
    taps_ref,
    bias_ref,
    bc_taps_ref,
    bc_bias_ref,
    head_ref,
    skip_ref,
    gain_ref,
    spread_ref,
    u_ref,
    y_ref,
    sq_ref,
    kept_ref,
    state,
    tail_x,
    tail_bc,
):
    width = x_ref.shape[1]

    @pl.when(pl.program_id(0) == 0)
    def _():
        state[...] = jnp.zeros_like(state)
        tail_x[...] = jnp.zeros_like(tail_x)
        tail_bc[...] = jnp.zeros_like(tail_bc)

    aux = aux_ref[...]
    bc_now = bcdt_ref[:, : 2 * STATE]
    joined_bc = jnp.concatenate([tail_bc[...], bc_now], 0)
    tail_bc[...] = bc_now[CHUNK - TAIL :]
    bc_pre = conv_pre(joined_bc, bc_taps_ref[...], bc_bias_ref[...], aux)
    bc = bc_pre * jax.nn.sigmoid(bc_pre)
    b_low = bc[:, :STATE].astype(BF16)
    c_low = bc[:, STATE:].astype(BF16)
    b_turned = bc[:, :STATE].T.astype(BF16)
    _, dt, log_decay, row, col = step_values(bcdt_ref[:, 2 * STATE :], head_ref)
    log_turned = log_decay.T
    meet = mm_t(c_low, b_low)
    visible = (aux[:, 0:1] == seg_ref[0]) & (row >= col)
    spread = spread_ref[...]
    dt_wide = expand(dt, spread)
    reach = expand(jnp.exp(log_decay) * aux[:, 4:5], spread)
    to_end = expand(jnp.exp(log_decay[CHUNK - 1 :] - log_decay) * aux[:, 5:6], spread)
    state_low = state[...].astype(BF16)
    kept_ref[0] = state_low
    carried = mm(c_low, state_low)
    low_lanes = iota((CHUNK, LANES), 1) < HEAD_DIM
    squares = jnp.zeros((CHUNK, LANES), F32)
    for pair in range(width // LANES):
        at = slice(pair * LANES, (pair + 1) * LANES)
        now = x_ref[:, at]
        joined = jnp.concatenate([tail_x[:, at], now], 0)
        tail_x[:, at] = now[CHUNK - TAIL :]
        pre = conv_pre(joined, taps_ref[:, at], bias_ref[:, at], aux)
        x_conv = pre * jax.nn.sigmoid(pre)
        inputs = x_conv * dt_wide[:, at]
        mats = []
        for head in (2 * pair, 2 * pair + 1):
            gap = log_decay[:, head : head + 1] - log_turned[head : head + 1, :]
            mats.append((jnp.exp(jnp.where(visible, gap, FAR)) * meet).astype(BF16))
        local = mm(jnp.concatenate(mats, 1), halves_rows(inputs.astype(BF16), low_lanes))
        y = local + carried[:, at] * reach[:, at] + skip_ref[:, at] * x_conv
        y_ref[:, at] = y.astype(y_ref.dtype)
        ending = (inputs * to_end[:, at]).astype(BF16)
        state[:, at] = state[:, at] * reach[CHUNK - 1 :, at] + mm(b_turned, ending)
        gate = gate_ref[:, at].astype(F32)
        gated = y * (gate * jax.nn.sigmoid(gate))
        grown = gated * gain_ref[:, at]
        u_ref[:, at] = grown.astype(BF16)
        squares = squares + gated * gated
    ones = jnp.ones((8, LANES), F32)
    sums = lax.dot_general(
        ones, squares, (((1,), (1,)), ((), ())), precision=PRECISE, preferred_element_type=F32
    )
    sq_ref[...] = sums


def whole(shape):
    return pl.BlockSpec(shape, lambda *_: (0,) * len(shape))


def place_of(chunk, chunks, me_ref):
    part = chunks // 4
    away = chunk // part ^ me_ref[0]
    return (2 * (away % 2) + away // 2) * part + chunk % part


def scan_fwd(me, x_pre, bcdt_pre, gate_pre, side, weights):
    length, width = x_pre.shape
    chunks = length // CHUNK
    aux, seg_rows = side
    at = lambda c, m: (place_of(c, chunks, m), 0)
    tile = lambda columns: pl.BlockSpec((CHUNK, columns), at)
    in_specs = [
        tile(width),
        tile(bcdt_pre.shape[1]),
        tile(width),
        pl.BlockSpec((CHUNK, LANES), lambda c, m: (c, 0)),
        pl.BlockSpec((1, 1, CHUNK), lambda c, m: (c, 0, 0)),
    ] + [whole(w.shape) for w in weights]
    return pl.pallas_call(
        scan_fwd_kernel,
        grid_spec=pltpu.PrefetchScalarGridSpec(
            num_scalar_prefetch=1,
            grid=(chunks,),
            in_specs=in_specs,
            out_specs=[
                tile(width),
                tile(width),
                pl.BlockSpec((8, CHUNK), lambda c, m: (0, c)),
                pl.BlockSpec((1, STATE, width), lambda c, m: (c, 0, 0)),
            ],
            scratch_shapes=[
                pltpu.VMEM((STATE, width), F32),
                pltpu.VMEM((TAIL, width), F32),
                pltpu.VMEM((TAIL, 2 * STATE), F32),
            ],
        ),
        out_shape=[
            jax.ShapeDtypeStruct((length, width), BF16),
            jax.ShapeDtypeStruct((length, width), BF16),
            jax.ShapeDtypeStruct((8, length), F32),
            jax.ShapeDtypeStruct((chunks, STATE, width), BF16),
        ],
        compiler_params=pltpu.CompilerParams(vmem_limit_bytes=VMEM_BYTES),
        cost_estimate=pl.CostEstimate(
            flops=140 * length * width * LANES,
            bytes_accessed=20 * length * width,
            transcendentals=0,
        ),
        name="scan_fwd",
    )(me, x_pre, bcdt_pre, gate_pre, aux, seg_rows, *weights)


def gate_bwd_kernel(
    me_ref, gs_ref, y_ref, gate_ref, col_ref, gain_ref, g_gate_ref, g_y_ref, d_gain_ref
):
    @pl.when(pl.program_id(0) == 0)
    def _():
        d_gain_ref[...] = jnp.zeros_like(d_gain_ref)

    inv = col_ref[:, 0:1]
    pull = col_ref[:, 1:2]
    for pair in range(gs_ref.shape[1] // LANES):
        at = slice(pair * LANES, (pair + 1) * LANES)
        gs = gs_ref[:, at].astype(F32)
        y = y_ref[:, at].astype(F32)
        gate = gate_ref[:, at].astype(F32)
        sig = jax.nn.sigmoid(gate)
        act = gate * sig
        gated = y * act
        grown = gs * inv
        d_gain_ref[:, at] += jnp.sum(grown * gated, 0, keepdims=True)
        g_gated = grown * gain_ref[:, at] - gated * pull
        g_y_ref[:, at] = (g_gated * act).astype(BF16)
        g_gate_ref[:, at] = (g_gated * y * sig * (1.0 + gate * (1.0 - sig))).astype(BF16)


def gate_bwd(me, gs, y, gate_pre, columns, gain):
    length, width = gs.shape
    rows = length // 4
    tile = pl.BlockSpec((rows, width), lambda p, m: (p, 0))
    return pl.pallas_call(
        gate_bwd_kernel,
        grid_spec=pltpu.PrefetchScalarGridSpec(
            num_scalar_prefetch=1,
            grid=(4,),
            in_specs=[
                tile,
                tile,
                tile,
                pl.BlockSpec((rows, columns.shape[1]), lambda p, m: (2 * (p % 2) + p // 2 ^ m[0], 0)),
                whole(gain.shape),
            ],
            out_specs=[tile, tile, whole((1, width))],
        ),
        out_shape=[jax.ShapeDtypeStruct((length, width), BF16)] * 2
        + [jax.ShapeDtypeStruct((1, width), F32)],
        compiler_params=pltpu.CompilerParams(vmem_limit_bytes=VMEM_BYTES),
        cost_estimate=pl.CostEstimate(
            flops=50 * length * width * LANES,
            bytes_accessed=18 * length * width,
            transcendentals=0,
        ),
        name="gate_bwd",
    )(me, gs, y, gate_pre, columns, gain)


def conv_bwd(joined, joined_grad, grad, taps, aux, acc_ref, at):
    acc_ref[4:5, at] += jnp.sum(grad, 0, keepdims=True)
    acc_ref[0:1, at] += jnp.sum(grad * joined[TAIL:], 0, keepdims=True)
    result = taps[0:1] * grad
    for offset in range(1, 4):
        moved = shifted_back(joined, offset) * aux[:, offset : offset + 1]
        acc_ref[offset : offset + 1, at] += jnp.sum(grad * moved, 0, keepdims=True)
        later = joined_grad[offset : offset + CHUNK] * aux[:, 5 + offset : 6 + offset]
        result = result + taps[offset : offset + 1] * later
    return result


def scan_bwd_kernel(
    me_ref,
    g_ref,
    x_ref,
    x_tail_ref,
    bcdt_ref,
    bc_tail_ref,
    kept_ref,
    aux_ref,
    seg_ref,
    taps_ref,
    bias_ref,
    bc_taps_ref,
    bc_bias_ref,
    head_ref,
    skip_ref,
    gain_ref,
    spread_ref,
    gx_ref,
    gbc_ref,
    gdt_ref,
    accx_ref,
    accbc_ref,
    grad_state,
    next_x,
    next_bc,
):
    width = x_ref.shape[1]

    @pl.when(pl.program_id(0) == 0)
    def _():
        grad_state[...] = jnp.zeros_like(grad_state)
        next_x[...] = jnp.zeros_like(next_x)
        next_bc[...] = jnp.zeros_like(next_bc)
        accx_ref[...] = jnp.zeros_like(accx_ref)
        accbc_ref[...] = jnp.zeros_like(accbc_ref)

    aux = aux_ref[...]
    joined_bc = jnp.concatenate([bc_tail_ref[:, : 2 * STATE], bcdt_ref[:, : 2 * STATE]], 0)
    bc_pre = conv_pre(joined_bc, bc_taps_ref[...], bc_bias_ref[...], aux)
    bc_sig = jax.nn.sigmoid(bc_pre)
    bc = bc_pre * bc_sig
    b_low = bc[:, :STATE].astype(BF16)
    c_low = bc[:, STATE:].astype(BF16)
    c_turned = bc[:, STATE:].T.astype(BF16)
    raw, dt, log_decay, row, col = step_values(bcdt_ref[:, 2 * STATE :], head_ref)
    log_turned = log_decay.T
    meet = mm_t(b_low, c_low)
    visible = (aux[:, 0:1] == seg_ref[0]) & (row <= col)
    spread = spread_ref[...]
    dt_wide = expand(dt, spread)
    reach = expand(jnp.exp(log_decay) * aux[:, 4:5], spread)
    to_end = expand(jnp.exp(log_decay[CHUNK - 1 :] - log_decay) * aux[:, 5:6], spread)
    low_lanes = iota((CHUNK, LANES), 1) < HEAD_DIM
    lane = iota((CHUNK, LANES), 1)
    grad_meet = jnp.zeros((CHUNK, CHUNK), F32)
    grad_b = jnp.zeros((CHUNK, STATE), F32)
    grad_c = jnp.zeros((CHUNK, STATE), F32)
    col_sums = jnp.zeros((CHUNK, LANES), F32)
    row_sums = jnp.zeros((LANES, CHUNK), F32)
    head_sums = jnp.zeros((3 * CHUNK, LANES), F32)
    through = jnp.zeros((8, LANES), F32)
    head_row = iota((LANES, CHUNK), 0)
    for pair in range(width // LANES):
        at = slice(pair * LANES, (pair + 1) * LANES)
        joined = jnp.concatenate([x_tail_ref[:, at], x_ref[:, at]], 0)
        pre = conv_pre(joined, taps_ref[:, at], bias_ref[:, at], aux)
        sig = jax.nn.sigmoid(pre)
        x_conv = pre * sig
        inputs = x_conv * dt_wide[:, at]
        g_low = g_ref[:, at]
        g = g_low.astype(F32)
        grad_mats = mm_t(halves_rows(inputs.astype(BF16), low_lanes), g_low)
        mats = []
        for member in range(2):
            head = 2 * pair + member
            gap = log_turned[head : head + 1, :] - log_decay[:, head : head + 1]
            weight = jnp.exp(jnp.where(visible, gap, FAR))
            mats.append((weight * meet).astype(BF16))
            part = weight * grad_mats[member * CHUNK : (member + 1) * CHUNK]
            grad_meet = grad_meet + part
            product = part * meet
            col_sums = jnp.where(lane == head, jnp.sum(product, 1, keepdims=True), col_sums)
            row_sums = jnp.where(head_row == head, jnp.sum(product, 0, keepdims=True), row_sums)
        local = mm(jnp.concatenate(mats, 1), halves_rows(g_low, low_lanes))
        reach_now = reach[:, at]
        to_end_now = to_end[:, at]
        state_low = kept_ref[0, :, at]
        coming = g * reach_now
        coming_low = coming.astype(BF16)
        carried = mm(c_low, state_low)
        grad_c = grad_c + mm_t(coming_low, state_low)
        grad_state_now = grad_state[:, at]
        grad_state_low = grad_state_now.astype(BF16)
        leaving = mm(b_low, grad_state_low)
        ending = inputs * to_end_now
        grad_b = grad_b + mm_t(ending.astype(BF16), grad_state_low)
        last = reach_now[CHUNK - 1 :]
        passed = jnp.sum(grad_state_now * state_low.astype(F32), 0, keepdims=True) * last
        through = through + mm_t(
            jnp.broadcast_to(passed, (8, LANES)).astype(BF16), spread[:, at]
        )
        grad_state[:, at] = grad_state_now * last + mm(c_turned, coming_low)
        grad_inputs = local + leaving * to_end_now
        stacked = jnp.concatenate([coming * carried, ending * leaving, grad_inputs * x_conv], 0)
        head_sums = head_sums + mm_t(stacked.astype(BF16), spread[:, at])
        accx_ref[5:6, at] += jnp.sum(g * x_conv, 0, keepdims=True)
        grad_conv = (grad_inputs * dt_wide[:, at] + g * skip_ref[:, at]) * (
            sig * (1.0 + pre * (1.0 - sig))
        )
        joined_grad = jnp.concatenate([grad_conv, next_x[:, at]], 0)
        next_x[:, at] = grad_conv[:TAIL]
        gx_ref[:, at] = conv_bwd(
            joined, joined_grad, grad_conv, taps_ref[:, at], aux, accx_ref, at
        ).astype(BF16)
    upper = (row <= col).astype(F32)
    strict = (row > col).astype(F32)
    straddle = (
        mm(upper, row_sums.T - col_sums + head_sums[:CHUNK], PRECISE)
        + mm(strict, head_sums[CHUNK : 2 * CHUNK], PRECISE)
        + through[0:1]
    )
    grad_dt = head_sums[2 * CHUNK :] + head_ref[1:2] * straddle
    grad_raw = jnp.where(lane < GROUP, grad_dt * jax.nn.sigmoid(raw), 0.0)
    gdt_ref[...] = grad_raw.astype(BF16)
    accx_ref[6:7, :LANES] += jnp.sum(grad_raw, 0, keepdims=True)
    accx_ref[7:8, :LANES] += jnp.sum(dt * straddle, 0, keepdims=True)
    grad_meet_low = grad_meet.astype(BF16)
    grad_b = grad_b + mm(grad_meet_low, c_low)
    grad_c = grad_c + t_mm(grad_meet_low, b_low)
    grad_bc = jnp.concatenate([grad_b, grad_c], 1) * (bc_sig * (1.0 + bc_pre * (1.0 - bc_sig)))
    joined_grad = jnp.concatenate([grad_bc, next_bc[...]], 0)
    next_bc[...] = grad_bc[:TAIL]
    gbc_ref[...] = conv_bwd(
        joined_bc, joined_grad, grad_bc, bc_taps_ref[...], aux, accbc_ref, slice(None)
    ).astype(BF16)


def scan_bwd(me, g_y, x_pre, bcdt_pre, kept, side, weights):
    length, width = x_pre.shape
    chunks = length // CHUNK
    aux, seg_rows = side
    back = lambda c: chunks - 1 - c
    place = lambda c, m: place_of(back(c), chunks, m)
    tile = lambda columns: pl.BlockSpec((CHUNK, columns), lambda c, m: (place(c, m), 0))

    def tail_at(c, m):
        before = place_of(jnp.maximum(back(c) - 1, 0), chunks, m)
        return (before * (CHUNK // TAIL) + CHUNK // TAIL - 1, 0)

    tail = lambda columns: pl.BlockSpec((TAIL, columns), tail_at)
    wide = bcdt_pre.shape[1]
    in_specs = [
        tile(width),
        tile(width),
        tail(width),
        tile(wide),
        tail(wide),
        pl.BlockSpec((1, STATE, width), lambda c, m: (back(c), 0, 0)),
        pl.BlockSpec((CHUNK, LANES), lambda c, m: (back(c), 0)),
        pl.BlockSpec((1, 1, CHUNK), lambda c, m: (back(c), 0, 0)),
    ] + [whole(w.shape) for w in weights]
    return pl.pallas_call(
        scan_bwd_kernel,
        grid_spec=pltpu.PrefetchScalarGridSpec(
            num_scalar_prefetch=1,
            grid=(chunks,),
            in_specs=in_specs,
            out_specs=[
                tile(width),
                tile(2 * STATE),
                tile(LANES),
                whole((8, width)),
                whole((8, 2 * STATE)),
            ],
            scratch_shapes=[
                pltpu.VMEM((STATE, width), F32),
                pltpu.VMEM((TAIL, width), F32),
                pltpu.VMEM((TAIL, 2 * STATE), F32),
            ],
        ),
        out_shape=[
            jax.ShapeDtypeStruct((length, width), BF16),
            jax.ShapeDtypeStruct((length, 2 * STATE), BF16),
            jax.ShapeDtypeStruct((length, LANES), BF16),
            jax.ShapeDtypeStruct((8, width), F32),
            jax.ShapeDtypeStruct((8, 2 * STATE), F32),
        ],
        compiler_params=pltpu.CompilerParams(vmem_limit_bytes=VMEM_BYTES),
        cost_estimate=pl.CostEstimate(
            flops=280 * length * width * LANES,
            bytes_accessed=20 * length * width,
            transcendentals=0,
        ),
        name="scan_bwd",
    )(me, g_y, x_pre, x_pre, bcdt_pre, bcdt_pre, kept, aux, seg_rows, *weights)


def side_arrays(segments):
    length = segments.shape[0]
    seg = segments.astype(F32)
    columns = [seg]
    nothing = lambda count: jnp.full((count,), -1.0, F32)
    for offset in range(1, 4):
        moved = jnp.concatenate([nothing(offset), seg[: length - offset]], 0)
        columns.append((moved == seg).astype(F32))
    blocks = seg.reshape(-1, CHUNK)
    ends = blocks[:, -1]
    before = jnp.concatenate([nothing(1), ends[:-1]], 0)
    columns.append((blocks == before[:, None]).astype(F32).reshape(-1))
    columns.append((blocks == ends[:, None]).astype(F32).reshape(-1))
    for offset in range(1, 4):
        moved = jnp.concatenate([seg[offset:], nothing(offset)], 0)
        columns.append((moved == seg).astype(F32))
    stacked = jnp.stack(columns, 1)
    aux = jnp.pad(stacked, ((0, 0), (0, LANES - stacked.shape[1])))
    return aux, blocks.reshape(-1, 1, CHUNK)


def in_groups(values):
    padded = jnp.pad(values, [(0, 0)] * (values.ndim - 1) + [(0, GROUP - values.shape[-1])])
    return jnp.tile(padded, (1,) * (values.ndim - 1) + (LANES // GROUP,))


def spread_matrix(width):
    head = lax.broadcasted_iota(jnp.int32, (LANES, width), 0) % GROUP
    owner = lax.broadcasted_iota(jnp.int32, (LANES, width), 1) // HEAD_DIM
    return (head == owner).astype(BF16)


def scan_weights(taps, bias, bc_taps, bc_bias, dt_bias, a_log, d_skip, gain, spread):
    rates = -jnp.exp(a_log)
    rows = jnp.stack([in_groups(dt_bias), in_groups(rates)])
    head = jnp.pad(rows, ((0, 6), (0, 0)))
    return (
        taps,
        bias[None],
        bc_taps,
        bc_bias[None],
        head,
        jnp.repeat(d_skip, HEAD_DIM)[None],
        gain[None],
        spread,
    )


def partners(count, step):
    return [(index, index ^ step) for index in range(count)]


def swap(values, axis, step):
    return lax.ppermute(values, axis, partners(lax.axis_size(axis), step))


def after(values, *earlier):
    return lax.optimization_barrier((values, *earlier))[0]


def dp_masks():
    masks = []
    step = lax.axis_size("dp") // 2
    while step > 0:
        masks.append(step)
        step = step // 2
    return masks


def offsets(masks):
    found = [0]
    for mask in masks:
        found = found + [offset ^ mask for offset in found]
    return found


class Rows:
    def __init__(self, own):
        self.rows = own

    def stage(self, mask, *earlier):
        got = swap(after(self.rows, *earlier), "dp", mask)
        self.rows = jnp.concatenate([self.rows, got], 0)
        return got

    def begin(self, masks, *earlier):
        for mask in masks[:-2]:
            got = self.stage(mask, *earlier)
            earlier = ()
        return got


def scatter_first(kept, got):
    total = kept + got.astype(F32)
    height = total.shape[0] // 2
    return total[:height], total[height:].astype(BF16)


def scatter_rest(kept, sent, masks):
    for mask in reversed(masks[1:-1]):
        kept, sent = scatter_first(kept, swap(sent, "dp", mask))
    return kept + swap(sent, "dp", masks[0]).astype(F32)


def grad_half(rows, grads, which):
    width = rows.shape[1] // 2
    dims = (((0,), (0,)), ((), ()))
    taken = rows[:, which * width : (which + 1) * width]
    return lax.dot_general(taken, grads, dims, preferred_element_type=F32)


def sent_half(rows, grads):
    return grad_half(rows, grads, 1).astype(BF16)


def reordered(values, me):
    size = values.shape[0] // 4
    return jnp.concatenate(
        [lax.dynamic_slice_in_dim(values, (away ^ me) * size, size, 0) for away in (0, 2, 1, 3)], 0
    )


def restored(values, me):
    size = values.shape[0] // 4
    parts = []
    for part in range(4):
        away = part ^ me
        parts.append(
            lax.dynamic_slice_in_dim(values, (2 * (away % 2) + away // 2) * size, size, 0)
        )
    return jnp.concatenate(parts, 0)


def turned_over(values, size):
    shaped = values.reshape(-1, 2, size, values.shape[1])
    return shaped[:, ::-1].reshape(values.shape)


def own_quarter(values, me):
    size = values.shape[0] // 4
    return lax.dynamic_slice_in_dim(values, me * size, size, 0)


def tensor_sum(values):
    values = values + swap(values, "tensor", 1)
    return values + swap(values, "tensor", 2)


def dp_sum(values):
    step = 1
    while step < lax.axis_size("dp"):
        values = values + swap(values, "dp", step)
        step = 2 * step
    return values


def dot(lhs, rhs):
    return lax.dot_general(lhs, rhs, (((1,), (0,)), ((), ())), preferred_element_type=F32)


def dot_t(lhs, rhs):
    return lax.dot_general(lhs, rhs, (((1,), (1,)), ((), ())), preferred_element_type=F32)


def own_order(features, masks, earlier):
    place = after(lax.axis_index("dp"), earlier)
    found = offsets(masks)
    height = features // len(found)
    index = lax.broadcasted_iota(jnp.int32, (1, features), 1)
    part, within = index // height, index % height
    away = jnp.zeros_like(part)
    for position, offset in enumerate(found):
        away = jnp.where(part == position, offset, away)
    source = (away ^ place) * height + within
    return (lax.broadcasted_iota(jnp.int32, (features, features), 0) == source).astype(BF16)


def rms_of(stream):
    return lax.rsqrt(jnp.mean(stream * stream, -1, keepdims=True) + EPSILON)


def on_device(
    hidden,
    segments,
    norm_gain,
    w_z,
    w_x,
    w_bc,
    w_dt,
    conv_x_w,
    conv_x_b,
    conv_bc_w,
    conv_bc_b,
    dt_bias,
    a_log,
    d_skip,
    gated_gain,
    w_out,
    cotangent,
):
    length, features = hidden.shape
    width = w_x.shape[2]
    heads = dt_bias.shape[1]
    masks = dp_masks()
    place = lax.axis_index("tensor")
    core, far = place % 2, place // 2
    me = place
    me_row = me.astype(jnp.int32)[None]
    half = length // 2
    quarter = length // 4

    side_first = masks[-1:] + masks[:-1]
    seated = [offsets(side_first).index(offset) for offset in offsets(masks)]
    height = w_x.shape[1]
    quart_bc = w_bc.shape[2] // 4
    own_bc = lax.dynamic_slice_in_dim(w_bc, place * quart_bc, quart_bc, 2)
    w_small = jnp.concatenate([own_bc[0], own_bc[1], w_dt[0], w_dt[1]], 1)
    w_small = jnp.pad(w_small, ((0, 0), (0, 2 * LANES - w_small.shape[1])))

    x0, z0, out0 = Rows(w_x[0]), Rows(w_z[0]), Rows(w_out[0])
    x1, z1, out1 = Rows(w_x[1]), Rows(w_z[1]), Rows(w_out[1])
    small = Rows(w_small)
    near_mask, side_mask = masks[-2:]
    x0_far = x0.begin(masks)
    out1_side = out1.stage(side_mask)
    x0_near = x0.stage(near_mask)
    small_far = small.begin(masks, x0_far)
    z0_far = z0.begin(masks, x0_near, small_far)
    small_near = small.stage(near_mask, x0_near)
    x0.stage(side_mask)
    out0_far = out0.begin(masks, small_near, z0_far)
    z0_near = z0.stage(near_mask, small_near)
    small.stage(side_mask)
    x1_far = x1.begin(masks, z0_near, out0_far)
    out0_near = out0.stage(near_mask, z0_near)
    z0.stage(side_mask)
    z1_far = z1.begin(masks, out0_near, x1_far)
    x1_near = x1.stage(near_mask, out0_near)
    out0.stage(side_mask)
    out1_far = out1.begin(masks, x1_near, z1_far)
    z1_near = z1.stage(near_mask, x1_near)
    x1_side = x1.stage(side_mask)
    out1_near = out1.stage(near_mask, z1_near)
    z1_side = z1.stage(side_mask)
    out1_rows = [out1.rows[seat * height : (seat + 1) * height] for seat in seated]
    x_rows, z_rows = [x0.rows, x1.rows], [z0.rows, z1.rows]
    out_rows = [out0.rows, jnp.concatenate(out1_rows, 0)]
    small_rows = small.rows

    own_cols = small_rows[:, :LANES]
    across = swap(own_cols, "tensor", 2)
    beside = swap(jnp.concatenate([own_cols, across], 1), "tensor", 1)

    def small_columns(layer):
        low = layer * quart_bc
        parts = [
            own_cols[:, low : low + quart_bc],
            across[:, low : low + quart_bc],
            beside[:, low : low + quart_bc],
            beside[:, LANES + low : LANES + low + quart_bc],
        ]
        first = core == 0
        near = [jnp.where(first, parts[0], parts[2]), jnp.where(first, parts[2], parts[0])]
        away = [jnp.where(first, parts[1], parts[3]), jnp.where(first, parts[3], parts[1])]
        first = far == 0
        ordered = [jnp.where(first, n, a) for n, a in zip(near, away)]
        ordered += [jnp.where(first, a, n) for n, a in zip(near, away)]
        at = LANES + layer * heads
        return jnp.concatenate(ordered + [in_groups(small_rows[:, at : at + heads])], 1)

    bcdt_rows = [small_columns(layer) for layer in range(LAYERS)]

    order = lax.optimization_barrier(own_order(features, masks, x0_far))
    side = side_arrays(after(segments, x0_far))
    spread = spread_matrix(width)
    weights = [
        scan_weights(
            conv_x_w[layer],
            conv_x_b[layer],
            conv_bc_w[layer],
            conv_bc_b[layer],
            dt_bias[layer],
            a_log[layer],
            d_skip[layer],
            gated_gain[layer],
            spread,
        )
        for layer in range(LAYERS)
    ]
    order, side, weights = lax.optimization_barrier((order, side, weights))
    hidden_rows = reordered(after(hidden, x0_far), me)
    hidden_low = dot(after(hidden_rows, x0_near, small_far, out1_side), order).astype(BF16)
    cotangent_rows = reordered(after(cotangent, x0_far), me)
    cotangent_low = dot(after(cotangent_rows, small_near, z0_far), order).astype(BF16)
    gains = mm(after(norm_gain, small_near), order.astype(F32), PRECISE)
    hidden_low, cotangent_low, gains = lax.optimization_barrier(
        (hidden_low, cotangent_low, gains)
    )

    def columns_of(values, which):
        return lax.dynamic_slice_in_dim(values, which * STATE, STATE, 1)

    stream = hidden_low.astype(F32)
    normed0 = (stream * rms_of(stream) * gains[0]).astype(BF16)
    stream0 = hidden_low[:quarter].astype(F32)
    x_pre0 = dot(normed0, x_rows[0])
    bcdt_pre0 = dot(after(normed0, x_pre0, z0_near, out0_far), bcdt_rows[0])
    gate_pre0 = dot(after(normed0, bcdt_pre0, out0_near, x1_far), z_rows[0]).astype(BF16)
    u0, y0, sq, kept0 = scan_fwd(me_row, x_pre0, bcdt_pre0, gate_pre0, side, weights[0])
    u_now = after(u0, x1_near, z1_far)
    sent = dot_t(u_now[half:], out_rows[0]).astype(BF16)
    sq = sq[0:1]
    sq = sq + swap(sq, "tensor", 1)
    u_now = after(u_now, sent, sq)
    mine = dot_t(u_now[:half], out_rows[0]) + swap(sent, "tensor", 1).astype(F32)
    sq = sq + swap(sq, "tensor", 2)
    away = after(mine[quarter:].astype(BF16), sq)
    got = swap(away, "tensor", 2)
    inv0 = lax.rsqrt(sq / INNER + EPSILON)[0]
    got, mine, z1_near, out1_far, x1_side = lax.optimization_barrier(
        (got, mine, z1_near, out1_far, x1_side)
    )
    total0 = mine[:quarter] + got.astype(F32)
    stream1 = stream0 + own_quarter(inv0, me)[:, None] * total0
    normed_own = (stream1 * rms_of(stream1) * gains[1]).astype(BF16)
    normed_half = jnp.concatenate([normed_own, swap(normed_own, "tensor", 2)], 0)
    normed_half, z1_side = lax.optimization_barrier((normed_half, z1_side))
    normed1 = jnp.concatenate([normed_half, swap(normed_half, "tensor", 1)], 0)
    scaled0 = (u0.astype(F32) * reordered(inv0, me)[:, None]).astype(BF16)

    x_pre1 = dot(after(normed1, out1_near), x_rows[1])
    bcdt_pre1 = dot(normed1, bcdt_rows[1])
    gate_pre1 = dot(normed1, z_rows[1]).astype(BF16)
    u1, y1, sq, kept1 = scan_fwd(me_row, x_pre1, bcdt_pre1, gate_pre1, side, weights[1])
    scaled_grad1 = dot(cotangent_low, out_rows[1])
    cross = restored(jnp.sum(scaled_grad1 * u1.astype(F32), -1), me)
    both = tensor_sum(jnp.stack([sq[0], cross]))
    mixed_sent = dot_t(u1[half:], out_rows[1]).astype(BF16)
    mixed_mine = dot_t(u1[:half], out_rows[1])
    mixed_mine = mixed_mine + swap(mixed_sent, "tensor", 1).astype(F32)
    both = after(both, mixed_sent, mixed_mine)
    mixed_got = swap(mixed_mine[quarter:].astype(BF16), "tensor", 2)
    inv1 = lax.rsqrt(both[0] / INNER + EPSILON)

    columns = jnp.stack([inv1, inv1 * inv1 * inv1 * both[1] / INNER], 1)
    g_gate1, g_y, d_gain1 = gate_bwd(
        me_row, scaled_grad1, y1, gate_pre1, columns, gated_gain[1][None]
    )
    z_sent = sent_half(normed1, g_gate1)
    z_got = swap(z_sent, "dp", 1)
    g_y = after(g_y, z_sent)
    g_x1, g_bc1, g_dt1, acc_x1, acc_bc1 = scan_bwd(
        me_row, g_y, x_pre1, bcdt_pre1, kept1, side, weights[1]
    )
    g_x1, z_got, mixed_got = lax.optimization_barrier((g_x1, z_got, mixed_got))

    def grad_rows(rows, g_gate, g_x, g_bcdt, layer):
        return (
            dot_t(g_gate[rows], z_rows[layer])
            + dot_t(g_x[rows], x_rows[layer])
            + dot_t(g_bcdt[rows], bcdt_rows[layer])
        )

    g_bcdt = jnp.concatenate([g_bc1, g_dt1], 1)
    sent = grad_rows(slice(half, length), g_gate1, g_x1, g_bcdt, 1).astype(BF16)
    cotangent_now = after(cotangent_low, sent)
    scaled1 = (u1.astype(F32) * reordered(inv1, me)[:, None]).astype(BF16)
    out_sent = sent_half(cotangent_now, scaled1)
    out_got = swap(out_sent, "dp", 1)
    own = grad_rows(slice(0, half), after(g_gate1, out_sent), g_x1, g_bcdt, 1)
    mine = own + swap(sent, "tensor", 1).astype(F32)
    away = mine[quarter:].astype(BF16)
    got = swap(away, "tensor", 2)
    normed_now = after(normed1, away)
    z_kept, z_next = scatter_first(grad_half(normed_now, g_gate1, 0), z_got)
    z_near = swap(z_next, "dp", near_mask)
    normed_now = after(normed_now, z_next)
    x_sent = sent_half(normed_now, g_x1)
    x_kept_half = grad_half(normed_now, g_x1, 0)
    out_kept_half = grad_half(after(cotangent_now, away), scaled1, 0)
    mixed_total = mixed_mine[:quarter] + mixed_got.astype(F32)
    last = stream1 + own_quarter(inv1, me)[:, None] * mixed_total
    mixed_own = dot_t(last.astype(BF16), order).astype(BF16)
    got, mine, out_got, z_near, x_sent, out_kept_half, x_kept_half, mixed_own = (
        lax.optimization_barrier(
            (got, mine, out_got, z_near, x_sent, out_kept_half, x_kept_half, mixed_own)
        )
    )
    x_got = swap(x_sent, "dp", 1)
    total = mine[:quarter] + got.astype(F32)
    rms = rms_of(stream1)
    normal = stream1 * rms
    grown = total * gains[1]
    grad_stream = cotangent_low[:quarter].astype(F32) + rms * (
        grown - normal * jnp.mean(grown * normal, -1, keepdims=True)
    )
    grad_own = grad_stream.astype(BF16)
    out_kept, out_next = scatter_first(out_kept_half, out_got)
    out_near = swap(out_next, "dp", near_mask)
    z_kept, z_next = scatter_first(z_kept, z_near)
    z_far = swap(z_next, "dp", masks[-3])
    total_now = after(total, grad_own)
    d_norm1 = jnp.sum(total_now * normal, 0)
    cross = jnp.sum(grad_own.astype(F32) * total0, -1)
    grad_half_rows = jnp.concatenate([grad_own, swap(grad_own, "tensor", 2)], 0)
    cross = jnp.concatenate([cross, swap(cross, "tensor", 2)], 0)
    grad_half_rows, cross, z_far, out_near = lax.optimization_barrier(
        (grad_half_rows, cross, z_far, out_near)
    )
    grad0 = jnp.concatenate([grad_half_rows, swap(grad_half_rows, "tensor", 1)], 0)
    cross = restored(jnp.concatenate([cross, swap(cross, "tensor", 1)], 0), me)
    out_kept, out_next = scatter_first(out_kept, out_near)
    out_far = swap(out_next, "dp", masks[-3])

    grad0 = lax.optimization_barrier(grad0)
    out_sent0 = sent_half(grad0, scaled0)
    out_got0 = swap(out_sent0, "dp", 1)
    scaled_grad0 = dot(after(grad0, out_sent0), out_rows[0])
    columns = jnp.stack([inv0, inv0 * inv0 * inv0 * cross / INNER], 1)
    g_gate0, g_y, d_gain0 = gate_bwd(
        me_row, scaled_grad0, y0, gate_pre0, columns, gated_gain[0][None]
    )
    z_sent0 = sent_half(normed0, g_gate0)
    z_got0 = swap(z_sent0, "dp", 1)
    g_y, z_sent0, x_got, out_far = lax.optimization_barrier((g_y, z_sent0, x_got, out_far))
    x_kept, x_next = scatter_first(x_kept_half, x_got)
    x_near = swap(x_next, "dp", near_mask)
    g_y = after(g_y, x_next)
    mixed = lax.all_gather(after(mixed_own, grad0), "tensor", axis=0).reshape(length, features)
    away1 = swap(after(columns_of(g_bc1, 1 - far), grad0), "tensor", 2)
    g_x0, g_bc0, g_dt0, acc_x0, acc_bc0 = scan_bwd(
        me_row, g_y, x_pre0, bcdt_pre0, kept0, side, weights[0]
    )
    away0 = swap(columns_of(g_bc0, 1 - far), "tensor", 2)
    g_x0, away1, x_near, out_got0 = lax.optimization_barrier((g_x0, away1, x_near, out_got0))
    x_sent0 = sent_half(normed0, g_x0)
    x_got0 = swap(x_sent0, "dp", 1)
    g_x0 = after(g_x0, x_sent0)
    g_bcdt = jnp.concatenate([g_bc0, g_dt0], 1)
    sent = grad_rows(slice(half, length), g_gate0, g_x0, g_bcdt, 0).astype(BF16)
    out_kept_half0 = grad_half(after(grad0, sent), scaled0, 0)
    out_kept0, out_next0 = scatter_first(out_kept_half0, out_got0)
    out_near0 = swap(out_next0, "dp", near_mask)
    own = grad_rows(slice(0, half), after(g_gate0, out_next0), g_x0, g_bcdt, 0)
    mine = own + swap(sent, "tensor", 1).astype(F32)
    away = mine[quarter:].astype(BF16)
    got = swap(away, "tensor", 2)
    normed_now, z_got0, x_near, away0, _ = lax.optimization_barrier(
        (normed0, z_got0, x_near, away0, away)
    )
    z_kept0, z_next0 = scatter_first(grad_half(normed_now, g_gate0, 0), z_got0)
    z_near0 = swap(z_next0, "dp", near_mask)
    normed_now = after(normed_now, z_next0)
    x_kept, x_next = scatter_first(x_kept, x_near)
    x_kept_half0 = grad_half(normed_now, g_x0, 0)
    x_kept_half0, out_near0, x_next = lax.optimization_barrier((x_kept_half0, out_near0, x_next))
    x_far = swap(x_next, "dp", masks[-3])
    out_kept0, out_next0 = scatter_first(out_kept0, out_near0)
    out_far0 = swap(out_next0, "dp", masks[-3])
    got, mine, x_got0, z_near0, out_next0 = lax.optimization_barrier(
        (got, mine, x_got0, z_near0, out_next0)
    )
    total = mine[:quarter] + got.astype(F32)
    rms = rms_of(stream0)
    normal = stream0 * rms
    grown = total * gains[0]
    grad_stream = grad_stream + rms * (
        grown - normal * jnp.mean(grown * normal, -1, keepdims=True)
    )
    d_hidden = dot_t(grad_stream.astype(BF16), order).astype(BF16)
    x_kept0, x_next0 = scatter_first(x_kept_half0, x_got0)
    x_near0 = swap(x_next0, "dp", near_mask)
    z_kept0, z_next0 = scatter_first(z_kept0, z_near0)
    z_far0 = swap(z_next0, "dp", masks[-3])
    total_now = after(total, d_hidden)
    d_norm0 = jnp.sum(total_now * normal, 0)
    d_hidden = jnp.concatenate([d_hidden, swap(d_hidden, "tensor", 2)], 0)
    d_hidden = jnp.concatenate([d_hidden, swap(d_hidden, "tensor", 1)], 0)
    d_hidden = restored(d_hidden, me).astype(F32)

    def finished(kept, sent):
        for mask in reversed(masks[:-3]):
            kept, sent = scatter_first(kept, sent)
            sent = swap(sent, "dp", mask)
        return kept + sent.astype(F32)

    x_kept0, x_next0 = scatter_first(x_kept0, x_near0)
    d_out1 = finished(out_kept, out_far)
    d_x1 = finished(x_kept, x_far)
    d_z1 = finished(z_kept, z_far)
    d_out0 = finished(out_kept0, out_far0)
    d_z0 = finished(z_kept0, z_far0)
    d_x0 = finished(x_kept0, swap(x_next0, "dp", masks[-3]))

    near_cols = jnp.concatenate([columns_of(v, far) for v in (g_bc0, g_bc1)], 1)
    away_cols = jnp.concatenate([away0, away1], 1)
    bc_sum = near_cols.astype(F32) + turned_over(away_cols, quarter).astype(F32)
    across_sum = swap(bc_sum.astype(BF16), "tensor", 1)
    bc_sum = bc_sum + turned_over(across_sum, half).astype(F32)
    small_sent, small_kept = [], []
    for layer, (rows, g_dt) in enumerate(((normed0, g_dt0), (normed1, g_dt1))):
        summed = bc_sum[:, layer * STATE : (layer + 1) * STATE]
        rolled = jnp.roll(summed, STATE // 2, 1)
        own_cols = jnp.where(core == 0, summed, rolled)[:, : STATE // 2].astype(BF16)
        own_cols = jnp.concatenate([own_cols, g_dt[:, : STATE // 2]], 1)
        small_sent.append(sent_half(rows, own_cols))
        small_kept.append(grad_half(rows, own_cols, 0))
    small_sent = after(jnp.concatenate(small_sent, 1), x_got0)
    small_got = swap(small_sent, "dp", 1)
    small_kept, small_next = scatter_first(jnp.concatenate(small_kept, 1), small_got)
    d_small = scatter_rest(small_kept, small_next, masks)
    d_small = jnp.stack([d_small[:, layer * LANES : (layer + 1) * LANES] for layer in range(LAYERS)])
    found = jnp.array(offsets(masks), jnp.int32)
    norm_part = jnp.stack([d_norm0, d_norm1]).reshape(LAYERS, len(found), 1, height)
    here = (found ^ lax.axis_index("dp"))[:, None] == jnp.arange(len(found))[None]
    norm_part = jnp.sum(jnp.where(here[None, :, :, None], norm_part, 0.0), 1)
    shared = jnp.concatenate(
        [acc_bc0, acc_bc1, jnp.zeros((8, width - 4 * STATE), F32)], 1
    )
    shared = tensor_sum(jnp.concatenate([shared, norm_part.reshape(-1, width)], 0))
    gains_part = jnp.concatenate([d_gain0, d_gain1], 0)
    summed = dp_sum(jnp.concatenate([acc_x0, acc_x1, gains_part, shared], 0))
    acc = summed[:16].reshape(LAYERS, 8, width)
    shared = summed[16 + LAYERS :]
    bc_acc = jnp.stack([shared[:8, : 2 * STATE], shared[:8, 2 * STATE : 4 * STATE]])
    d_norm_gain = shared[8:].reshape(LAYERS, features)
    d_skips = acc[:, 5].reshape(LAYERS, heads, HEAD_DIM).sum(2)
    own_width = STATE // 2
    return (
        mixed,
        d_hidden,
        d_norm_gain,
        jnp.stack([d_z0, d_z1]),
        jnp.stack([d_x0, d_x1]),
        d_small[:, :, :own_width],
        d_small[:, :, own_width : own_width + heads],
        acc[:, :4],
        acc[:, 4],
        bc_acc[:, :4],
        bc_acc[:, 4],
        acc[:, 6, :heads],
        acc[:, 7, :heads] * -jnp.exp(a_log),
        d_skips,
        summed[16 : 16 + LAYERS],
        jnp.stack([d_out0, d_out1]),
    )


def solution(mesh):
    in_specs = (
        P("dp", None),
        P("dp"),
        P(),
        P(None, "dp", "tensor"),
        P(None, "dp", "tensor"),
        P(None, "dp", None),
        P(None, "dp", "tensor"),
        P(None, None, "tensor"),
        P(None, "tensor"),
        P(),
        P(),
        P(None, "tensor"),
        P(None, "tensor"),
        P(None, "tensor"),
        P(None, "tensor"),
        P(None, "dp", "tensor"),
        P("dp", None),
    )
    out_specs = (
        P("dp", None),
        P("dp", None),
        P(),
        P(None, "dp", "tensor"),
        P(None, "dp", "tensor"),
        P(None, "dp", "tensor"),
        P(None, "dp", "tensor"),
        P(None, None, "tensor"),
        P(None, "tensor"),
        P(),
        P(),
        P(None, "tensor"),
        P(None, "tensor"),
        P(None, "tensor"),
        P(None, "tensor"),
        P(None, "dp", "tensor"),
    )
    return jax.shard_map(
        on_device, mesh=mesh, in_specs=in_specs, out_specs=out_specs, check_vma=False
    )
```

```python
import jax
import jax.numpy as jnp
from jax import lax
from jax.sharding import PartitionSpec as P
from jax.experimental import pallas as pl
from jax.experimental.pallas import tpu as pltpu

HEAD_DIM = 64
STATE = 128
PACK = 1024
LAYERS = 2
INNER = 3072
EPSILON = 1e-05
CHUNK = 128
LANES = 128
GROUP = 16
TAIL = 8
FAR = -10000.0
PRECISE = lax.Precision.HIGHEST
BF16 = jnp.bfloat16
F32 = jnp.float32
VMEM_BYTES = 48 * 1024 * 1024


def mm(lhs, rhs, precision=None):
    return lax.dot_general(
        lhs, rhs, (((1,), (0,)), ((), ())), precision=precision, preferred_element_type=F32
    )


def mm_t(lhs, rhs):
    return lax.dot_general(lhs, rhs, (((1,), (1,)), ((), ())), preferred_element_type=F32)


def t_mm(lhs, rhs):
    return lax.dot_general(lhs, rhs, (((0,), (0,)), ((), ())), preferred_element_type=F32)


def iota(shape, dim):
    return lax.broadcasted_iota(jnp.int32, shape, dim)


def expand(values, spread):
    lane = iota(values.shape, 1)
    high = values.astype(BF16).astype(F32)
    parts = jnp.where(lane < GROUP, high, jnp.where(lane < 2 * GROUP, values - high, 0.0))
    return mm(parts.astype(BF16), spread)


def conv_pre(joined_ref, at, taps, bias_row, aux):
    summed = bias_row + taps[0:1] * joined_ref[TAIL:, at]
    for offset in range(1, 4):
        moved = joined_ref[TAIL - offset : TAIL - offset + CHUNK, at]
        summed = summed + taps[offset : offset + 1] * (moved * aux[:, offset : offset + 1])
    return summed


def halves_rows(tile, low_lanes):
    zero = jnp.zeros_like(tile)
    return jnp.concatenate(
        [jnp.where(low_lanes, tile, zero), jnp.where(low_lanes, zero, tile)], 0
    )


def parts_of(values, count):
    parts = []
    for _ in range(count):
        low = values.astype(BF16)
        parts.append(low)
        values = values - low.astype(F32)
    return jnp.concatenate(parts, 0)


def order_masks():
    row = iota((CHUNK, CHUNK), 0)
    col = iota((CHUNK, CHUNK), 1)
    return row, col


def step_values(dt_ref, head_ref):
    raw = dt_ref + head_ref[0:1]
    dt = jnp.maximum(raw, 0.0) + jnp.log1p(jnp.exp(-jnp.abs(raw)))
    row, col = order_masks()
    lower = (row >= col).astype(BF16)
    log_decay = mm(jnp.concatenate([lower] * 3, 1), parts_of(dt * head_ref[1:2], 3))
    return raw, dt, log_decay, row, col


def scan_fwd_kernel(
    me_ref,
    x_ref,
    bcdt_ref,
    gate_ref,
    aux_ref,
    seg_ref,
    taps_ref,
    bias_ref,
    bc_taps_ref,
    bc_bias_ref,
    head_ref,
    skip_ref,
    gain_ref,
    spread_ref,
    u_ref,
    y_ref,
    sq_ref,
    kept_ref,
    state,
    tail_x,
    tail_bc,
    ending_ref,
):
    width = x_ref.shape[1]

    @pl.when(pl.program_id(0) == 0)
    def _():
        state[...] = jnp.zeros_like(state)
        tail_x[...] = jnp.zeros_like(tail_x)
        tail_bc[...] = jnp.zeros_like(tail_bc)

    aux = aux_ref[...]
    bc_now = bcdt_ref[:, : 2 * STATE]
    tail_bc[:TAIL] = tail_bc[CHUNK:]
    tail_bc[TAIL:] = bc_now
    bc_pre = conv_pre(tail_bc, slice(None), bc_taps_ref[...], bc_bias_ref[...], aux)
    bc = bc_pre * jax.nn.sigmoid(bc_pre)
    b_low = bc[:, :STATE].astype(BF16)
    c_low = bc[:, STATE:].astype(BF16)
    b_turned = bc[:, :STATE].T.astype(BF16)
    _, dt, log_decay, row, col = step_values(bcdt_ref[:, 2 * STATE :], head_ref)
    log_turned = log_decay.T
    meet = mm_t(c_low, b_low)
    visible = (aux[:, 0:1] == seg_ref[0]) & (row >= col)
    spread = spread_ref[...]
    dt_wide = expand(dt, spread)
    reach = expand(jnp.exp(log_decay) * aux[:, 4:5], spread)
    to_end = expand(jnp.exp(log_decay[CHUNK - 1 :] - log_decay) * aux[:, 5:6], spread)
    state_low = state[...].astype(BF16)
    kept_ref[0] = state_low
    carried = mm(c_low, state_low)
    low_lanes = iota((CHUNK, LANES), 1) < HEAD_DIM
    squares = jnp.zeros((CHUNK, LANES), F32)
    for pair in range(width // LANES):
        at = slice(pair * LANES, (pair + 1) * LANES)
        tail_x[:TAIL, at] = tail_x[CHUNK:, at]
        tail_x[TAIL:, at] = x_ref[:, at]
        pre = conv_pre(tail_x, at, taps_ref[:, at], bias_ref[:, at], aux)
        x_conv = pre * jax.nn.sigmoid(pre)
        inputs = x_conv * dt_wide[:, at]
        mats = []
        for head in (2 * pair, 2 * pair + 1):
            gap = log_decay[:, head : head + 1] - log_turned[head : head + 1, :]
            mats.append((jnp.exp(jnp.where(visible, gap, FAR)) * meet).astype(BF16))
        local = mm(jnp.concatenate(mats, 1), halves_rows(inputs.astype(BF16), low_lanes))
        y = local + carried[:, at] * reach[:, at] + skip_ref[:, at] * x_conv
        y_ref[:, at] = y.astype(y_ref.dtype)
        ending_ref[:, at] = (inputs * to_end[:, at]).astype(BF16)
        gate = gate_ref[:, at].astype(F32)
        gated = y * (gate * jax.nn.sigmoid(gate))
        grown = gated * gain_ref[:, at]
        u_ref[:, at] = grown.astype(BF16)
        squares = squares + gated * gated
    state[...] = state[...] * reach[CHUNK - 1 :] + mm(b_turned, ending_ref[...])
    ones = jnp.ones((8, LANES), F32)
    sums = lax.dot_general(
        ones, squares, (((1,), (1,)), ((), ())), precision=PRECISE, preferred_element_type=F32
    )
    sq_ref[...] = sums


def whole(shape):
    return pl.BlockSpec(shape, lambda *_: (0,) * len(shape))


def place_of(chunk, chunks, me_ref):
    part = chunks // 4
    away = chunk // part ^ me_ref[0]
    return (2 * (away % 2) + away // 2) * part + chunk % part


def scan_fwd(me, x_pre, bcdt_pre, gate_pre, side, weights):
    length, width = x_pre.shape
    chunks = length // CHUNK
    aux, seg_rows = side
    at = lambda c, m: (place_of(c, chunks, m), 0)
    tile = lambda columns: pl.BlockSpec((CHUNK, columns), at)
    in_specs = [
        tile(width),
        tile(bcdt_pre.shape[1]),
        tile(width),
        pl.BlockSpec((CHUNK, LANES), lambda c, m: (c, 0)),
        pl.BlockSpec((1, 1, CHUNK), lambda c, m: (c, 0, 0)),
    ] + [whole(w.shape) for w in weights]
    return pl.pallas_call(
        scan_fwd_kernel,
        grid_spec=pltpu.PrefetchScalarGridSpec(
            num_scalar_prefetch=1,
            grid=(chunks,),
            in_specs=in_specs,
            out_specs=[
                tile(width),
                tile(width),
                pl.BlockSpec((8, CHUNK), lambda c, m: (0, c)),
                pl.BlockSpec((1, STATE, width), lambda c, m: (c, 0, 0)),
            ],
            scratch_shapes=[
                pltpu.VMEM((STATE, width), F32),
                pltpu.VMEM((TAIL + CHUNK, width), F32),
                pltpu.VMEM((TAIL + CHUNK, 2 * STATE), F32),
                pltpu.VMEM((CHUNK, width), BF16),
            ],
        ),
        out_shape=[
            jax.ShapeDtypeStruct((length, width), BF16),
            jax.ShapeDtypeStruct((length, width), BF16),
            jax.ShapeDtypeStruct((8, length), F32),
            jax.ShapeDtypeStruct((chunks, STATE, width), BF16),
        ],
        compiler_params=pltpu.CompilerParams(vmem_limit_bytes=VMEM_BYTES),
        cost_estimate=pl.CostEstimate(
            flops=140 * length * width * LANES,
            bytes_accessed=20 * length * width,
            transcendentals=0,
        ),
        name="scan_fwd",
    )(me, x_pre, bcdt_pre, gate_pre, aux, seg_rows, *weights)


def gate_bwd_kernel(
    me_ref, gs_ref, y_ref, gate_ref, col_ref, gain_ref, g_gate_ref, g_y_ref, d_gain_ref
):
    @pl.when(pl.program_id(0) == 0)
    def _():
        d_gain_ref[...] = jnp.zeros_like(d_gain_ref)

    inv = col_ref[:, 0:1]
    pull = col_ref[:, 1:2]
    for pair in range(gs_ref.shape[1] // LANES):
        at = slice(pair * LANES, (pair + 1) * LANES)
        gs = gs_ref[:, at].astype(F32)
        y = y_ref[:, at].astype(F32)
        gate = gate_ref[:, at].astype(F32)
        sig = jax.nn.sigmoid(gate)
        act = gate * sig
        gated = y * act
        grown = gs * inv
        d_gain_ref[:, at] += jnp.sum(grown * gated, 0, keepdims=True)
        g_gated = grown * gain_ref[:, at] - gated * pull
        g_y_ref[:, at] = (g_gated * act).astype(BF16)
        g_gate_ref[:, at] = (g_gated * y * sig * (1.0 + gate * (1.0 - sig))).astype(BF16)


def gate_bwd(me, gs, y, gate_pre, columns, gain):
    length, width = gs.shape
    rows = length // 4
    tile = pl.BlockSpec((rows, width), lambda p, m: (p, 0))
    return pl.pallas_call(
        gate_bwd_kernel,
        grid_spec=pltpu.PrefetchScalarGridSpec(
            num_scalar_prefetch=1,
            grid=(4,),
            in_specs=[
                tile,
                tile,
                tile,
                pl.BlockSpec((rows, columns.shape[1]), lambda p, m: (2 * (p % 2) + p // 2 ^ m[0], 0)),
                whole(gain.shape),
            ],
            out_specs=[tile, tile, whole((1, width))],
        ),
        out_shape=[jax.ShapeDtypeStruct((length, width), BF16)] * 2
        + [jax.ShapeDtypeStruct((1, width), F32)],
        compiler_params=pltpu.CompilerParams(vmem_limit_bytes=VMEM_BYTES),
        cost_estimate=pl.CostEstimate(
            flops=50 * length * width * LANES,
            bytes_accessed=18 * length * width,
            transcendentals=0,
        ),
        name="gate_bwd",
    )(me, gs, y, gate_pre, columns, gain)


def conv_bwd(joined_ref, later_ref, grad, taps, aux, acc_ref, at):
    acc_ref[4:5, at] += jnp.sum(grad, 0, keepdims=True)
    acc_ref[0:1, at] += jnp.sum(grad * joined_ref[TAIL:, at], 0, keepdims=True)
    result = taps[0:1] * grad
    for offset in range(1, 4):
        moved = joined_ref[TAIL - offset : TAIL - offset + CHUNK, at]
        moved = moved * aux[:, offset : offset + 1]
        acc_ref[offset : offset + 1, at] += jnp.sum(grad * moved, 0, keepdims=True)
        later = later_ref[offset : offset + CHUNK, at] * aux[:, 5 + offset : 6 + offset]
        result = result + taps[offset : offset + 1] * later
    return result


def scan_bwd_kernel(
    me_ref,
    g_ref,
    x_ref,
    x_tail_ref,
    bcdt_ref,
    bc_tail_ref,
    kept_ref,
    aux_ref,
    seg_ref,
    taps_ref,
    bias_ref,
    bc_taps_ref,
    bc_bias_ref,
    head_ref,
    skip_ref,
    gain_ref,
    spread_ref,
    gx_ref,
    gbc_ref,
    gdt_ref,
    accx_ref,
    accbc_ref,
    grad_state,
    next_x,
    next_bc,
    joined_x,
    joined_bc,
    conv_ref,
    slope_ref,
    inputs_ref,
    coming_ref,
    ending_ref,
    sums_ref,
):
    width = x_ref.shape[1]

    @pl.when(pl.program_id(0) == 0)
    def _():
        grad_state[...] = jnp.zeros_like(grad_state)
        next_x[...] = jnp.zeros_like(next_x)
        next_bc[...] = jnp.zeros_like(next_bc)
        accx_ref[...] = jnp.zeros_like(accx_ref)
        accbc_ref[...] = jnp.zeros_like(accbc_ref)

    aux = aux_ref[...]
    joined_bc[:TAIL] = bc_tail_ref[:, : 2 * STATE]
    joined_bc[TAIL:] = bcdt_ref[:, : 2 * STATE]
    bc_pre = conv_pre(joined_bc, slice(None), bc_taps_ref[...], bc_bias_ref[...], aux)
    bc_sig = jax.nn.sigmoid(bc_pre)
    bc = bc_pre * bc_sig
    b_low = bc[:, :STATE].astype(BF16)
    c_low = bc[:, STATE:].astype(BF16)
    c_turned = bc[:, STATE:].T.astype(BF16)
    raw, dt, log_decay, row, col = step_values(bcdt_ref[:, 2 * STATE :], head_ref)
    log_turned = log_decay.T
    meet = mm_t(b_low, c_low)
    visible = (aux[:, 0:1] == seg_ref[0]) & (row <= col)
    spread = spread_ref[...]
    dt_wide = expand(dt, spread)
    reach = expand(jnp.exp(log_decay) * aux[:, 4:5], spread)
    to_end = expand(jnp.exp(log_decay[CHUNK - 1 :] - log_decay) * aux[:, 5:6], spread)
    low_lanes = iota((CHUNK, LANES), 1) < HEAD_DIM
    lane = iota((CHUNK, LANES), 1)
    for pair in range(width // LANES):
        at = slice(pair * LANES, (pair + 1) * LANES)
        joined_x[:TAIL, at] = x_tail_ref[:, at]
        joined_x[TAIL:, at] = x_ref[:, at]
        pre = conv_pre(joined_x, at, taps_ref[:, at], bias_ref[:, at], aux)
        sig = jax.nn.sigmoid(pre)
        x_conv = pre * sig
        inputs = x_conv * dt_wide[:, at]
        conv_ref[:, at] = x_conv
        slope_ref[:, at] = sig * (1.0 + pre * (1.0 - sig))
        inputs_ref[:, at] = inputs.astype(BF16)
        ending_ref[:, at] = (inputs * to_end[:, at]).astype(BF16)
        coming_ref[:, at] = (g_ref[:, at].astype(F32) * reach[:, at]).astype(BF16)
    state_low = kept_ref[0]
    grad_state_low = grad_state[...].astype(BF16)
    coming_low = coming_ref[...]
    ending_low = ending_ref[...]
    carried = mm(c_low, state_low)
    leaving = mm(b_low, grad_state_low)
    grad_c = mm_t(coming_low, state_low)
    grad_b = mm_t(ending_low, grad_state_low)
    last = reach[CHUNK - 1 :]
    passed = jnp.sum(grad_state[...] * state_low.astype(F32), 0, keepdims=True) * last
    through = mm_t(jnp.broadcast_to(passed, (8, width)).astype(BF16), spread)
    grad_state[...] = grad_state[...] * last + mm(c_turned, coming_low)
    grad_meet = jnp.zeros((CHUNK, CHUNK), F32)
    col_sums = jnp.zeros((CHUNK, LANES), F32)
    row_sums = jnp.zeros((LANES, CHUNK), F32)
    head_row = iota((LANES, CHUNK), 0)
    for pair in range(width // LANES):
        at = slice(pair * LANES, (pair + 1) * LANES)
        g_low = g_ref[:, at]
        grad_mats = mm_t(halves_rows(inputs_ref[:, at], low_lanes), g_low)
        mats = []
        for member in range(2):
            head = 2 * pair + member
            gap = log_turned[head : head + 1, :] - log_decay[:, head : head + 1]
            weight = jnp.exp(jnp.where(visible, gap, FAR))
            mats.append((weight * meet).astype(BF16))
            part = weight * grad_mats[member * CHUNK : (member + 1) * CHUNK]
            grad_meet = grad_meet + part
            product = part * meet
            col_sums = jnp.where(lane == head, jnp.sum(product, 1, keepdims=True), col_sums)
            row_sums = jnp.where(head_row == head, jnp.sum(product, 0, keepdims=True), row_sums)
        local = mm(jnp.concatenate(mats, 1), halves_rows(g_low, low_lanes))
        g = g_low.astype(F32)
        x_conv = conv_ref[:, at]
        leaving_now = leaving[:, at]
        grad_inputs = local + leaving_now * to_end[:, at]
        sums_ref[:CHUNK, at] = (coming_ref[:, at].astype(F32) * carried[:, at]).astype(BF16)
        sums_ref[CHUNK : 2 * CHUNK, at] = (
            ending_ref[:, at].astype(F32) * leaving_now
        ).astype(BF16)
        sums_ref[2 * CHUNK :, at] = (grad_inputs * x_conv).astype(BF16)
        accx_ref[5:6, at] += jnp.sum(g * x_conv, 0, keepdims=True)
        grad_conv = (grad_inputs * dt_wide[:, at] + g * skip_ref[:, at]) * slope_ref[:, at]
        next_x[CHUNK:, at] = next_x[:TAIL, at]
        next_x[:CHUNK, at] = grad_conv
        gx_ref[:, at] = conv_bwd(
            joined_x, next_x, grad_conv, taps_ref[:, at], aux, accx_ref, at
        ).astype(BF16)
    head_sums = mm_t(sums_ref[...], spread)
    upper = (row <= col).astype(BF16)
    strict = (row > col).astype(BF16)
    straddle = mm(
        jnp.concatenate([upper] * 3 + [strict] * 2, 1),
        jnp.concatenate(
            [
                parts_of(row_sums.T - col_sums + head_sums[:CHUNK], 3),
                parts_of(head_sums[CHUNK : 2 * CHUNK], 2),
            ],
            0,
        ),
    )
    straddle = straddle + through[0:1]
    grad_dt = head_sums[2 * CHUNK :] + head_ref[1:2] * straddle
    grad_raw = jnp.where(lane < GROUP, grad_dt * jax.nn.sigmoid(raw), 0.0)
    gdt_ref[...] = grad_raw.astype(BF16)
    accx_ref[6:7, :LANES] += jnp.sum(grad_raw, 0, keepdims=True)
    accx_ref[7:8, :LANES] += jnp.sum(dt * straddle, 0, keepdims=True)
    grad_meet_low = grad_meet.astype(BF16)
    grad_b = grad_b + mm(grad_meet_low, c_low)
    grad_c = grad_c + t_mm(grad_meet_low, b_low)
    grad_bc = jnp.concatenate([grad_b, grad_c], 1) * (bc_sig * (1.0 + bc_pre * (1.0 - bc_sig)))
    next_bc[CHUNK:] = next_bc[:TAIL]
    next_bc[:CHUNK] = grad_bc
    gbc_ref[...] = conv_bwd(
        joined_bc, next_bc, grad_bc, bc_taps_ref[...], aux, accbc_ref, slice(None)
    ).astype(BF16)


def scan_bwd(me, g_y, x_pre, bcdt_pre, kept, side, weights):
    length, width = x_pre.shape
    chunks = length // CHUNK
    aux, seg_rows = side
    back = lambda c: chunks - 1 - c
    place = lambda c, m: place_of(back(c), chunks, m)
    tile = lambda columns: pl.BlockSpec((CHUNK, columns), lambda c, m: (place(c, m), 0))

    def tail_at(c, m):
        before = place_of(jnp.maximum(back(c) - 1, 0), chunks, m)
        return (before * (CHUNK // TAIL) + CHUNK // TAIL - 1, 0)

    tail = lambda columns: pl.BlockSpec((TAIL, columns), tail_at)
    wide = bcdt_pre.shape[1]
    in_specs = [
        tile(width),
        tile(width),
        tail(width),
        tile(wide),
        tail(wide),
        pl.BlockSpec((1, STATE, width), lambda c, m: (back(c), 0, 0)),
        pl.BlockSpec((CHUNK, LANES), lambda c, m: (back(c), 0)),
        pl.BlockSpec((1, 1, CHUNK), lambda c, m: (back(c), 0, 0)),
    ] + [whole(w.shape) for w in weights]
    return pl.pallas_call(
        scan_bwd_kernel,
        grid_spec=pltpu.PrefetchScalarGridSpec(
            num_scalar_prefetch=1,
            grid=(chunks,),
            in_specs=in_specs,
            out_specs=[
                tile(width),
                tile(2 * STATE),
                tile(LANES),
                whole((8, width)),
                whole((8, 2 * STATE)),
            ],
            scratch_shapes=[
                pltpu.VMEM((STATE, width), F32),
                pltpu.VMEM((TAIL + CHUNK, width), F32),
                pltpu.VMEM((TAIL + CHUNK, 2 * STATE), F32),
                pltpu.VMEM((TAIL + CHUNK, width), F32),
                pltpu.VMEM((TAIL + CHUNK, 2 * STATE), F32),
                pltpu.VMEM((CHUNK, width), F32),
                pltpu.VMEM((CHUNK, width), F32),
                pltpu.VMEM((CHUNK, width), BF16),
                pltpu.VMEM((CHUNK, width), BF16),
                pltpu.VMEM((CHUNK, width), BF16),
                pltpu.VMEM((3 * CHUNK, width), BF16),
            ],
        ),
        out_shape=[
            jax.ShapeDtypeStruct((length, width), BF16),
            jax.ShapeDtypeStruct((length, 2 * STATE), BF16),
            jax.ShapeDtypeStruct((length, LANES), BF16),
            jax.ShapeDtypeStruct((8, width), F32),
            jax.ShapeDtypeStruct((8, 2 * STATE), F32),
        ],
        compiler_params=pltpu.CompilerParams(vmem_limit_bytes=VMEM_BYTES),
        cost_estimate=pl.CostEstimate(
            flops=280 * length * width * LANES,
            bytes_accessed=20 * length * width,
            transcendentals=0,
        ),
        name="scan_bwd",
    )(me, g_y, x_pre, x_pre, bcdt_pre, bcdt_pre, kept, aux, seg_rows, *weights)


def side_arrays(segments):
    length = segments.shape[0]
    seg = segments.astype(F32)
    columns = [seg]
    nothing = lambda count: jnp.full((count,), -1.0, F32)
    for offset in range(1, 4):
        moved = jnp.concatenate([nothing(offset), seg[: length - offset]], 0)
        columns.append((moved == seg).astype(F32))
    blocks = seg.reshape(-1, CHUNK)
    ends = blocks[:, -1]
    before = jnp.concatenate([nothing(1), ends[:-1]], 0)
    columns.append((blocks == before[:, None]).astype(F32).reshape(-1))
    columns.append((blocks == ends[:, None]).astype(F32).reshape(-1))
    for offset in range(1, 4):
        moved = jnp.concatenate([seg[offset:], nothing(offset)], 0)
        columns.append((moved == seg).astype(F32))
    stacked = jnp.stack(columns, 1)
    aux = jnp.pad(stacked, ((0, 0), (0, LANES - stacked.shape[1])))
    return aux, blocks.reshape(-1, 1, CHUNK)


def in_groups(values):
    padded = jnp.pad(values, [(0, 0)] * (values.ndim - 1) + [(0, GROUP - values.shape[-1])])
    return jnp.tile(padded, (1,) * (values.ndim - 1) + (LANES // GROUP,))


def spread_matrix(width):
    head = lax.broadcasted_iota(jnp.int32, (LANES, width), 0) % GROUP
    owner = lax.broadcasted_iota(jnp.int32, (LANES, width), 1) // HEAD_DIM
    return (head == owner).astype(BF16)


def scan_weights(taps, bias, bc_taps, bc_bias, dt_bias, a_log, d_skip, gain, spread):
    rates = -jnp.exp(a_log)
    rows = jnp.stack([in_groups(dt_bias), in_groups(rates)])
    head = jnp.pad(rows, ((0, 6), (0, 0)))
    return (
        taps,
        bias[None],
        bc_taps,
        bc_bias[None],
        head,
        jnp.repeat(d_skip, HEAD_DIM)[None],
        gain[None],
        spread,
    )


def partners(count, step):
    return [(index, index ^ step) for index in range(count)]


def swap(values, axis, step):
    return lax.ppermute(values, axis, partners(lax.axis_size(axis), step))


def after(values, *earlier):
    return lax.optimization_barrier((values, *earlier))[0]


def dp_masks():
    masks = []
    step = lax.axis_size("dp") // 2
    while step > 0:
        masks.append(step)
        step = step // 2
    return masks


def offsets(masks):
    found = [0]
    for mask in masks:
        found = found + [offset ^ mask for offset in found]
    return found


class Rows:
    def __init__(self, own):
        self.rows = own

    def stage(self, mask, *earlier):
        got = swap(after(self.rows, *earlier), "dp", mask)
        self.rows = jnp.concatenate([self.rows, got], 0)
        return got

    def begin(self, masks, *earlier):
        for mask in masks[:-2]:
            got = self.stage(mask, *earlier)
            earlier = ()
        return got


def scatter_first(kept, got):
    total = kept + got.astype(F32)
    height = total.shape[0] // 2
    return total[:height], total[height:].astype(BF16)


def scatter_rest(kept, sent, masks):
    for mask in reversed(masks[1:-1]):
        kept, sent = scatter_first(kept, swap(sent, "dp", mask))
    return kept + swap(sent, "dp", masks[0]).astype(F32)


def grad_half(rows, grads, which):
    width = rows.shape[1] // 2
    dims = (((0,), (0,)), ((), ()))
    taken = rows[:, which * width : (which + 1) * width]
    return lax.dot_general(taken, grads, dims, preferred_element_type=F32)


def sent_half(rows, grads):
    return grad_half(rows, grads, 1).astype(BF16)


def reordered(values, me):
    size = values.shape[0] // 4
    return jnp.concatenate(
        [lax.dynamic_slice_in_dim(values, (away ^ me) * size, size, 0) for away in (0, 2, 1, 3)], 0
    )


def restored(values, me):
    size = values.shape[0] // 4
    parts = []
    for part in range(4):
        away = part ^ me
        parts.append(
            lax.dynamic_slice_in_dim(values, (2 * (away % 2) + away // 2) * size, size, 0)
        )
    return jnp.concatenate(parts, 0)


def turned_over(values, size):
    shaped = values.reshape(-1, 2, size, values.shape[1])
    return shaped[:, ::-1].reshape(values.shape)


def own_quarter(values, me):
    size = values.shape[0] // 4
    return lax.dynamic_slice_in_dim(values, me * size, size, 0)


def tensor_sum(values):
    values = values + swap(values, "tensor", 1)
    return values + swap(values, "tensor", 2)


def dp_sum(values):
    step = 1
    while step < lax.axis_size("dp"):
        values = values + swap(values, "dp", step)
        step = 2 * step
    return values


def dot(lhs, rhs):
    return lax.dot_general(lhs, rhs, (((1,), (0,)), ((), ())), preferred_element_type=F32)


def dot_t(lhs, rhs):
    return lax.dot_general(lhs, rhs, (((1,), (1,)), ((), ())), preferred_element_type=F32)


def own_order(features, masks, earlier):
    place = after(lax.axis_index("dp"), earlier)
    found = offsets(masks)
    height = features // len(found)
    index = lax.broadcasted_iota(jnp.int32, (1, features), 1)
    part, within = index // height, index % height
    away = jnp.zeros_like(part)
    for position, offset in enumerate(found):
        away = jnp.where(part == position, offset, away)
    source = (away ^ place) * height + within
    return (lax.broadcasted_iota(jnp.int32, (features, features), 0) == source).astype(BF16)


def rms_of(stream):
    return lax.rsqrt(jnp.mean(stream * stream, -1, keepdims=True) + EPSILON)


def on_device(
    hidden,
    segments,
    norm_gain,
    w_z,
    w_x,
    w_bc,
    w_dt,
    conv_x_w,
    conv_x_b,
    conv_bc_w,
    conv_bc_b,
    dt_bias,
    a_log,
    d_skip,
    gated_gain,
    w_out,
    cotangent,
):
    length, features = hidden.shape
    width = w_x.shape[2]
    heads = dt_bias.shape[1]
    masks = dp_masks()
    place = lax.axis_index("tensor")
    core, far = place % 2, place // 2
    me = place
    me_row = me.astype(jnp.int32)[None]
    half = length // 2
    quarter = length // 4

    side_first = masks[-1:] + masks[:-1]
    seated = [offsets(side_first).index(offset) for offset in offsets(masks)]
    height = w_x.shape[1]
    quart_bc = w_bc.shape[2] // 4
    own_bc = lax.dynamic_slice_in_dim(w_bc, place * quart_bc, quart_bc, 2)
    w_small = jnp.concatenate([own_bc[0], own_bc[1], w_dt[0], w_dt[1]], 1)
    w_small = jnp.pad(w_small, ((0, 0), (0, 2 * LANES - w_small.shape[1])))

    x0, z0, out0 = Rows(w_x[0]), Rows(w_z[0]), Rows(w_out[0])
    x1, z1, out1 = Rows(w_x[1]), Rows(w_z[1]), Rows(w_out[1])
    small = Rows(w_small)
    near_mask, side_mask = masks[-2:]
    x0_far = x0.begin(masks)
    small_far = small.begin(masks)
    out1_side = out1.stage(side_mask)
    x0_near = x0.stage(near_mask, small_far)
    small_near = small.stage(near_mask, x0_far)
    z0_far = z0.begin(masks, x0_far, small_far)
    small.stage(side_mask)
    x0.stage(side_mask)
    out0_far = out0.begin(masks, x0_near, small_near, z0_far)
    z0_near = z0.stage(near_mask, x0_near, small_near)
    x1_far = x1.begin(masks, z0_near, out0_far)
    out0_near = out0.stage(near_mask, z0_near)
    z0.stage(side_mask)
    z1_far = z1.begin(masks, out0_near, x1_far)
    x1_near = x1.stage(near_mask, out0_near)
    out0.stage(side_mask)
    out1_far = out1.begin(masks, x1_near, z1_far)
    z1_near = z1.stage(near_mask, x1_near)
    x1_side = x1.stage(side_mask)
    out1_near = out1.stage(near_mask, z1_near)
    z1_side = z1.stage(side_mask)
    out1_rows = [out1.rows[seat * height : (seat + 1) * height] for seat in seated]
    x_rows, z_rows = [x0.rows, x1.rows], [z0.rows, z1.rows]
    out_rows = [out0.rows, jnp.concatenate(out1_rows, 0)]
    small_rows = small.rows

    own_cols = small_rows[:, :LANES]
    across = swap(own_cols, "tensor", 2)
    beside = swap(jnp.concatenate([own_cols, across], 1), "tensor", 1)

    def small_columns(layer):
        low = layer * quart_bc
        parts = [
            own_cols[:, low : low + quart_bc],
            across[:, low : low + quart_bc],
            beside[:, low : low + quart_bc],
            beside[:, LANES + low : LANES + low + quart_bc],
        ]
        first = core == 0
        near = [jnp.where(first, parts[0], parts[2]), jnp.where(first, parts[2], parts[0])]
        away = [jnp.where(first, parts[1], parts[3]), jnp.where(first, parts[3], parts[1])]
        first = far == 0
        ordered = [jnp.where(first, n, a) for n, a in zip(near, away)]
        ordered += [jnp.where(first, a, n) for n, a in zip(near, away)]
        at = LANES + layer * heads
        return jnp.concatenate(ordered + [in_groups(small_rows[:, at : at + heads])], 1)

    bcdt_rows = [small_columns(layer) for layer in range(LAYERS)]

    order = lax.optimization_barrier(own_order(features, masks, x0_far))
    side = side_arrays(after(segments, x0_far))
    spread = spread_matrix(width)
    weights = [
        scan_weights(
            conv_x_w[layer],
            conv_x_b[layer],
            conv_bc_w[layer],
            conv_bc_b[layer],
            dt_bias[layer],
            a_log[layer],
            d_skip[layer],
            gated_gain[layer],
            spread,
        )
        for layer in range(LAYERS)
    ]
    order, side, weights = lax.optimization_barrier((order, side, weights))
    hidden_rows = reordered(after(hidden, x0_far), me)
    hidden_low = dot(after(hidden_rows, x0_near, small_near, out1_side), order).astype(BF16)
    cotangent_rows = reordered(after(cotangent, x0_far), me)
    cotangent_low = dot(after(cotangent_rows, hidden_low, z0_near), order).astype(BF16)
    gains = mm(after(norm_gain, small_near), order.astype(F32), PRECISE)
    hidden_low, cotangent_low, gains = lax.optimization_barrier(
        (hidden_low, cotangent_low, gains)
    )

    def columns_of(values, which):
        return lax.dynamic_slice_in_dim(values, which * STATE, STATE, 1)

    stream = hidden_low.astype(F32)
    normed0 = (stream * rms_of(stream) * gains[0]).astype(BF16)
    stream0 = hidden_low[:quarter].astype(F32)
    x_pre0 = dot(normed0, x_rows[0])
    bcdt_pre0 = dot(after(normed0, x_pre0, z0_near, out0_far), bcdt_rows[0])
    gate_pre0 = dot(after(normed0, bcdt_pre0, out0_near, x1_far), z_rows[0]).astype(BF16)
    u0, y0, sq, kept0 = scan_fwd(me_row, x_pre0, bcdt_pre0, gate_pre0, side, weights[0])
    u_now = after(u0, x1_near, z1_far)
    sent = dot_t(u_now[half:], out_rows[0]).astype(BF16)
    sq = sq[0:1]
    sq = sq + swap(sq, "tensor", 1)
    u_now = after(u_now, sent, sq)
    mine = dot_t(u_now[:half], out_rows[0]) + swap(sent, "tensor", 1).astype(F32)
    sq = sq + swap(sq, "tensor", 2)
    away = after(mine[quarter:].astype(BF16), sq)
    got = swap(away, "tensor", 2)
    inv0 = lax.rsqrt(sq / INNER + EPSILON)[0]
    got, mine, z1_near, out1_far, x1_side = lax.optimization_barrier(
        (got, mine, z1_near, out1_far, x1_side)
    )
    total0 = mine[:quarter] + got.astype(F32)
    stream1 = stream0 + own_quarter(inv0, me)[:, None] * total0
    normed_own = (stream1 * rms_of(stream1) * gains[1]).astype(BF16)
    normed_half = jnp.concatenate([normed_own, swap(normed_own, "tensor", 2)], 0)
    normed_half, z1_side = lax.optimization_barrier((normed_half, z1_side))
    normed1 = jnp.concatenate([normed_half, swap(normed_half, "tensor", 1)], 0)
    scaled0 = (u0.astype(F32) * reordered(inv0, me)[:, None]).astype(BF16)

    x_pre1 = dot(after(normed1, out1_near), x_rows[1])
    bcdt_pre1 = dot(normed1, bcdt_rows[1])
    gate_pre1 = dot(normed1, z_rows[1]).astype(BF16)
    u1, y1, sq, kept1 = scan_fwd(me_row, x_pre1, bcdt_pre1, gate_pre1, side, weights[1])
    scaled_grad1 = dot(cotangent_low, out_rows[1])
    cross = restored(jnp.sum(scaled_grad1 * u1.astype(F32), -1), me)
    both = tensor_sum(jnp.stack([sq[0], cross]))
    mixed_sent = dot_t(u1[half:], out_rows[1]).astype(BF16)
    mixed_mine = dot_t(u1[:half], out_rows[1])
    mixed_mine = mixed_mine + swap(mixed_sent, "tensor", 1).astype(F32)
    both = after(both, mixed_sent, mixed_mine)
    mixed_got = swap(mixed_mine[quarter:].astype(BF16), "tensor", 2)
    inv1 = lax.rsqrt(both[0] / INNER + EPSILON)

    columns = jnp.stack([inv1, inv1 * inv1 * inv1 * both[1] / INNER], 1)
    g_gate1, g_y, d_gain1 = gate_bwd(
        me_row, scaled_grad1, y1, gate_pre1, columns, gated_gain[1][None]
    )
    z_sent = sent_half(normed1, g_gate1)
    z_got = swap(z_sent, "dp", 1)
    g_y = after(g_y, z_sent)
    g_x1, g_bc1, g_dt1, acc_x1, acc_bc1 = scan_bwd(
        me_row, g_y, x_pre1, bcdt_pre1, kept1, side, weights[1]
    )
    g_x1, z_got, mixed_got = lax.optimization_barrier((g_x1, z_got, mixed_got))

    def grad_rows(rows, g_gate, g_x, g_bcdt, layer):
        return (
            dot_t(g_gate[rows], z_rows[layer])
            + dot_t(g_x[rows], x_rows[layer])
            + dot_t(g_bcdt[rows], bcdt_rows[layer])
        )

    g_bcdt = jnp.concatenate([g_bc1, g_dt1], 1)
    sent = grad_rows(slice(half, length), g_gate1, g_x1, g_bcdt, 1).astype(BF16)
    cotangent_now = after(cotangent_low, sent)
    scaled1 = (u1.astype(F32) * reordered(inv1, me)[:, None]).astype(BF16)
    out_sent = sent_half(cotangent_now, scaled1)
    out_got = swap(out_sent, "dp", 1)
    own = grad_rows(slice(0, half), after(g_gate1, out_sent), g_x1, g_bcdt, 1)
    mine = own + swap(sent, "tensor", 1).astype(F32)
    away = mine[quarter:].astype(BF16)
    got = swap(away, "tensor", 2)
    normed_now = after(normed1, away)
    z_kept, z_next = scatter_first(grad_half(normed_now, g_gate1, 0), z_got)
    z_near = swap(z_next, "dp", near_mask)
    normed_now = after(normed_now, z_next)
    x_sent = sent_half(normed_now, g_x1)
    x_kept_half = grad_half(normed_now, g_x1, 0)
    out_kept_half = grad_half(after(cotangent_now, away), scaled1, 0)
    mixed_total = mixed_mine[:quarter] + mixed_got.astype(F32)
    last = stream1 + own_quarter(inv1, me)[:, None] * mixed_total
    mixed_own = dot_t(last.astype(BF16), order).astype(BF16)
    got, mine, out_got, z_near, x_sent, out_kept_half, x_kept_half, mixed_own = (
        lax.optimization_barrier(
            (got, mine, out_got, z_near, x_sent, out_kept_half, x_kept_half, mixed_own)
        )
    )
    x_got = swap(x_sent, "dp", 1)
    total = mine[:quarter] + got.astype(F32)
    rms = rms_of(stream1)
    normal = stream1 * rms
    grown = total * gains[1]
    grad_stream = cotangent_low[:quarter].astype(F32) + rms * (
        grown - normal * jnp.mean(grown * normal, -1, keepdims=True)
    )
    grad_own = grad_stream.astype(BF16)
    out_kept, out_next = scatter_first(out_kept_half, out_got)
    out_near = swap(out_next, "dp", near_mask)
    z_kept, z_next = scatter_first(z_kept, z_near)
    z_far = swap(z_next, "dp", masks[-3])
    total_now = after(total, grad_own)
    d_norm1 = jnp.sum(total_now * normal, 0)
    cross = jnp.sum(grad_own.astype(F32) * total0, -1)
    grad_half_rows = jnp.concatenate([grad_own, swap(grad_own, "tensor", 2)], 0)
    cross = jnp.concatenate([cross, swap(cross, "tensor", 2)], 0)
    grad_half_rows, cross, z_far, out_near = lax.optimization_barrier(
        (grad_half_rows, cross, z_far, out_near)
    )
    grad0 = jnp.concatenate([grad_half_rows, swap(grad_half_rows, "tensor", 1)], 0)
    cross = restored(jnp.concatenate([cross, swap(cross, "tensor", 1)], 0), me)
    out_kept, out_next = scatter_first(out_kept, out_near)
    out_far = swap(out_next, "dp", masks[-3])

    grad0 = lax.optimization_barrier(grad0)
    out_sent0 = sent_half(grad0, scaled0)
    out_got0 = swap(out_sent0, "dp", 1)
    scaled_grad0 = dot(after(grad0, out_sent0), out_rows[0])
    columns = jnp.stack([inv0, inv0 * inv0 * inv0 * cross / INNER], 1)
    g_gate0, g_y, d_gain0 = gate_bwd(
        me_row, scaled_grad0, y0, gate_pre0, columns, gated_gain[0][None]
    )
    z_sent0 = sent_half(normed0, g_gate0)
    z_got0 = swap(z_sent0, "dp", 1)
    g_y, z_sent0, x_got, out_far = lax.optimization_barrier((g_y, z_sent0, x_got, out_far))
    x_kept, x_next = scatter_first(x_kept_half, x_got)
    x_near = swap(x_next, "dp", near_mask)
    g_y = after(g_y, x_next)
    mixed = lax.all_gather(after(mixed_own, grad0), "tensor", axis=0).reshape(length, features)
    away1 = swap(after(columns_of(g_bc1, 1 - far), grad0), "tensor", 2)
    g_x0, g_bc0, g_dt0, acc_x0, acc_bc0 = scan_bwd(
        me_row, g_y, x_pre0, bcdt_pre0, kept0, side, weights[0]
    )
    away0 = swap(columns_of(g_bc0, 1 - far), "tensor", 2)
    g_x0, away1, x_near, out_got0 = lax.optimization_barrier((g_x0, away1, x_near, out_got0))
    x_sent0 = sent_half(normed0, g_x0)
    x_got0 = swap(x_sent0, "dp", 1)
    g_x0 = after(g_x0, x_sent0)
    g_bcdt = jnp.concatenate([g_bc0, g_dt0], 1)
    sent = grad_rows(slice(half, length), g_gate0, g_x0, g_bcdt, 0).astype(BF16)
    out_kept_half0 = grad_half(after(grad0, sent), scaled0, 0)
    out_kept0, out_next0 = scatter_first(out_kept_half0, out_got0)
    out_near0 = swap(out_next0, "dp", near_mask)
    own = grad_rows(slice(0, half), after(g_gate0, out_next0), g_x0, g_bcdt, 0)
    mine = own + swap(sent, "tensor", 1).astype(F32)
    away = mine[quarter:].astype(BF16)
    got = swap(away, "tensor", 2)
    normed_now, z_got0, x_near, away0, _ = lax.optimization_barrier(
        (normed0, z_got0, x_near, away0, away)
    )
    z_kept0, z_next0 = scatter_first(grad_half(normed_now, g_gate0, 0), z_got0)
    z_near0 = swap(z_next0, "dp", near_mask)
    normed_now = after(normed_now, z_next0)
    x_kept, x_next = scatter_first(x_kept, x_near)
    x_kept_half0 = grad_half(normed_now, g_x0, 0)
    x_kept_half0, out_near0, x_next = lax.optimization_barrier((x_kept_half0, out_near0, x_next))
    x_far = swap(x_next, "dp", masks[-3])
    out_kept0, out_next0 = scatter_first(out_kept0, out_near0)
    out_far0 = swap(out_next0, "dp", masks[-3])
    got, mine, out_next0 = lax.optimization_barrier((got, mine, out_next0))
    total = mine[:quarter] + got.astype(F32)
    rms = rms_of(stream0)
    normal = stream0 * rms
    grown = total * gains[0]
    grad_stream = grad_stream + rms * (
        grown - normal * jnp.mean(grown * normal, -1, keepdims=True)
    )
    d_hidden = dot_t(grad_stream.astype(BF16), order).astype(BF16)
    x_got0, z_near0, _ = lax.optimization_barrier((x_got0, z_near0, d_hidden))
    x_kept0, x_next0 = scatter_first(x_kept_half0, x_got0)
    x_near0 = swap(x_next0, "dp", near_mask)
    x_next0_first = x_next0
    z_kept0, z_next0 = scatter_first(z_kept0, z_near0)
    z_far0 = swap(z_next0, "dp", masks[-3])
    total_now = after(total, d_hidden, z_next0)
    d_norm0 = jnp.sum(total_now * normal, 0)
    d_hidden = jnp.concatenate([d_hidden, swap(d_hidden, "tensor", 2)], 0)
    d_half = d_hidden
    d_hidden = jnp.concatenate([d_hidden, swap(d_hidden, "tensor", 1)], 0)
    out_kept, x_kept, z_kept, out_kept0, z_kept0, _ = lax.optimization_barrier(
        (out_kept, x_kept, z_kept, out_kept0, z_kept0, d_half)
    )
    d_hidden = restored(d_hidden, me).astype(F32)

    def finished(kept, sent):
        for mask in reversed(masks[:-3]):
            kept, sent = scatter_first(kept, sent)
            sent = swap(sent, "dp", mask)
        return kept + sent.astype(F32)

    x_kept0, x_next0 = scatter_first(x_kept0, x_near0)
    d_out1 = finished(out_kept, out_far)
    d_x1 = finished(x_kept, x_far)
    d_z1 = finished(z_kept, z_far)
    d_out0 = finished(out_kept0, out_far0)
    d_z0 = finished(z_kept0, z_far0)
    d_x0 = finished(x_kept0, swap(x_next0, "dp", masks[-3]))

    near_cols = jnp.concatenate([columns_of(v, far) for v in (g_bc0, g_bc1)], 1)
    near_cols = after(near_cols, x_next0_first)
    away_cols = jnp.concatenate([away0, away1], 1)
    bc_sum = near_cols.astype(F32) + turned_over(away_cols, quarter).astype(F32)
    across_sum = swap(bc_sum.astype(BF16), "tensor", 1)
    bc_sum = bc_sum + turned_over(across_sum, half).astype(F32)
    small_sent, small_kept = [], []
    for layer, (rows, g_dt) in enumerate(((normed0, g_dt0), (normed1, g_dt1))):
        summed = bc_sum[:, layer * STATE : (layer + 1) * STATE]
        rolled = jnp.roll(summed, STATE // 2, 1)
        own_cols = jnp.where(core == 0, summed, rolled)[:, : STATE // 2].astype(BF16)
        own_cols = jnp.concatenate([own_cols, g_dt[:, : STATE // 2]], 1)
        small_sent.append(sent_half(rows, own_cols))
        small_kept.append(grad_half(rows, own_cols, 0))
    small_sent = after(jnp.concatenate(small_sent, 1), x_got0)
    small_got = swap(small_sent, "dp", 1)
    small_kept, small_next = scatter_first(jnp.concatenate(small_kept, 1), small_got)
    d_small = scatter_rest(small_kept, small_next, masks)
    d_small = jnp.stack([d_small[:, layer * LANES : (layer + 1) * LANES] for layer in range(LAYERS)])
    found = jnp.array(offsets(masks), jnp.int32)
    norm_part = jnp.stack([d_norm0, d_norm1]).reshape(LAYERS, len(found), 1, height)
    here = (found ^ lax.axis_index("dp"))[:, None] == jnp.arange(len(found))[None]
    norm_part = jnp.sum(jnp.where(here[None, :, :, None], norm_part, 0.0), 1)
    shared = jnp.concatenate(
        [acc_bc0, acc_bc1, jnp.zeros((8, width - 4 * STATE), F32)], 1
    )
    shared = tensor_sum(jnp.concatenate([shared, norm_part.reshape(-1, width)], 0))
    gains_part = jnp.concatenate([d_gain0, d_gain1], 0)
    summed = dp_sum(jnp.concatenate([acc_x0, acc_x1, gains_part, shared], 0))
    acc = summed[:16].reshape(LAYERS, 8, width)
    shared = summed[16 + LAYERS :]
    bc_acc = jnp.stack([shared[:8, : 2 * STATE], shared[:8, 2 * STATE : 4 * STATE]])
    d_norm_gain = shared[8:].reshape(LAYERS, features)
    d_skips = acc[:, 5].reshape(LAYERS, heads, HEAD_DIM).sum(2)
    own_width = STATE // 2
    return (
        mixed,
        d_hidden,
        d_norm_gain,
        jnp.stack([d_z0, d_z1]),
        jnp.stack([d_x0, d_x1]),
        d_small[:, :, :own_width],
        d_small[:, :, own_width : own_width + heads],
        acc[:, :4],
        acc[:, 4],
        bc_acc[:, :4],
        bc_acc[:, 4],
        acc[:, 6, :heads],
        acc[:, 7, :heads] * -jnp.exp(a_log),
        d_skips,
        summed[16 : 16 + LAYERS],
        jnp.stack([d_out0, d_out1]),
    )


def solution(mesh):
    in_specs = (
        P("dp", None),
        P("dp"),
        P(),
        P(None, "dp", "tensor"),
        P(None, "dp", "tensor"),
        P(None, "dp", None),
        P(None, "dp", "tensor"),
        P(None, None, "tensor"),
        P(None, "tensor"),
        P(),
        P(),
        P(None, "tensor"),
        P(None, "tensor"),
        P(None, "tensor"),
        P(None, "tensor"),
        P(None, "dp", "tensor"),
        P("dp", None),
    )
    out_specs = (
        P("dp", None),
        P("dp", None),
        P(),
        P(None, "dp", "tensor"),
        P(None, "dp", "tensor"),
        P(None, "dp", "tensor"),
        P(None, "dp", "tensor"),
        P(None, None, "tensor"),
        P(None, "tensor"),
        P(),
        P(),
        P(None, "tensor"),
        P(None, "tensor"),
        P(None, "tensor"),
        P(None, "tensor"),
        P(None, "dp", "tensor"),
    )
    return jax.shard_map(
        on_device, mesh=mesh, in_specs=in_specs, out_specs=out_specs, check_vma=False
    )
```

```python
import jax
import jax.numpy as jnp
from jax import lax
from jax.sharding import PartitionSpec as P
from jax.experimental import pallas as pl
from jax.experimental.pallas import tpu as pltpu

HEAD_DIM = 64
STATE = 128
PACK = 1024
LAYERS = 2
INNER = 3072
EPSILON = 1e-05
CHUNK = 128
LANES = 128
GROUP = 16
TAIL = 8
FAR = -10000.0
PRECISE = lax.Precision.HIGHEST
BF16 = jnp.bfloat16
F32 = jnp.float32
VMEM_BYTES = 48 * 1024 * 1024


def mm(lhs, rhs, precision=None):
    return lax.dot_general(
        lhs, rhs, (((1,), (0,)), ((), ())), precision=precision, preferred_element_type=F32
    )


def mm_t(lhs, rhs):
    return lax.dot_general(lhs, rhs, (((1,), (1,)), ((), ())), preferred_element_type=F32)


def t_mm(lhs, rhs):
    return lax.dot_general(lhs, rhs, (((0,), (0,)), ((), ())), preferred_element_type=F32)


def iota(shape, dim):
    return lax.broadcasted_iota(jnp.int32, shape, dim)


def expand(values, spread):
    lane = iota(values.shape, 1)
    high = values.astype(BF16).astype(F32)
    parts = jnp.where(lane < GROUP, high, jnp.where(lane < 2 * GROUP, values - high, 0.0))
    return mm(parts.astype(BF16), spread)


def conv_pre(joined_ref, at, taps, bias_row, aux):
    summed = bias_row + taps[0:1] * joined_ref[TAIL:, at]
    for offset in range(1, 4):
        moved = joined_ref[TAIL - offset : TAIL - offset + CHUNK, at]
        summed = summed + taps[offset : offset + 1] * (moved * aux[:, offset : offset + 1])
    return summed


def halves_rows(tile, low_lanes):
    zero = jnp.zeros_like(tile)
    return jnp.concatenate(
        [jnp.where(low_lanes, tile, zero), jnp.where(low_lanes, zero, tile)], 0
    )


def parts_of(values, count):
    parts = []
    for _ in range(count):
        low = values.astype(BF16)
        parts.append(low)
        values = values - low.astype(F32)
    return jnp.concatenate(parts, 0)


def order_masks():
    row = iota((CHUNK, CHUNK), 0)
    col = iota((CHUNK, CHUNK), 1)
    return row, col


def step_values(dt_ref, head_ref):
    raw = dt_ref + head_ref[0:1]
    dt = jnp.maximum(raw, 0.0) + jnp.log1p(jnp.exp(-jnp.abs(raw)))
    row, col = order_masks()
    lower = (row >= col).astype(BF16)
    log_decay = mm(jnp.concatenate([lower] * 3, 1), parts_of(dt * head_ref[1:2], 3))
    return raw, dt, log_decay, row, col


def scan_fwd_kernel(
    me_ref,
    x_ref,
    bcdt_ref,
    gate_ref,
    aux_ref,
    seg_ref,
    taps_ref,
    bias_ref,
    bc_taps_ref,
    bc_bias_ref,
    head_ref,
    skip_ref,
    gain_ref,
    spread_ref,
    u_ref,
    y_ref,
    sq_ref,
    kept_ref,
    state,
    tail_x,
    tail_bc,
    ending_ref,
):
    width = x_ref.shape[1]

    @pl.when(pl.program_id(0) == 0)
    def _():
        state[...] = jnp.zeros_like(state)
        tail_x[...] = jnp.zeros_like(tail_x)
        tail_bc[...] = jnp.zeros_like(tail_bc)

    aux = aux_ref[...]
    bc_now = bcdt_ref[:, : 2 * STATE]
    tail_bc[:TAIL] = tail_bc[CHUNK:]
    tail_bc[TAIL:] = bc_now
    bc_pre = conv_pre(tail_bc, slice(None), bc_taps_ref[...], bc_bias_ref[...], aux)
    bc = bc_pre * jax.nn.sigmoid(bc_pre)
    b_low = bc[:, :STATE].astype(BF16)
    c_low = bc[:, STATE:].astype(BF16)
    b_turned = bc[:, :STATE].T.astype(BF16)
    _, dt, log_decay, row, col = step_values(bcdt_ref[:, 2 * STATE :], head_ref)
    log_turned = log_decay.T
    meet = mm_t(c_low, b_low)
    visible = (aux[:, 0:1] == seg_ref[0]) & (row >= col)
    spread = spread_ref[...]
    dt_wide = expand(dt, spread)
    reach = expand(jnp.exp(log_decay) * aux[:, 4:5], spread)
    to_end = expand(jnp.exp(log_decay[CHUNK - 1 :] - log_decay) * aux[:, 5:6], spread)
    state_low = state[...].astype(BF16)
    kept_ref[0] = state_low
    carried = mm(c_low, state_low)
    low_lanes = iota((CHUNK, LANES), 1) < HEAD_DIM
    squares = jnp.zeros((CHUNK, LANES), F32)
    for pair in range(width // LANES):
        at = slice(pair * LANES, (pair + 1) * LANES)
        tail_x[:TAIL, at] = tail_x[CHUNK:, at]
        tail_x[TAIL:, at] = x_ref[:, at]
        pre = conv_pre(tail_x, at, taps_ref[:, at], bias_ref[:, at], aux)
        x_conv = pre * jax.nn.sigmoid(pre)
        inputs = x_conv * dt_wide[:, at]
        mats = []
        for head in (2 * pair, 2 * pair + 1):
            gap = log_decay[:, head : head + 1] - log_turned[head : head + 1, :]
            mats.append((jnp.exp(jnp.where(visible, gap, FAR)) * meet).astype(BF16))
        local = mm(jnp.concatenate(mats, 1), halves_rows(inputs.astype(BF16), low_lanes))
        y = local + carried[:, at] * reach[:, at] + skip_ref[:, at] * x_conv
        y_ref[:, at] = y.astype(y_ref.dtype)
        ending_ref[:, at] = (inputs * to_end[:, at]).astype(BF16)
        gate = gate_ref[:, at].astype(F32)
        gated = y * (gate * jax.nn.sigmoid(gate))
        grown = gated * gain_ref[:, at]
        u_ref[:, at] = grown.astype(BF16)
        squares = squares + gated * gated
    state[...] = state[...] * reach[CHUNK - 1 :] + mm(b_turned, ending_ref[...])
    ones = jnp.ones((8, LANES), F32)
    sums = lax.dot_general(
        ones, squares, (((1,), (1,)), ((), ())), precision=PRECISE, preferred_element_type=F32
    )
    sq_ref[...] = sums


def whole(shape):
    return pl.BlockSpec(shape, lambda *_: (0,) * len(shape))


def place_of(chunk, chunks, me_ref):
    part = chunks // 4
    away = chunk // part ^ me_ref[0]
    return (2 * (away % 2) + away // 2) * part + chunk % part


def scan_fwd(me, x_pre, bcdt_pre, gate_pre, side, weights):
    length, width = x_pre.shape
    chunks = length // CHUNK
    aux, seg_rows = side
    at = lambda c, m: (place_of(c, chunks, m), 0)
    tile = lambda columns: pl.BlockSpec((CHUNK, columns), at)
    in_specs = [
        tile(width),
        tile(bcdt_pre.shape[1]),
        tile(width),
        pl.BlockSpec((CHUNK, LANES), lambda c, m: (c, 0)),
        pl.BlockSpec((1, 1, CHUNK), lambda c, m: (c, 0, 0)),
    ] + [whole(w.shape) for w in weights]
    return pl.pallas_call(
        scan_fwd_kernel,
        grid_spec=pltpu.PrefetchScalarGridSpec(
            num_scalar_prefetch=1,
            grid=(chunks,),
            in_specs=in_specs,
            out_specs=[
                tile(width),
                tile(width),
                pl.BlockSpec((8, CHUNK), lambda c, m: (0, c)),
                pl.BlockSpec((1, STATE, width), lambda c, m: (c, 0, 0)),
            ],
            scratch_shapes=[
                pltpu.VMEM((STATE, width), F32),
                pltpu.VMEM((TAIL + CHUNK, width), F32),
                pltpu.VMEM((TAIL + CHUNK, 2 * STATE), F32),
                pltpu.VMEM((CHUNK, width), BF16),
            ],
        ),
        out_shape=[
            jax.ShapeDtypeStruct((length, width), BF16),
            jax.ShapeDtypeStruct((length, width), BF16),
            jax.ShapeDtypeStruct((8, length), F32),
            jax.ShapeDtypeStruct((chunks, STATE, width), BF16),
        ],
        compiler_params=pltpu.CompilerParams(vmem_limit_bytes=VMEM_BYTES),
        cost_estimate=pl.CostEstimate(
            flops=140 * length * width * LANES,
            bytes_accessed=20 * length * width,
            transcendentals=0,
        ),
        name="scan_fwd",
    )(me, x_pre, bcdt_pre, gate_pre, aux, seg_rows, *weights)


def gate_bwd_kernel(
    me_ref, gs_ref, y_ref, gate_ref, col_ref, gain_ref, g_gate_ref, g_y_ref, d_gain_ref
):
    @pl.when(pl.program_id(0) == 0)
    def _():
        d_gain_ref[...] = jnp.zeros_like(d_gain_ref)

    inv = col_ref[:, 0:1]
    pull = col_ref[:, 1:2]
    for pair in range(gs_ref.shape[1] // LANES):
        at = slice(pair * LANES, (pair + 1) * LANES)
        gs = gs_ref[:, at].astype(F32)
        y = y_ref[:, at].astype(F32)
        gate = gate_ref[:, at].astype(F32)
        sig = jax.nn.sigmoid(gate)
        act = gate * sig
        gated = y * act
        grown = gs * inv
        d_gain_ref[:, at] += jnp.sum(grown * gated, 0, keepdims=True)
        g_gated = grown * gain_ref[:, at] - gated * pull
        g_y_ref[:, at] = (g_gated * act).astype(BF16)
        g_gate_ref[:, at] = (g_gated * y * sig * (1.0 + gate * (1.0 - sig))).astype(BF16)


def gate_bwd(me, gs, y, gate_pre, columns, gain):
    length, width = gs.shape
    rows = length // 4
    tile = pl.BlockSpec((rows, width), lambda p, m: (p, 0))
    return pl.pallas_call(
        gate_bwd_kernel,
        grid_spec=pltpu.PrefetchScalarGridSpec(
            num_scalar_prefetch=1,
            grid=(4,),
            in_specs=[
                tile,
                tile,
                tile,
                pl.BlockSpec((rows, columns.shape[1]), lambda p, m: (2 * (p % 2) + p // 2 ^ m[0], 0)),
                whole(gain.shape),
            ],
            out_specs=[tile, tile, whole((1, width))],
        ),
        out_shape=[jax.ShapeDtypeStruct((length, width), BF16)] * 2
        + [jax.ShapeDtypeStruct((1, width), F32)],
        compiler_params=pltpu.CompilerParams(vmem_limit_bytes=VMEM_BYTES),
        cost_estimate=pl.CostEstimate(
            flops=50 * length * width * LANES,
            bytes_accessed=18 * length * width,
            transcendentals=0,
        ),
        name="gate_bwd",
    )(me, gs, y, gate_pre, columns, gain)


def conv_bwd(joined_ref, later_ref, grad, taps, aux, acc_ref, at):
    acc_ref[4:5, at] += jnp.sum(grad, 0, keepdims=True)
    acc_ref[0:1, at] += jnp.sum(grad * joined_ref[TAIL:, at], 0, keepdims=True)
    result = taps[0:1] * grad
    for offset in range(1, 4):
        moved = joined_ref[TAIL - offset : TAIL - offset + CHUNK, at]
        moved = moved * aux[:, offset : offset + 1]
        acc_ref[offset : offset + 1, at] += jnp.sum(grad * moved, 0, keepdims=True)
        later = later_ref[offset : offset + CHUNK, at] * aux[:, 5 + offset : 6 + offset]
        result = result + taps[offset : offset + 1] * later
    return result


def scan_bwd_kernel(
    me_ref,
    g_ref,
    x_ref,
    x_tail_ref,
    bcdt_ref,
    bc_tail_ref,
    kept_ref,
    aux_ref,
    seg_ref,
    taps_ref,
    bias_ref,
    bc_taps_ref,
    bc_bias_ref,
    head_ref,
    skip_ref,
    gain_ref,
    spread_ref,
    gx_ref,
    gbc_ref,
    gdt_ref,
    accx_ref,
    accbc_ref,
    grad_state,
    next_x,
    next_bc,
    joined_x,
    joined_bc,
    conv_ref,
    slope_ref,
    inputs_ref,
    coming_ref,
    ending_ref,
    sums_ref,
):
    width = x_ref.shape[1]

    @pl.when(pl.program_id(0) == 0)
    def _():
        grad_state[...] = jnp.zeros_like(grad_state)
        next_x[...] = jnp.zeros_like(next_x)
        next_bc[...] = jnp.zeros_like(next_bc)
        accx_ref[...] = jnp.zeros_like(accx_ref)
        accbc_ref[...] = jnp.zeros_like(accbc_ref)

    aux = aux_ref[...]
    joined_bc[:TAIL] = bc_tail_ref[:, : 2 * STATE]
    joined_bc[TAIL:] = bcdt_ref[:, : 2 * STATE]
    bc_pre = conv_pre(joined_bc, slice(None), bc_taps_ref[...], bc_bias_ref[...], aux)
    bc_sig = jax.nn.sigmoid(bc_pre)
    bc = bc_pre * bc_sig
    b_low = bc[:, :STATE].astype(BF16)
    c_low = bc[:, STATE:].astype(BF16)
    c_turned = bc[:, STATE:].T.astype(BF16)
    raw, dt, log_decay, row, col = step_values(bcdt_ref[:, 2 * STATE :], head_ref)
    log_turned = log_decay.T
    meet = mm_t(b_low, c_low)
    visible = (aux[:, 0:1] == seg_ref[0]) & (row <= col)
    spread = spread_ref[...]
    dt_wide = expand(dt, spread)
    reach = expand(jnp.exp(log_decay) * aux[:, 4:5], spread)
    to_end = expand(jnp.exp(log_decay[CHUNK - 1 :] - log_decay) * aux[:, 5:6], spread)
    low_lanes = iota((CHUNK, LANES), 1) < HEAD_DIM
    lane = iota((CHUNK, LANES), 1)
    for pair in range(width // LANES):
        at = slice(pair * LANES, (pair + 1) * LANES)
        joined_x[:TAIL, at] = x_tail_ref[:, at]
        joined_x[TAIL:, at] = x_ref[:, at]
        pre = conv_pre(joined_x, at, taps_ref[:, at], bias_ref[:, at], aux)
        sig = jax.nn.sigmoid(pre)
        x_conv = pre * sig
        inputs = x_conv * dt_wide[:, at]
        conv_ref[:, at] = x_conv
        slope_ref[:, at] = sig * (1.0 + pre * (1.0 - sig))
        inputs_ref[:, at] = inputs.astype(BF16)
        ending_ref[:, at] = (inputs * to_end[:, at]).astype(BF16)
        coming_ref[:, at] = (g_ref[:, at].astype(F32) * reach[:, at]).astype(BF16)
    state_low = kept_ref[0]
    grad_state_low = grad_state[...].astype(BF16)
    coming_low = coming_ref[...]
    ending_low = ending_ref[...]
    carried = mm(c_low, state_low)
    leaving = mm(b_low, grad_state_low)
    grad_c = mm_t(coming_low, state_low)
    grad_b = mm_t(ending_low, grad_state_low)
    last = reach[CHUNK - 1 :]
    passed = jnp.sum(grad_state[...] * state_low.astype(F32), 0, keepdims=True) * last
    through = mm_t(jnp.broadcast_to(passed, (8, width)).astype(BF16), spread)
    grad_state[...] = grad_state[...] * last + mm(c_turned, coming_low)
    grad_meet = jnp.zeros((CHUNK, CHUNK), F32)
    col_sums = jnp.zeros((CHUNK, LANES), F32)
    row_sums = jnp.zeros((LANES, CHUNK), F32)
    head_row = iota((LANES, CHUNK), 0)
    for pair in range(width // LANES):
        at = slice(pair * LANES, (pair + 1) * LANES)
        g_low = g_ref[:, at]
        grad_mats = mm_t(halves_rows(inputs_ref[:, at], low_lanes), g_low)
        mats = []
        for member in range(2):
            head = 2 * pair + member
            gap = log_turned[head : head + 1, :] - log_decay[:, head : head + 1]
            weight = jnp.exp(jnp.where(visible, gap, FAR))
            mats.append((weight * meet).astype(BF16))
            part = weight * grad_mats[member * CHUNK : (member + 1) * CHUNK]
            grad_meet = grad_meet + part
            product = part * meet
            col_sums = jnp.where(lane == head, jnp.sum(product, 1, keepdims=True), col_sums)
            row_sums = jnp.where(head_row == head, jnp.sum(product, 0, keepdims=True), row_sums)
        local = mm(jnp.concatenate(mats, 1), halves_rows(g_low, low_lanes))
        g = g_low.astype(F32)
        x_conv = conv_ref[:, at]
        leaving_now = leaving[:, at]
        grad_inputs = local + leaving_now * to_end[:, at]
        sums_ref[:CHUNK, at] = (coming_ref[:, at].astype(F32) * carried[:, at]).astype(BF16)
        sums_ref[CHUNK : 2 * CHUNK, at] = (
            ending_ref[:, at].astype(F32) * leaving_now
        ).astype(BF16)
        sums_ref[2 * CHUNK :, at] = (grad_inputs * x_conv).astype(BF16)
        accx_ref[5:6, at] += jnp.sum(g * x_conv, 0, keepdims=True)
        grad_conv = (grad_inputs * dt_wide[:, at] + g * skip_ref[:, at]) * slope_ref[:, at]
        next_x[CHUNK:, at] = next_x[:TAIL, at]
        next_x[:CHUNK, at] = grad_conv
        gx_ref[:, at] = conv_bwd(
            joined_x, next_x, grad_conv, taps_ref[:, at], aux, accx_ref, at
        ).astype(BF16)
    head_sums = mm_t(sums_ref[...], spread)
    upper = (row <= col).astype(BF16)
    strict = (row > col).astype(BF16)
    straddle = mm(
        jnp.concatenate([upper] * 3 + [strict] * 2, 1),
        jnp.concatenate(
            [
                parts_of(row_sums.T - col_sums + head_sums[:CHUNK], 3),
                parts_of(head_sums[CHUNK : 2 * CHUNK], 2),
            ],
            0,
        ),
    )
    straddle = straddle + through[0:1]
    grad_dt = head_sums[2 * CHUNK :] + head_ref[1:2] * straddle
    grad_raw = jnp.where(lane < GROUP, grad_dt * jax.nn.sigmoid(raw), 0.0)
    gdt_ref[...] = grad_raw.astype(BF16)
    accx_ref[6:7, :LANES] += jnp.sum(grad_raw, 0, keepdims=True)
    accx_ref[7:8, :LANES] += jnp.sum(dt * straddle, 0, keepdims=True)
    grad_meet_low = grad_meet.astype(BF16)
    grad_b = grad_b + mm(grad_meet_low, c_low)
    grad_c = grad_c + t_mm(grad_meet_low, b_low)
    grad_bc = jnp.concatenate([grad_b, grad_c], 1) * (bc_sig * (1.0 + bc_pre * (1.0 - bc_sig)))
    next_bc[CHUNK:] = next_bc[:TAIL]
    next_bc[:CHUNK] = grad_bc
    gbc_ref[...] = conv_bwd(
        joined_bc, next_bc, grad_bc, bc_taps_ref[...], aux, accbc_ref, slice(None)
    ).astype(BF16)


def scan_bwd(me, g_y, x_pre, bcdt_pre, kept, side, weights):
    length, width = x_pre.shape
    chunks = length // CHUNK
    aux, seg_rows = side
    back = lambda c: chunks - 1 - c
    place = lambda c, m: place_of(back(c), chunks, m)
    tile = lambda columns: pl.BlockSpec((CHUNK, columns), lambda c, m: (place(c, m), 0))

    def tail_at(c, m):
        before = place_of(jnp.maximum(back(c) - 1, 0), chunks, m)
        return (before * (CHUNK // TAIL) + CHUNK // TAIL - 1, 0)

    tail = lambda columns: pl.BlockSpec((TAIL, columns), tail_at)
    wide = bcdt_pre.shape[1]
    in_specs = [
        tile(width),
        tile(width),
        tail(width),
        tile(wide),
        tail(wide),
        pl.BlockSpec((1, STATE, width), lambda c, m: (back(c), 0, 0)),
        pl.BlockSpec((CHUNK, LANES), lambda c, m: (back(c), 0)),
        pl.BlockSpec((1, 1, CHUNK), lambda c, m: (back(c), 0, 0)),
    ] + [whole(w.shape) for w in weights]
    return pl.pallas_call(
        scan_bwd_kernel,
        grid_spec=pltpu.PrefetchScalarGridSpec(
            num_scalar_prefetch=1,
            grid=(chunks,),
            in_specs=in_specs,
            out_specs=[
                tile(width),
                tile(2 * STATE),
                tile(LANES),
                whole((8, width)),
                whole((8, 2 * STATE)),
            ],
            scratch_shapes=[
                pltpu.VMEM((STATE, width), F32),
                pltpu.VMEM((TAIL + CHUNK, width), F32),
                pltpu.VMEM((TAIL + CHUNK, 2 * STATE), F32),
                pltpu.VMEM((TAIL + CHUNK, width), F32),
                pltpu.VMEM((TAIL + CHUNK, 2 * STATE), F32),
                pltpu.VMEM((CHUNK, width), F32),
                pltpu.VMEM((CHUNK, width), F32),
                pltpu.VMEM((CHUNK, width), BF16),
                pltpu.VMEM((CHUNK, width), BF16),
                pltpu.VMEM((CHUNK, width), BF16),
                pltpu.VMEM((3 * CHUNK, width), BF16),
            ],
        ),
        out_shape=[
            jax.ShapeDtypeStruct((length, width), BF16),
            jax.ShapeDtypeStruct((length, 2 * STATE), BF16),
            jax.ShapeDtypeStruct((length, LANES), BF16),
            jax.ShapeDtypeStruct((8, width), F32),
            jax.ShapeDtypeStruct((8, 2 * STATE), F32),
        ],
        compiler_params=pltpu.CompilerParams(vmem_limit_bytes=VMEM_BYTES),
        cost_estimate=pl.CostEstimate(
            flops=280 * length * width * LANES,
            bytes_accessed=20 * length * width,
            transcendentals=0,
        ),
        name="scan_bwd",
    )(me, g_y, x_pre, x_pre, bcdt_pre, bcdt_pre, kept, aux, seg_rows, *weights)


def side_arrays(segments):
    length = segments.shape[0]
    seg = segments.astype(F32)
    columns = [seg]
    nothing = lambda count: jnp.full((count,), -1.0, F32)
    for offset in range(1, 4):
        moved = jnp.concatenate([nothing(offset), seg[: length - offset]], 0)
        columns.append((moved == seg).astype(F32))
    blocks = seg.reshape(-1, CHUNK)
    ends = blocks[:, -1]
    before = jnp.concatenate([nothing(1), ends[:-1]], 0)
    columns.append((blocks == before[:, None]).astype(F32).reshape(-1))
    columns.append((blocks == ends[:, None]).astype(F32).reshape(-1))
    for offset in range(1, 4):
        moved = jnp.concatenate([seg[offset:], nothing(offset)], 0)
        columns.append((moved == seg).astype(F32))
    stacked = jnp.stack(columns, 1)
    aux = jnp.pad(stacked, ((0, 0), (0, LANES - stacked.shape[1])))
    return aux, blocks.reshape(-1, 1, CHUNK)


def in_groups(values):
    padded = jnp.pad(values, [(0, 0)] * (values.ndim - 1) + [(0, GROUP - values.shape[-1])])
    return jnp.tile(padded, (1,) * (values.ndim - 1) + (LANES // GROUP,))


def spread_matrix(width):
    head = lax.broadcasted_iota(jnp.int32, (LANES, width), 0) % GROUP
    owner = lax.broadcasted_iota(jnp.int32, (LANES, width), 1) // HEAD_DIM
    return (head == owner).astype(BF16)


def scan_weights(taps, bias, bc_taps, bc_bias, dt_bias, a_log, d_skip, gain, spread):
    rates = -jnp.exp(a_log)
    rows = jnp.stack([in_groups(dt_bias), in_groups(rates)])
    head = jnp.pad(rows, ((0, 6), (0, 0)))
    return (
        taps,
        bias[None],
        bc_taps,
        bc_bias[None],
        head,
        jnp.repeat(d_skip, HEAD_DIM)[None],
        gain[None],
        spread,
    )


def partners(count, step):
    return [(index, index ^ step) for index in range(count)]


def swap(values, axis, step):
    return lax.ppermute(values, axis, partners(lax.axis_size(axis), step))


def after(values, *earlier):
    return lax.optimization_barrier((values, *earlier))[0]


def dp_masks():
    masks = []
    step = lax.axis_size("dp") // 2
    while step > 0:
        masks.append(step)
        step = step // 2
    return masks


def offsets(masks):
    found = [0]
    for mask in masks:
        found = found + [offset ^ mask for offset in found]
    return found


class Rows:
    def __init__(self, own):
        self.rows = own

    def stage(self, mask, *earlier):
        got = swap(after(self.rows, *earlier), "dp", mask)
        self.rows = jnp.concatenate([self.rows, got], 0)
        return got

    def begin(self, masks, *earlier):
        for mask in masks[:-2]:
            got = self.stage(mask, *earlier)
            earlier = ()
        return got


def scatter_first(kept, got):
    total = kept + got.astype(F32)
    height = total.shape[0] // 2
    return total[:height], total[height:].astype(BF16)


def scatter_rest(kept, sent, masks):
    for mask in reversed(masks[1:-1]):
        kept, sent = scatter_first(kept, swap(sent, "dp", mask))
    return kept + swap(sent, "dp", masks[0]).astype(F32)


def grad_half(rows, grads, which):
    width = rows.shape[1] // 2
    dims = (((0,), (0,)), ((), ()))
    taken = rows[:, which * width : (which + 1) * width]
    return lax.dot_general(taken, grads, dims, preferred_element_type=F32)


def sent_half(rows, grads):
    return grad_half(rows, grads, 1).astype(BF16)


def reordered(values, me):
    size = values.shape[0] // 4
    return jnp.concatenate(
        [lax.dynamic_slice_in_dim(values, (away ^ me) * size, size, 0) for away in (0, 2, 1, 3)], 0
    )


def restored(values, me):
    size = values.shape[0] // 4
    parts = []
    for part in range(4):
        away = part ^ me
        parts.append(
            lax.dynamic_slice_in_dim(values, (2 * (away % 2) + away // 2) * size, size, 0)
        )
    return jnp.concatenate(parts, 0)


def turned_over(values, size):
    shaped = values.reshape(-1, 2, size, values.shape[1])
    return shaped[:, ::-1].reshape(values.shape)


def own_quarter(values, me):
    size = values.shape[0] // 4
    return lax.dynamic_slice_in_dim(values, me * size, size, 0)


def tensor_sum(values):
    values = values + swap(values, "tensor", 1)
    return values + swap(values, "tensor", 2)


def dp_sum(values):
    step = 1
    while step < lax.axis_size("dp"):
        values = values + swap(values, "dp", step)
        step = 2 * step
    return values


def dot(lhs, rhs):
    return lax.dot_general(lhs, rhs, (((1,), (0,)), ((), ())), preferred_element_type=F32)


def dot_t(lhs, rhs):
    return lax.dot_general(lhs, rhs, (((1,), (1,)), ((), ())), preferred_element_type=F32)


def own_order(features, masks, earlier):
    place = after(lax.axis_index("dp"), earlier)
    found = offsets(masks)
    height = features // len(found)
    index = lax.broadcasted_iota(jnp.int32, (1, features), 1)
    part, within = index // height, index % height
    away = jnp.zeros_like(part)
    for position, offset in enumerate(found):
        away = jnp.where(part == position, offset, away)
    source = (away ^ place) * height + within
    return (lax.broadcasted_iota(jnp.int32, (features, features), 0) == source).astype(BF16)


def rms_of(stream):
    return lax.rsqrt(jnp.mean(stream * stream, -1, keepdims=True) + EPSILON)


def on_device(
    hidden,
    segments,
    norm_gain,
    w_z,
    w_x,
    w_bc,
    w_dt,
    conv_x_w,
    conv_x_b,
    conv_bc_w,
    conv_bc_b,
    dt_bias,
    a_log,
    d_skip,
    gated_gain,
    w_out,
    cotangent,
):
    length, features = hidden.shape
    width = w_x.shape[2]
    heads = dt_bias.shape[1]
    masks = dp_masks()
    place = lax.axis_index("tensor")
    core, far = place % 2, place // 2
    me = place
    me_row = me.astype(jnp.int32)[None]
    half = length // 2
    quarter = length // 4

    side_first = masks[-1:] + masks[:-1]
    seated = [offsets(side_first).index(offset) for offset in offsets(masks)]
    height = w_x.shape[1]
    quart_bc = w_bc.shape[2] // 4
    own_bc = lax.dynamic_slice_in_dim(w_bc, place * quart_bc, quart_bc, 2)
    w_small = jnp.concatenate([own_bc[0], own_bc[1], w_dt[0], w_dt[1]], 1)
    w_small = jnp.pad(w_small, ((0, 0), (0, 2 * LANES - w_small.shape[1])))

    x0, z0, out0 = Rows(w_x[0]), Rows(w_z[0]), Rows(w_out[0])
    x1, z1, out1 = Rows(w_x[1]), Rows(w_z[1]), Rows(w_out[1])
    small = Rows(w_small)
    near_mask, side_mask = masks[-2:]
    x0_far = x0.begin(masks)
    small_far = small.begin(masks)
    out1_side = out1.stage(side_mask)
    x0_near = x0.stage(near_mask, small_far)
    small_near = small.stage(near_mask, x0_far)
    z0_far = z0.begin(masks, x0_far, small_far)
    small.stage(side_mask)
    x0.stage(side_mask)
    out0_far = out0.begin(masks, x0_near, small_near, z0_far)
    z0_near = z0.stage(near_mask, x0_near, small_near)
    x1_far = x1.begin(masks, z0_near, out0_far)
    out0_near = out0.stage(near_mask, z0_near)
    z0.stage(side_mask)
    z1_far = z1.begin(masks, out0_near, x1_far)
    x1_near = x1.stage(near_mask, out0_near)
    out0.stage(side_mask)
    out1_far = out1.begin(masks, x1_near, z1_far)
    z1_near = z1.stage(near_mask, x1_near)
    x1_side = x1.stage(side_mask)
    out1_near = out1.stage(near_mask, z1_near)
    z1_side = z1.stage(side_mask)
    out1_rows = [out1.rows[seat * height : (seat + 1) * height] for seat in seated]
    x_rows, z_rows = [x0.rows, x1.rows], [z0.rows, z1.rows]
    out_rows = [out0.rows, jnp.concatenate(out1_rows, 0)]
    small_rows = small.rows

    own_cols = small_rows[:, :LANES]
    across = swap(own_cols, "tensor", 2)
    beside = swap(jnp.concatenate([own_cols, across], 1), "tensor", 1)

    def small_columns(layer):
        low = layer * quart_bc
        parts = [
            own_cols[:, low : low + quart_bc],
            across[:, low : low + quart_bc],
            beside[:, low : low + quart_bc],
            beside[:, LANES + low : LANES + low + quart_bc],
        ]
        first = core == 0
        near = [jnp.where(first, parts[0], parts[2]), jnp.where(first, parts[2], parts[0])]
        away = [jnp.where(first, parts[1], parts[3]), jnp.where(first, parts[3], parts[1])]
        first = far == 0
        ordered = [jnp.where(first, n, a) for n, a in zip(near, away)]
        ordered += [jnp.where(first, a, n) for n, a in zip(near, away)]
        at = LANES + layer * heads
        return jnp.concatenate(ordered + [in_groups(small_rows[:, at : at + heads])], 1)

    bcdt_rows = [small_columns(layer) for layer in range(LAYERS)]

    order = lax.optimization_barrier(own_order(features, masks, x0_far))
    side = side_arrays(after(segments, x0_far))
    spread = spread_matrix(width)
    weights = [
        scan_weights(
            conv_x_w[layer],
            conv_x_b[layer],
            conv_bc_w[layer],
            conv_bc_b[layer],
            dt_bias[layer],
            a_log[layer],
            d_skip[layer],
            gated_gain[layer],
            spread,
        )
        for layer in range(LAYERS)
    ]
    order, side, weights = lax.optimization_barrier((order, side, weights))
    hidden_rows = reordered(after(hidden, x0_far), me)
    hidden_low = dot(after(hidden_rows, x0_near, small_near, out1_side), order).astype(BF16)
    cotangent_rows = reordered(after(cotangent, x0_far), me)
    cotangent_low = dot(after(cotangent_rows, hidden_low, z0_near), order).astype(BF16)
    gains = mm(after(norm_gain, small_near), order.astype(F32), PRECISE)
    hidden_low, cotangent_low, gains = lax.optimization_barrier(
        (hidden_low, cotangent_low, gains)
    )

    def columns_of(values, which):
        return lax.dynamic_slice_in_dim(values, which * STATE, STATE, 1)

    stream = hidden_low.astype(F32)
    normed0 = (stream * rms_of(stream) * gains[0]).astype(BF16)
    stream0 = hidden_low[:quarter].astype(F32)
    x_pre0 = dot(normed0, x_rows[0])
    bcdt_pre0 = dot(after(normed0, x_pre0, z0_near, out0_far), bcdt_rows[0])
    gate_pre0 = dot(after(normed0, bcdt_pre0, out0_near, x1_far), z_rows[0]).astype(BF16)
    u0, y0, sq, kept0 = scan_fwd(me_row, x_pre0, bcdt_pre0, gate_pre0, side, weights[0])
    u_now = after(u0, x1_near, z1_far)
    sent = dot_t(u_now[half:], out_rows[0]).astype(BF16)
    sq = sq[0:1]
    sq = sq + swap(sq, "tensor", 1)
    u_now = after(u_now, sent, sq)
    mine = dot_t(u_now[:half], out_rows[0]) + swap(sent, "tensor", 1).astype(F32)
    sq = sq + swap(sq, "tensor", 2)
    away = after(mine[quarter:].astype(BF16), sq)
    got = swap(away, "tensor", 2)
    inv0 = lax.rsqrt(sq / INNER + EPSILON)[0]
    got, mine, z1_near, out1_far, x1_side = lax.optimization_barrier(
        (got, mine, z1_near, out1_far, x1_side)
    )
    total0 = mine[:quarter] + got.astype(F32)
    stream1 = stream0 + own_quarter(inv0, me)[:, None] * total0
    normed_own = (stream1 * rms_of(stream1) * gains[1]).astype(BF16)
    normed_half = jnp.concatenate([normed_own, swap(normed_own, "tensor", 2)], 0)
    normed_half, z1_side = lax.optimization_barrier((normed_half, z1_side))
    normed1 = jnp.concatenate([normed_half, swap(normed_half, "tensor", 1)], 0)
    scaled0 = (u0.astype(F32) * reordered(inv0, me)[:, None]).astype(BF16)

    x_pre1 = dot(after(normed1, out1_near), x_rows[1])
    bcdt_pre1 = dot(normed1, bcdt_rows[1])
    gate_pre1 = dot(normed1, z_rows[1]).astype(BF16)
    u1, y1, sq, kept1 = scan_fwd(me_row, x_pre1, bcdt_pre1, gate_pre1, side, weights[1])
    scaled_grad1 = dot(cotangent_low, out_rows[1])
    cross = restored(jnp.sum(scaled_grad1 * u1.astype(F32), -1), me)
    both = tensor_sum(jnp.stack([sq[0], cross]))
    mixed_sent = dot_t(u1[half:], out_rows[1]).astype(BF16)
    mixed_mine = dot_t(u1[:half], out_rows[1])
    mixed_mine = mixed_mine + swap(mixed_sent, "tensor", 1).astype(F32)
    both = after(both, mixed_sent, mixed_mine)
    mixed_got = swap(mixed_mine[quarter:].astype(BF16), "tensor", 2)
    inv1 = lax.rsqrt(both[0] / INNER + EPSILON)

    columns = jnp.stack([inv1, inv1 * inv1 * inv1 * both[1] / INNER], 1)
    g_gate1, g_y, d_gain1 = gate_bwd(
        me_row, scaled_grad1, y1, gate_pre1, columns, gated_gain[1][None]
    )
    z_sent = sent_half(normed1, g_gate1)
    z_got = swap(z_sent, "dp", 1)
    g_y = after(g_y, z_sent)
    g_x1, g_bc1, g_dt1, acc_x1, acc_bc1 = scan_bwd(
        me_row, g_y, x_pre1, bcdt_pre1, kept1, side, weights[1]
    )
    g_x1, z_got, mixed_got = lax.optimization_barrier((g_x1, z_got, mixed_got))

    def grad_rows(rows, g_gate, g_x, g_bcdt, layer):
        return (
            dot_t(g_gate[rows], z_rows[layer])
            + dot_t(g_x[rows], x_rows[layer])
            + dot_t(g_bcdt[rows], bcdt_rows[layer])
        )

    g_bcdt = jnp.concatenate([g_bc1, g_dt1], 1)
    sent = grad_rows(slice(half, length), g_gate1, g_x1, g_bcdt, 1).astype(BF16)
    cotangent_now = after(cotangent_low, sent)
    scaled1 = (u1.astype(F32) * reordered(inv1, me)[:, None]).astype(BF16)
    out_sent = sent_half(cotangent_now, scaled1)
    out_got = swap(out_sent, "dp", 1)
    own = grad_rows(slice(0, half), after(g_gate1, out_sent), g_x1, g_bcdt, 1)
    mine = own + swap(sent, "tensor", 1).astype(F32)
    away = mine[quarter:].astype(BF16)
    got = swap(away, "tensor", 2)
    normed_now = after(normed1, away)
    z_kept, z_next = scatter_first(grad_half(normed_now, g_gate1, 0), z_got)
    z_near = swap(z_next, "dp", near_mask)
    normed_now = after(normed_now, z_next)
    x_sent = sent_half(normed_now, g_x1)
    x_kept_half = grad_half(normed_now, g_x1, 0)
    out_kept_half = grad_half(after(cotangent_now, away), scaled1, 0)
    mixed_total = mixed_mine[:quarter] + mixed_got.astype(F32)
    last = stream1 + own_quarter(inv1, me)[:, None] * mixed_total
    mixed_own = dot_t(last.astype(BF16), order).astype(BF16)
    got, mine, out_got, z_near, x_sent, out_kept_half, x_kept_half, mixed_own = (
        lax.optimization_barrier(
            (got, mine, out_got, z_near, x_sent, out_kept_half, x_kept_half, mixed_own)
        )
    )
    x_got = swap(x_sent, "dp", 1)
    total = mine[:quarter] + got.astype(F32)
    rms = rms_of(stream1)
    normal = stream1 * rms
    grown = total * gains[1]
    grad_stream = cotangent_low[:quarter].astype(F32) + rms * (
        grown - normal * jnp.mean(grown * normal, -1, keepdims=True)
    )
    grad_own = grad_stream.astype(BF16)
    out_kept, out_next = scatter_first(out_kept_half, out_got)
    out_near = swap(out_next, "dp", near_mask)
    z_kept, z_next = scatter_first(z_kept, z_near)
    z_far = swap(z_next, "dp", masks[-3])
    total_now = after(total, grad_own)
    d_norm1 = jnp.sum(total_now * normal, 0)
    cross = jnp.sum(grad_own.astype(F32) * total0, -1)
    grad_half_rows = jnp.concatenate([grad_own, swap(grad_own, "tensor", 2)], 0)
    cross = jnp.concatenate([cross, swap(cross, "tensor", 2)], 0)
    grad_half_rows, cross, z_far, out_near = lax.optimization_barrier(
        (grad_half_rows, cross, z_far, out_near)
    )
    grad0 = jnp.concatenate([grad_half_rows, swap(grad_half_rows, "tensor", 1)], 0)
    cross = restored(jnp.concatenate([cross, swap(cross, "tensor", 1)], 0), me)
    out_kept, out_next = scatter_first(out_kept, out_near)
    out_far = swap(out_next, "dp", masks[-3])

    grad0 = lax.optimization_barrier(grad0)
    out_sent0 = sent_half(grad0, scaled0)
    out_got0 = swap(out_sent0, "dp", 1)
    scaled_grad0 = dot(after(grad0, out_sent0), out_rows[0])
    columns = jnp.stack([inv0, inv0 * inv0 * inv0 * cross / INNER], 1)
    g_gate0, g_y, d_gain0 = gate_bwd(
        me_row, scaled_grad0, y0, gate_pre0, columns, gated_gain[0][None]
    )
    z_sent0 = sent_half(normed0, g_gate0)
    z_got0 = swap(z_sent0, "dp", 1)
    g_y, z_sent0, x_got, out_far = lax.optimization_barrier((g_y, z_sent0, x_got, out_far))
    x_kept, x_next = scatter_first(x_kept_half, x_got)
    x_near = swap(x_next, "dp", near_mask)
    g_y = after(g_y, x_next)
    mixed = lax.all_gather(after(mixed_own, grad0), "tensor", axis=0).reshape(length, features)
    away1 = swap(after(columns_of(g_bc1, 1 - far), grad0), "tensor", 2)
    g_x0, g_bc0, g_dt0, acc_x0, acc_bc0 = scan_bwd(
        me_row, g_y, x_pre0, bcdt_pre0, kept0, side, weights[0]
    )
    away0 = swap(columns_of(g_bc0, 1 - far), "tensor", 2)
    g_x0, away1, x_near, out_got0 = lax.optimization_barrier((g_x0, away1, x_near, out_got0))
    x_sent0 = sent_half(normed0, g_x0)
    x_got0 = swap(x_sent0, "dp", 1)
    g_x0 = after(g_x0, x_sent0)
    g_bcdt = jnp.concatenate([g_bc0, g_dt0], 1)
    sent = grad_rows(slice(half, length), g_gate0, g_x0, g_bcdt, 0).astype(BF16)
    out_kept_half0 = grad_half(after(grad0, sent), scaled0, 0)
    out_kept0, out_next0 = scatter_first(out_kept_half0, out_got0)
    out_near0 = swap(out_next0, "dp", near_mask)
    own = grad_rows(slice(0, half), after(g_gate0, out_next0), g_x0, g_bcdt, 0)
    mine = own + swap(sent, "tensor", 1).astype(F32)
    away = mine[quarter:].astype(BF16)
    got = swap(away, "tensor", 2)
    normed_now, z_got0, x_near, away0, _ = lax.optimization_barrier(
        (normed0, z_got0, x_near, away0, away)
    )
    z_kept0, z_next0 = scatter_first(grad_half(normed_now, g_gate0, 0), z_got0)
    z_near0 = swap(z_next0, "dp", near_mask)
    normed_now = after(normed_now, z_next0)
    x_kept, x_next = scatter_first(x_kept, x_near)
    x_kept_half0 = grad_half(normed_now, g_x0, 0)
    x_kept_half0, out_near0, x_next = lax.optimization_barrier((x_kept_half0, out_near0, x_next))
    x_far = swap(x_next, "dp", masks[-3])
    out_kept0, out_next0 = scatter_first(out_kept0, out_near0)
    out_far0 = swap(out_next0, "dp", masks[-3])
    got, mine, out_next0 = lax.optimization_barrier((got, mine, out_next0))
    total = mine[:quarter] + got.astype(F32)
    rms = rms_of(stream0)
    normal = stream0 * rms
    grown = total * gains[0]
    grad_stream = grad_stream + rms * (
        grown - normal * jnp.mean(grown * normal, -1, keepdims=True)
    )
    d_hidden = dot_t(grad_stream.astype(BF16), order).astype(BF16)
    x_got0, z_near0, _ = lax.optimization_barrier((x_got0, z_near0, d_hidden))
    x_kept0, x_next0 = scatter_first(x_kept_half0, x_got0)
    x_near0 = swap(x_next0, "dp", near_mask)
    x_next0_first = x_next0
    z_kept0, z_next0 = scatter_first(z_kept0, z_near0)
    z_far0 = swap(z_next0, "dp", masks[-3])
    d_hidden = jnp.concatenate([d_hidden, swap(d_hidden, "tensor", 2)], 0)
    d_half = d_hidden
    d_norm0 = jnp.sum(after(total, d_half) * normal, 0)
    d_hidden = jnp.concatenate([d_hidden, swap(d_hidden, "tensor", 1)], 0)
    out_kept, x_kept, z_kept, out_kept0, z_kept0, _ = lax.optimization_barrier(
        (out_kept, x_kept, z_kept, out_kept0, z_kept0, d_half)
    )
    d_hidden = restored(d_hidden, me).astype(F32)

    def finished(kept, sent):
        for mask in reversed(masks[:-3]):
            kept, sent = scatter_first(kept, sent)
            sent = swap(sent, "dp", mask)
        return kept + sent.astype(F32)

    x_kept0, x_next0 = scatter_first(x_kept0, x_near0)
    d_out1 = finished(out_kept, out_far)
    d_x1 = finished(x_kept, x_far)
    d_z1 = finished(z_kept, z_far)
    d_out0 = finished(out_kept0, out_far0)
    d_z0 = finished(z_kept0, z_far0)
    d_x0 = finished(x_kept0, swap(x_next0, "dp", masks[-3]))

    near_cols = jnp.concatenate([columns_of(v, far) for v in (g_bc0, g_bc1)], 1)
    near_cols = after(near_cols, x_next0_first)
    away_cols = jnp.concatenate([away0, away1], 1)
    bc_sum = near_cols.astype(F32) + turned_over(away_cols, quarter).astype(F32)
    across_sum = swap(bc_sum.astype(BF16), "tensor", 1)
    bc_sum = bc_sum + turned_over(across_sum, half).astype(F32)
    small_sent, small_kept = [], []
    for layer, (rows, g_dt) in enumerate(((normed0, g_dt0), (normed1, g_dt1))):
        summed = bc_sum[:, layer * STATE : (layer + 1) * STATE]
        rolled = jnp.roll(summed, STATE // 2, 1)
        own_cols = jnp.where(core == 0, summed, rolled)[:, : STATE // 2].astype(BF16)
        own_cols = jnp.concatenate([own_cols, g_dt[:, : STATE // 2]], 1)
        small_sent.append(sent_half(rows, own_cols))
        small_kept.append(grad_half(rows, own_cols, 0))
    small_sent = after(jnp.concatenate(small_sent, 1), x_got0)
    small_got = swap(small_sent, "dp", 1)
    small_kept, small_next = scatter_first(jnp.concatenate(small_kept, 1), small_got)
    d_small = scatter_rest(small_kept, small_next, masks)
    d_small = jnp.stack([d_small[:, layer * LANES : (layer + 1) * LANES] for layer in range(LAYERS)])
    found = jnp.array(offsets(masks), jnp.int32)
    norm_part = jnp.stack([d_norm0, d_norm1]).reshape(LAYERS, len(found), 1, height)
    here = (found ^ lax.axis_index("dp"))[:, None] == jnp.arange(len(found))[None]
    norm_part = jnp.sum(jnp.where(here[None, :, :, None], norm_part, 0.0), 1)
    shared = jnp.concatenate(
        [acc_bc0, acc_bc1, jnp.zeros((8, width - 4 * STATE), F32)], 1
    )
    shared = tensor_sum(jnp.concatenate([shared, norm_part.reshape(-1, width)], 0))
    gains_part = jnp.concatenate([d_gain0, d_gain1], 0)
    summed = dp_sum(jnp.concatenate([acc_x0, acc_x1, gains_part, shared], 0))
    acc = summed[:16].reshape(LAYERS, 8, width)
    shared = summed[16 + LAYERS :]
    bc_acc = jnp.stack([shared[:8, : 2 * STATE], shared[:8, 2 * STATE : 4 * STATE]])
    d_norm_gain = shared[8:].reshape(LAYERS, features)
    d_skips = acc[:, 5].reshape(LAYERS, heads, HEAD_DIM).sum(2)
    own_width = STATE // 2
    return (
        mixed,
        d_hidden,
        d_norm_gain,
        jnp.stack([d_z0, d_z1]),
        jnp.stack([d_x0, d_x1]),
        d_small[:, :, :own_width],
        d_small[:, :, own_width : own_width + heads],
        acc[:, :4],
        acc[:, 4],
        bc_acc[:, :4],
        bc_acc[:, 4],
        acc[:, 6, :heads],
        acc[:, 7, :heads] * -jnp.exp(a_log),
        d_skips,
        summed[16 : 16 + LAYERS],
        jnp.stack([d_out0, d_out1]),
    )


def solution(mesh):
    in_specs = (
        P("dp", None),
        P("dp"),
        P(),
        P(None, "dp", "tensor"),
        P(None, "dp", "tensor"),
        P(None, "dp", None),
        P(None, "dp", "tensor"),
        P(None, None, "tensor"),
        P(None, "tensor"),
        P(),
        P(),
        P(None, "tensor"),
        P(None, "tensor"),
        P(None, "tensor"),
        P(None, "tensor"),
        P(None, "dp", "tensor"),
        P("dp", None),
    )
    out_specs = (
        P("dp", None),
        P("dp", None),
        P(),
        P(None, "dp", "tensor"),
        P(None, "dp", "tensor"),
        P(None, "dp", "tensor"),
        P(None, "dp", "tensor"),
        P(None, None, "tensor"),
        P(None, "tensor"),
        P(),
        P(),
        P(None, "tensor"),
        P(None, "tensor"),
        P(None, "tensor"),
        P(None, "tensor"),
        P(None, "dp", "tensor"),
    )
    return jax.shard_map(
        on_device, mesh=mesh, in_specs=in_specs, out_specs=out_specs, check_vma=False
    )
```

```python
import jax
import jax.numpy as jnp
from jax import lax
from jax.sharding import PartitionSpec as P
from jax.experimental import pallas as pl
from jax.experimental.pallas import tpu as pltpu

HEAD_DIM = 64
STATE = 128
PACK = 1024
LAYERS = 2
INNER = 3072
EPSILON = 1e-05
CHUNK = 128
LANES = 128
GROUP = 16
TAIL = 16
FAR = -10000.0
PRECISE = lax.Precision.HIGHEST
BF16 = jnp.bfloat16
F32 = jnp.float32
VMEM_BYTES = 48 * 1024 * 1024


def mm(lhs, rhs, precision=None):
    return lax.dot_general(
        lhs, rhs, (((1,), (0,)), ((), ())), precision=precision, preferred_element_type=F32
    )


def mm_t(lhs, rhs):
    return lax.dot_general(lhs, rhs, (((1,), (1,)), ((), ())), preferred_element_type=F32)


def t_mm(lhs, rhs):
    return lax.dot_general(lhs, rhs, (((0,), (0,)), ((), ())), preferred_element_type=F32)


def iota(shape, dim):
    return lax.broadcasted_iota(jnp.int32, shape, dim)


def expand(values, spread):
    lane = iota(values.shape, 1)
    high = values.astype(BF16).astype(F32)
    parts = jnp.where(lane < GROUP, high, jnp.where(lane < 2 * GROUP, values - high, 0.0))
    return mm(parts.astype(BF16), spread)


def conv_pre(joined_ref, at, taps, bias_row, aux):
    summed = bias_row + taps[0:1] * joined_ref[TAIL:, at]
    for offset in range(1, 4):
        moved = joined_ref[TAIL - offset : TAIL - offset + CHUNK, at]
        summed = summed + taps[offset : offset + 1] * (moved * aux[:, offset : offset + 1])
    return summed


def halves_rows(tile, low_lanes):
    zero = jnp.zeros_like(tile)
    return jnp.concatenate(
        [jnp.where(low_lanes, tile, zero), jnp.where(low_lanes, zero, tile)], 0
    )


def parts_of(values, count):
    parts = []
    for _ in range(count):
        low = values.astype(BF16)
        parts.append(low)
        values = values - low.astype(F32)
    return jnp.concatenate(parts, 0)


def order_masks():
    row = iota((CHUNK, CHUNK), 0)
    col = iota((CHUNK, CHUNK), 1)
    return row, col


def step_values(dt_ref, head_ref):
    raw = dt_ref + head_ref[0:1]
    dt = jnp.maximum(raw, 0.0) + jnp.log1p(jnp.exp(-jnp.abs(raw)))
    row, col = order_masks()
    lower = (row >= col).astype(BF16)
    log_decay = mm(jnp.concatenate([lower] * 3, 1), parts_of(dt * head_ref[1:2], 3))
    return raw, dt, log_decay, row, col


def scan_fwd_kernel(
    me_ref,
    x_ref,
    bcdt_ref,
    gate_ref,
    aux_ref,
    seg_ref,
    taps_ref,
    bias_ref,
    bc_taps_ref,
    bc_bias_ref,
    head_ref,
    skip_ref,
    gain_ref,
    spread_ref,
    u_ref,
    y_ref,
    sq_ref,
    kept_ref,
    state,
    tail_x,
    tail_bc,
    ending_ref,
):
    width = x_ref.shape[1]

    @pl.when(pl.program_id(0) == 0)
    def _():
        state[...] = jnp.zeros_like(state)
        tail_x[...] = jnp.zeros_like(tail_x)
        tail_bc[...] = jnp.zeros_like(tail_bc)

    aux = aux_ref[...]
    bc_now = bcdt_ref[:, : 2 * STATE]
    tail_bc[:TAIL] = tail_bc[CHUNK:]
    tail_bc[TAIL:] = bc_now
    bc_pre = conv_pre(tail_bc, slice(None), bc_taps_ref[...], bc_bias_ref[...], aux)
    bc = bc_pre * jax.nn.sigmoid(bc_pre)
    b_low = bc[:, :STATE].astype(BF16)
    c_low = bc[:, STATE:].astype(BF16)
    b_turned = bc[:, :STATE].T.astype(BF16)
    _, dt, log_decay, row, col = step_values(bcdt_ref[:, 2 * STATE :], head_ref)
    log_turned = log_decay.T
    meet = mm_t(c_low, b_low)
    visible = (aux[:, 0:1] == seg_ref[0]) & (row >= col)
    spread = spread_ref[...]
    dt_wide = expand(dt, spread)
    reach = expand(jnp.exp(log_decay) * aux[:, 4:5], spread)
    to_end = expand(jnp.exp(log_decay[CHUNK - 1 :] - log_decay) * aux[:, 5:6], spread)
    state_low = state[...].astype(BF16)
    kept_ref[0] = state_low
    carried = mm(c_low, state_low)
    low_lanes = iota((CHUNK, LANES), 1) < HEAD_DIM
    squares = jnp.zeros((CHUNK, LANES), F32)
    for pair in range(width // LANES):
        at = slice(pair * LANES, (pair + 1) * LANES)
        tail_x[:TAIL, at] = tail_x[CHUNK:, at]
        tail_x[TAIL:, at] = x_ref[:, at].astype(F32)
        pre = conv_pre(tail_x, at, taps_ref[:, at], bias_ref[:, at], aux)
        x_conv = pre * jax.nn.sigmoid(pre)
        inputs = x_conv * dt_wide[:, at]
        mats = []
        for head in (2 * pair, 2 * pair + 1):
            gap = log_decay[:, head : head + 1] - log_turned[head : head + 1, :]
            mats.append((jnp.exp(jnp.where(visible, gap, FAR)) * meet).astype(BF16))
        local = mm(jnp.concatenate(mats, 1), halves_rows(inputs.astype(BF16), low_lanes))
        y = local + carried[:, at] * reach[:, at] + skip_ref[:, at] * x_conv
        y_ref[:, at] = y.astype(y_ref.dtype)
        ending_ref[:, at] = (inputs * to_end[:, at]).astype(BF16)
        gate = gate_ref[:, at].astype(F32)
        gated = y * (gate * jax.nn.sigmoid(gate))
        grown = gated * gain_ref[:, at]
        u_ref[:, at] = grown.astype(BF16)
        squares = squares + gated * gated
    state[...] = state[...] * reach[CHUNK - 1 :] + mm(b_turned, ending_ref[...])
    ones = jnp.ones((8, LANES), F32)
    sums = lax.dot_general(
        ones, squares, (((1,), (1,)), ((), ())), precision=PRECISE, preferred_element_type=F32
    )
    sq_ref[...] = sums


def whole(shape):
    return pl.BlockSpec(shape, lambda *_: (0,) * len(shape))


def place_of(chunk, chunks, me_ref):
    part = chunks // 4
    away = chunk // part ^ me_ref[0]
    return (2 * (away % 2) + away // 2) * part + chunk % part


def scan_fwd(me, x_pre, bcdt_pre, gate_pre, side, weights):
    length, width = x_pre.shape
    chunks = length // CHUNK
    aux, seg_rows = side
    at = lambda c, m: (place_of(c, chunks, m), 0)
    tile = lambda columns: pl.BlockSpec((CHUNK, columns), at)
    in_specs = [
        tile(width),
        tile(bcdt_pre.shape[1]),
        tile(width),
        pl.BlockSpec((CHUNK, LANES), lambda c, m: (c, 0)),
        pl.BlockSpec((1, 1, CHUNK), lambda c, m: (c, 0, 0)),
    ] + [whole(w.shape) for w in weights]
    return pl.pallas_call(
        scan_fwd_kernel,
        grid_spec=pltpu.PrefetchScalarGridSpec(
            num_scalar_prefetch=1,
            grid=(chunks,),
            in_specs=in_specs,
            out_specs=[
                tile(width),
                tile(width),
                pl.BlockSpec((8, CHUNK), lambda c, m: (0, c)),
                pl.BlockSpec((1, STATE, width), lambda c, m: (c, 0, 0)),
            ],
            scratch_shapes=[
                pltpu.VMEM((STATE, width), F32),
                pltpu.VMEM((TAIL + CHUNK, width), F32),
                pltpu.VMEM((TAIL + CHUNK, 2 * STATE), F32),
                pltpu.VMEM((CHUNK, width), BF16),
            ],
        ),
        out_shape=[
            jax.ShapeDtypeStruct((length, width), BF16),
            jax.ShapeDtypeStruct((length, width), BF16),
            jax.ShapeDtypeStruct((8, length), F32),
            jax.ShapeDtypeStruct((chunks, STATE, width), BF16),
        ],
        compiler_params=pltpu.CompilerParams(vmem_limit_bytes=VMEM_BYTES),
        cost_estimate=pl.CostEstimate(
            flops=140 * length * width * LANES,
            bytes_accessed=20 * length * width,
            transcendentals=0,
        ),
        name="scan_fwd",
    )(me, x_pre, bcdt_pre, gate_pre, aux, seg_rows, *weights)


def gate_bwd_kernel(
    me_ref, gs_ref, y_ref, gate_ref, col_ref, gain_ref, g_gate_ref, g_y_ref, d_gain_ref
):
    @pl.when(pl.program_id(0) == 0)
    def _():
        d_gain_ref[...] = jnp.zeros_like(d_gain_ref)

    inv = col_ref[:, 0:1]
    pull = col_ref[:, 1:2]
    for pair in range(gs_ref.shape[1] // LANES):
        at = slice(pair * LANES, (pair + 1) * LANES)
        gs = gs_ref[:, at].astype(F32)
        y = y_ref[:, at].astype(F32)
        gate = gate_ref[:, at].astype(F32)
        sig = jax.nn.sigmoid(gate)
        act = gate * sig
        gated = y * act
        grown = gs * inv
        d_gain_ref[:, at] += jnp.sum(grown * gated, 0, keepdims=True)
        g_gated = grown * gain_ref[:, at] - gated * pull
        g_y_ref[:, at] = (g_gated * act).astype(BF16)
        g_gate_ref[:, at] = (g_gated * y * sig * (1.0 + gate * (1.0 - sig))).astype(BF16)


def gate_bwd(me, gs, y, gate_pre, columns, gain):
    length, width = gs.shape
    rows = length // 4
    tile = pl.BlockSpec((rows, width), lambda p, m: (p, 0))
    return pl.pallas_call(
        gate_bwd_kernel,
        grid_spec=pltpu.PrefetchScalarGridSpec(
            num_scalar_prefetch=1,
            grid=(4,),
            in_specs=[
                tile,
                tile,
                tile,
                pl.BlockSpec((rows, columns.shape[1]), lambda p, m: (2 * (p % 2) + p // 2 ^ m[0], 0)),
                whole(gain.shape),
            ],
            out_specs=[tile, tile, whole((1, width))],
        ),
        out_shape=[jax.ShapeDtypeStruct((length, width), BF16)] * 2
        + [jax.ShapeDtypeStruct((1, width), F32)],
        compiler_params=pltpu.CompilerParams(vmem_limit_bytes=VMEM_BYTES),
        cost_estimate=pl.CostEstimate(
            flops=50 * length * width * LANES,
            bytes_accessed=18 * length * width,
            transcendentals=0,
        ),
        name="gate_bwd",
    )(me, gs, y, gate_pre, columns, gain)


def conv_bwd(joined_ref, later_ref, grad, taps, aux, acc_ref, at):
    acc_ref[4:5, at] += jnp.sum(grad, 0, keepdims=True)
    acc_ref[0:1, at] += jnp.sum(grad * joined_ref[TAIL:, at], 0, keepdims=True)
    result = taps[0:1] * grad
    for offset in range(1, 4):
        moved = joined_ref[TAIL - offset : TAIL - offset + CHUNK, at]
        moved = moved * aux[:, offset : offset + 1]
        acc_ref[offset : offset + 1, at] += jnp.sum(grad * moved, 0, keepdims=True)
        later = later_ref[offset : offset + CHUNK, at] * aux[:, 5 + offset : 6 + offset]
        result = result + taps[offset : offset + 1] * later
    return result


def scan_bwd_kernel(
    me_ref,
    g_ref,
    x_ref,
    x_tail_ref,
    bcdt_ref,
    bc_tail_ref,
    kept_ref,
    aux_ref,
    seg_ref,
    taps_ref,
    bias_ref,
    bc_taps_ref,
    bc_bias_ref,
    head_ref,
    skip_ref,
    gain_ref,
    spread_ref,
    gx_ref,
    gbc_ref,
    gdt_ref,
    accx_ref,
    accbc_ref,
    grad_state,
    next_x,
    next_bc,
    joined_x,
    joined_bc,
    conv_ref,
    slope_ref,
    inputs_ref,
    coming_ref,
    ending_ref,
    sums_ref,
):
    width = x_ref.shape[1]

    @pl.when(pl.program_id(0) == 0)
    def _():
        grad_state[...] = jnp.zeros_like(grad_state)
        next_x[...] = jnp.zeros_like(next_x)
        next_bc[...] = jnp.zeros_like(next_bc)
        accx_ref[...] = jnp.zeros_like(accx_ref)
        accbc_ref[...] = jnp.zeros_like(accbc_ref)

    aux = aux_ref[...]
    joined_bc[:TAIL] = bc_tail_ref[:, : 2 * STATE]
    joined_bc[TAIL:] = bcdt_ref[:, : 2 * STATE]
    bc_pre = conv_pre(joined_bc, slice(None), bc_taps_ref[...], bc_bias_ref[...], aux)
    bc_sig = jax.nn.sigmoid(bc_pre)
    bc = bc_pre * bc_sig
    b_low = bc[:, :STATE].astype(BF16)
    c_low = bc[:, STATE:].astype(BF16)
    c_turned = bc[:, STATE:].T.astype(BF16)
    raw, dt, log_decay, row, col = step_values(bcdt_ref[:, 2 * STATE :], head_ref)
    log_turned = log_decay.T
    meet = mm_t(b_low, c_low)
    visible = (aux[:, 0:1] == seg_ref[0]) & (row <= col)
    spread = spread_ref[...]
    dt_wide = expand(dt, spread)
    reach = expand(jnp.exp(log_decay) * aux[:, 4:5], spread)
    to_end = expand(jnp.exp(log_decay[CHUNK - 1 :] - log_decay) * aux[:, 5:6], spread)
    low_lanes = iota((CHUNK, LANES), 1) < HEAD_DIM
    lane = iota((CHUNK, LANES), 1)
    for pair in range(width // LANES):
        at = slice(pair * LANES, (pair + 1) * LANES)
        joined_x[:TAIL, at] = x_tail_ref[:, at].astype(F32)
        joined_x[TAIL:, at] = x_ref[:, at].astype(F32)
        pre = conv_pre(joined_x, at, taps_ref[:, at], bias_ref[:, at], aux)
        sig = jax.nn.sigmoid(pre)
        x_conv = pre * sig
        inputs = x_conv * dt_wide[:, at]
        conv_ref[:, at] = x_conv
        slope_ref[:, at] = sig * (1.0 + pre * (1.0 - sig))
        inputs_ref[:, at] = inputs.astype(BF16)
        ending_ref[:, at] = (inputs * to_end[:, at]).astype(BF16)
        coming_ref[:, at] = (g_ref[:, at].astype(F32) * reach[:, at]).astype(BF16)
    state_low = kept_ref[0]
    grad_state_low = grad_state[...].astype(BF16)
    coming_low = coming_ref[...]
    ending_low = ending_ref[...]
    carried = mm(c_low, state_low)
    leaving = mm(b_low, grad_state_low)
    grad_c = mm_t(coming_low, state_low)
    grad_b = mm_t(ending_low, grad_state_low)
    last = reach[CHUNK - 1 :]
    passed = jnp.sum(grad_state[...] * state_low.astype(F32), 0, keepdims=True) * last
    through = mm_t(jnp.broadcast_to(passed, (8, width)).astype(BF16), spread)
    grad_state[...] = grad_state[...] * last + mm(c_turned, coming_low)
    grad_meet = jnp.zeros((CHUNK, CHUNK), F32)
    col_sums = jnp.zeros((CHUNK, LANES), F32)
    row_sums = jnp.zeros((LANES, CHUNK), F32)
    head_row = iota((LANES, CHUNK), 0)
    for pair in range(width // LANES):
        at = slice(pair * LANES, (pair + 1) * LANES)
        g_low = g_ref[:, at]
        grad_mats = mm_t(halves_rows(inputs_ref[:, at], low_lanes), g_low)
        mats = []
        for member in range(2):
            head = 2 * pair + member
            gap = log_turned[head : head + 1, :] - log_decay[:, head : head + 1]
            weight = jnp.exp(jnp.where(visible, gap, FAR))
            mats.append((weight * meet).astype(BF16))
            part = weight * grad_mats[member * CHUNK : (member + 1) * CHUNK]
            grad_meet = grad_meet + part
            product = part * meet
            col_sums = jnp.where(lane == head, jnp.sum(product, 1, keepdims=True), col_sums)
            row_sums = jnp.where(head_row == head, jnp.sum(product, 0, keepdims=True), row_sums)
        local = mm(jnp.concatenate(mats, 1), halves_rows(g_low, low_lanes))
        g = g_low.astype(F32)
        x_conv = conv_ref[:, at]
        leaving_now = leaving[:, at]
        grad_inputs = local + leaving_now * to_end[:, at]
        sums_ref[:CHUNK, at] = (coming_ref[:, at].astype(F32) * carried[:, at]).astype(BF16)
        sums_ref[CHUNK : 2 * CHUNK, at] = (
            ending_ref[:, at].astype(F32) * leaving_now
        ).astype(BF16)
        sums_ref[2 * CHUNK :, at] = (grad_inputs * x_conv).astype(BF16)
        accx_ref[5:6, at] += jnp.sum(g * x_conv, 0, keepdims=True)
        grad_conv = (grad_inputs * dt_wide[:, at] + g * skip_ref[:, at]) * slope_ref[:, at]
        next_x[CHUNK:, at] = next_x[:TAIL, at]
        next_x[:CHUNK, at] = grad_conv
        gx_ref[:, at] = conv_bwd(
            joined_x, next_x, grad_conv, taps_ref[:, at], aux, accx_ref, at
        ).astype(BF16)
    head_sums = mm_t(sums_ref[...], spread)
    upper = (row <= col).astype(BF16)
    strict = (row > col).astype(BF16)
    straddle = mm(
        jnp.concatenate([upper] * 3 + [strict] * 2, 1),
        jnp.concatenate(
            [
                parts_of(row_sums.T - col_sums + head_sums[:CHUNK], 3),
                parts_of(head_sums[CHUNK : 2 * CHUNK], 2),
            ],
            0,
        ),
    )
    straddle = straddle + through[0:1]
    grad_dt = head_sums[2 * CHUNK :] + head_ref[1:2] * straddle
    grad_raw = jnp.where(lane < GROUP, grad_dt * jax.nn.sigmoid(raw), 0.0)
    gdt_ref[...] = grad_raw.astype(BF16)
    accx_ref[6:7, :LANES] += jnp.sum(grad_raw, 0, keepdims=True)
    accx_ref[7:8, :LANES] += jnp.sum(dt * straddle, 0, keepdims=True)
    grad_meet_low = grad_meet.astype(BF16)
    grad_b = grad_b + mm(grad_meet_low, c_low)
    grad_c = grad_c + t_mm(grad_meet_low, b_low)
    grad_bc = jnp.concatenate([grad_b, grad_c], 1) * (bc_sig * (1.0 + bc_pre * (1.0 - bc_sig)))
    next_bc[CHUNK:] = next_bc[:TAIL]
    next_bc[:CHUNK] = grad_bc
    gbc_ref[...] = conv_bwd(
        joined_bc, next_bc, grad_bc, bc_taps_ref[...], aux, accbc_ref, slice(None)
    ).astype(BF16)


def scan_bwd(me, g_y, x_pre, bcdt_pre, kept, side, weights):
    length, width = x_pre.shape
    chunks = length // CHUNK
    aux, seg_rows = side
    back = lambda c: chunks - 1 - c
    place = lambda c, m: place_of(back(c), chunks, m)
    tile = lambda columns: pl.BlockSpec((CHUNK, columns), lambda c, m: (place(c, m), 0))

    def tail_at(c, m):
        before = place_of(jnp.maximum(back(c) - 1, 0), chunks, m)
        return (before * (CHUNK // TAIL) + CHUNK // TAIL - 1, 0)

    tail = lambda columns: pl.BlockSpec((TAIL, columns), tail_at)
    wide = bcdt_pre.shape[1]
    in_specs = [
        tile(width),
        tile(width),
        tail(width),
        tile(wide),
        tail(wide),
        pl.BlockSpec((1, STATE, width), lambda c, m: (back(c), 0, 0)),
        pl.BlockSpec((CHUNK, LANES), lambda c, m: (back(c), 0)),
        pl.BlockSpec((1, 1, CHUNK), lambda c, m: (back(c), 0, 0)),
    ] + [whole(w.shape) for w in weights]
    return pl.pallas_call(
        scan_bwd_kernel,
        grid_spec=pltpu.PrefetchScalarGridSpec(
            num_scalar_prefetch=1,
            grid=(chunks,),
            in_specs=in_specs,
            out_specs=[
                tile(width),
                tile(2 * STATE),
                tile(LANES),
                whole((8, width)),
                whole((8, 2 * STATE)),
            ],
            scratch_shapes=[
                pltpu.VMEM((STATE, width), F32),
                pltpu.VMEM((TAIL + CHUNK, width), F32),
                pltpu.VMEM((TAIL + CHUNK, 2 * STATE), F32),
                pltpu.VMEM((TAIL + CHUNK, width), F32),
                pltpu.VMEM((TAIL + CHUNK, 2 * STATE), F32),
                pltpu.VMEM((CHUNK, width), F32),
                pltpu.VMEM((CHUNK, width), F32),
                pltpu.VMEM((CHUNK, width), BF16),
                pltpu.VMEM((CHUNK, width), BF16),
                pltpu.VMEM((CHUNK, width), BF16),
                pltpu.VMEM((3 * CHUNK, width), BF16),
            ],
        ),
        out_shape=[
            jax.ShapeDtypeStruct((length, width), BF16),
            jax.ShapeDtypeStruct((length, 2 * STATE), BF16),
            jax.ShapeDtypeStruct((length, LANES), BF16),
            jax.ShapeDtypeStruct((8, width), F32),
            jax.ShapeDtypeStruct((8, 2 * STATE), F32),
        ],
        compiler_params=pltpu.CompilerParams(vmem_limit_bytes=VMEM_BYTES),
        cost_estimate=pl.CostEstimate(
            flops=280 * length * width * LANES,
            bytes_accessed=20 * length * width,
            transcendentals=0,
        ),
        name="scan_bwd",
    )(me, g_y, x_pre, x_pre, bcdt_pre, bcdt_pre, kept, aux, seg_rows, *weights)


def side_arrays(segments):
    length = segments.shape[0]
    seg = segments.astype(F32)
    columns = [seg]
    nothing = lambda count: jnp.full((count,), -1.0, F32)
    for offset in range(1, 4):
        moved = jnp.concatenate([nothing(offset), seg[: length - offset]], 0)
        columns.append((moved == seg).astype(F32))
    blocks = seg.reshape(-1, CHUNK)
    ends = blocks[:, -1]
    before = jnp.concatenate([nothing(1), ends[:-1]], 0)
    columns.append((blocks == before[:, None]).astype(F32).reshape(-1))
    columns.append((blocks == ends[:, None]).astype(F32).reshape(-1))
    for offset in range(1, 4):
        moved = jnp.concatenate([seg[offset:], nothing(offset)], 0)
        columns.append((moved == seg).astype(F32))
    stacked = jnp.stack(columns, 1)
    aux = jnp.pad(stacked, ((0, 0), (0, LANES - stacked.shape[1])))
    return aux, blocks.reshape(-1, 1, CHUNK)


def in_groups(values):
    padded = jnp.pad(values, [(0, 0)] * (values.ndim - 1) + [(0, GROUP - values.shape[-1])])
    return jnp.tile(padded, (1,) * (values.ndim - 1) + (LANES // GROUP,))


def spread_matrix(width):
    head = lax.broadcasted_iota(jnp.int32, (LANES, width), 0) % GROUP
    owner = lax.broadcasted_iota(jnp.int32, (LANES, width), 1) // HEAD_DIM
    return (head == owner).astype(BF16)


def scan_weights(taps, bias, bc_taps, bc_bias, dt_bias, a_log, d_skip, gain, spread):
    rates = -jnp.exp(a_log)
    rows = jnp.stack([in_groups(dt_bias), in_groups(rates)])
    head = jnp.pad(rows, ((0, 6), (0, 0)))
    return (
        taps,
        bias[None],
        bc_taps,
        bc_bias[None],
        head,
        jnp.repeat(d_skip, HEAD_DIM)[None],
        gain[None],
        spread,
    )


def partners(count, step):
    return [(index, index ^ step) for index in range(count)]


def swap(values, axis, step):
    return lax.ppermute(values, axis, partners(lax.axis_size(axis), step))


def after(values, *earlier):
    return lax.optimization_barrier((values, *earlier))[0]


def dp_masks():
    masks = []
    step = lax.axis_size("dp") // 2
    while step > 0:
        masks.append(step)
        step = step // 2
    return masks


def offsets(masks):
    found = [0]
    for mask in masks:
        found = found + [offset ^ mask for offset in found]
    return found


class Rows:
    def __init__(self, own):
        self.rows = own

    def stage(self, mask, *earlier):
        got = swap(after(self.rows, *earlier), "dp", mask)
        self.rows = jnp.concatenate([self.rows, got], 0)
        return got

    def begin(self, masks, *earlier):
        for mask in masks[:-2]:
            got = self.stage(mask, *earlier)
            earlier = ()
        return got


def scatter_first(kept, got):
    total = kept + got.astype(F32)
    height = total.shape[0] // 2
    return total[:height], total[height:].astype(BF16)


def scatter_rest(kept, sent, masks):
    for mask in reversed(masks[1:-1]):
        kept, sent = scatter_first(kept, swap(sent, "dp", mask))
    return kept + swap(sent, "dp", masks[0]).astype(F32)


def grad_half(rows, grads, which):
    width = rows.shape[1] // 2
    dims = (((0,), (0,)), ((), ()))
    taken = rows[:, which * width : (which + 1) * width]
    return lax.dot_general(taken, grads, dims, preferred_element_type=F32)


def sent_half(rows, grads):
    return grad_half(rows, grads, 1).astype(BF16)


def reordered(values, me):
    size = values.shape[0] // 4
    return jnp.concatenate(
        [lax.dynamic_slice_in_dim(values, (away ^ me) * size, size, 0) for away in (0, 2, 1, 3)], 0
    )


def restored(values, me):
    size = values.shape[0] // 4
    parts = []
    for part in range(4):
        away = part ^ me
        parts.append(
            lax.dynamic_slice_in_dim(values, (2 * (away % 2) + away // 2) * size, size, 0)
        )
    return jnp.concatenate(parts, 0)


def turned_over(values, size):
    shaped = values.reshape(-1, 2, size, values.shape[1])
    return shaped[:, ::-1].reshape(values.shape)


def own_quarter(values, me):
    size = values.shape[0] // 4
    return lax.dynamic_slice_in_dim(values, me * size, size, 0)


def tensor_sum(values):
    values = values + swap(values, "tensor", 1)
    return values + swap(values, "tensor", 2)


def dp_sum(values):
    step = 1
    while step < lax.axis_size("dp"):
        values = values + swap(values, "dp", step)
        step = 2 * step
    return values


def dot(lhs, rhs):
    return lax.dot_general(lhs, rhs, (((1,), (0,)), ((), ())), preferred_element_type=F32)


def dot_t(lhs, rhs):
    return lax.dot_general(lhs, rhs, (((1,), (1,)), ((), ())), preferred_element_type=F32)


def own_order(features, masks, earlier):
    place = after(lax.axis_index("dp"), earlier)
    found = offsets(masks)
    height = features // len(found)
    index = lax.broadcasted_iota(jnp.int32, (1, features), 1)
    part, within = index // height, index % height
    away = jnp.zeros_like(part)
    for position, offset in enumerate(found):
        away = jnp.where(part == position, offset, away)
    source = (away ^ place) * height + within
    return (lax.broadcasted_iota(jnp.int32, (features, features), 0) == source).astype(BF16)


def rms_of(stream):
    return lax.rsqrt(jnp.mean(stream * stream, -1, keepdims=True) + EPSILON)


def on_device(
    hidden,
    segments,
    norm_gain,
    w_z,
    w_x,
    w_bc,
    w_dt,
    conv_x_w,
    conv_x_b,
    conv_bc_w,
    conv_bc_b,
    dt_bias,
    a_log,
    d_skip,
    gated_gain,
    w_out,
    cotangent,
):
    length, features = hidden.shape
    width = w_x.shape[2]
    heads = dt_bias.shape[1]
    masks = dp_masks()
    place = lax.axis_index("tensor")
    core, far = place % 2, place // 2
    me = place
    me_row = me.astype(jnp.int32)[None]
    half = length // 2
    quarter = length // 4

    side_first = masks[-1:] + masks[:-1]
    seated = [offsets(side_first).index(offset) for offset in offsets(masks)]
    height = w_x.shape[1]
    quart_bc = w_bc.shape[2] // 4
    own_bc = lax.dynamic_slice_in_dim(w_bc, place * quart_bc, quart_bc, 2)
    w_small = jnp.concatenate([own_bc[0], own_bc[1], w_dt[0], w_dt[1]], 1)
    w_small = jnp.pad(w_small, ((0, 0), (0, 2 * LANES - w_small.shape[1])))

    x0, z0, out0 = Rows(w_x[0]), Rows(w_z[0]), Rows(w_out[0])
    x1, z1, out1 = Rows(w_x[1]), Rows(w_z[1]), Rows(w_out[1])
    small = Rows(w_small)
    near_mask, side_mask = masks[-2:]
    x0_far = x0.begin(masks)
    small_far = small.begin(masks)
    out1_side = out1.stage(side_mask)
    x0_near = x0.stage(near_mask, small_far)
    small_near = small.stage(near_mask, x0_far)
    z0_far = z0.begin(masks, x0_far, small_far)
    small.stage(side_mask)
    x0.stage(side_mask)
    out0_far = out0.begin(masks, x0_near, small_near, z0_far)
    z0_near = z0.stage(near_mask, x0_near, small_near)
    x1_far = x1.begin(masks, z0_near, out0_far)
    out0_near = out0.stage(near_mask, z0_near)
    z0.stage(side_mask)
    z1_far = z1.begin(masks, out0_near, x1_far)
    x1_near = x1.stage(near_mask, out0_near)
    out0.stage(side_mask)
    out1_far = out1.begin(masks, x1_near, z1_far)
    z1_near = z1.stage(near_mask, x1_near)
    x1_side = x1.stage(side_mask)
    out1_near = out1.stage(near_mask, z1_near)
    z1_side = z1.stage(side_mask)
    out1_rows = [out1.rows[seat * height : (seat + 1) * height] for seat in seated]
    x_rows, z_rows = [x0.rows, x1.rows], [z0.rows, z1.rows]
    out_rows = [out0.rows, jnp.concatenate(out1_rows, 0)]
    small_rows = small.rows

    own_cols = small_rows[:, :LANES]
    across = swap(own_cols, "tensor", 2)
    beside = swap(jnp.concatenate([own_cols, across], 1), "tensor", 1)

    def small_columns(layer):
        low = layer * quart_bc
        parts = [
            own_cols[:, low : low + quart_bc],
            across[:, low : low + quart_bc],
            beside[:, low : low + quart_bc],
            beside[:, LANES + low : LANES + low + quart_bc],
        ]
        first = core == 0
        near = [jnp.where(first, parts[0], parts[2]), jnp.where(first, parts[2], parts[0])]
        away = [jnp.where(first, parts[1], parts[3]), jnp.where(first, parts[3], parts[1])]
        first = far == 0
        ordered = [jnp.where(first, n, a) for n, a in zip(near, away)]
        ordered += [jnp.where(first, a, n) for n, a in zip(near, away)]
        at = LANES + layer * heads
        return jnp.concatenate(ordered + [in_groups(small_rows[:, at : at + heads])], 1)

    bcdt_rows = [small_columns(layer) for layer in range(LAYERS)]

    order = lax.optimization_barrier(own_order(features, masks, x0_far))
    side = side_arrays(after(segments, x0_far))
    spread = spread_matrix(width)
    weights = [
        scan_weights(
            conv_x_w[layer],
            conv_x_b[layer],
            conv_bc_w[layer],
            conv_bc_b[layer],
            dt_bias[layer],
            a_log[layer],
            d_skip[layer],
            gated_gain[layer],
            spread,
        )
        for layer in range(LAYERS)
    ]
    order, side, weights = lax.optimization_barrier((order, side, weights))
    hidden_rows = reordered(after(hidden, x0_far), me)
    hidden_low = dot(after(hidden_rows, x0_near, small_near, out1_side), order).astype(BF16)
    cotangent_rows = reordered(after(cotangent, x0_far), me)
    cotangent_low = dot(after(cotangent_rows, hidden_low, z0_near), order).astype(BF16)
    gains = mm(after(norm_gain, small_near), order.astype(F32), PRECISE)
    hidden_low, cotangent_low, gains = lax.optimization_barrier(
        (hidden_low, cotangent_low, gains)
    )

    def columns_of(values, which):
        return lax.dynamic_slice_in_dim(values, which * STATE, STATE, 1)

    stream = hidden_low.astype(F32)
    normed0 = (stream * rms_of(stream) * gains[0]).astype(BF16)
    stream0 = hidden_low[:quarter].astype(F32)
    x_pre0 = dot(normed0, x_rows[0]).astype(BF16)
    bcdt_pre0 = dot(after(normed0, x_pre0, z0_near, out0_far), bcdt_rows[0])
    gate_pre0 = dot(after(normed0, bcdt_pre0, out0_near, x1_far), z_rows[0]).astype(BF16)
    u0, y0, sq, kept0 = scan_fwd(me_row, x_pre0, bcdt_pre0, gate_pre0, side, weights[0])
    u_now = after(u0, x1_near, z1_far)
    sent = dot_t(u_now[half:], out_rows[0]).astype(BF16)
    sq = sq[0:1]
    sq = sq + swap(sq, "tensor", 1)
    u_now = after(u_now, sent, sq)
    mine = dot_t(u_now[:half], out_rows[0]) + swap(sent, "tensor", 1).astype(F32)
    sq = sq + swap(sq, "tensor", 2)
    away = after(mine[quarter:].astype(BF16), sq)
    got = swap(away, "tensor", 2)
    inv0 = lax.rsqrt(sq / INNER + EPSILON)[0]
    got, mine, z1_near, out1_far, x1_side = lax.optimization_barrier(
        (got, mine, z1_near, out1_far, x1_side)
    )
    total0 = mine[:quarter] + got.astype(F32)
    stream1 = stream0 + own_quarter(inv0, me)[:, None] * total0
    normed_own = (stream1 * rms_of(stream1) * gains[1]).astype(BF16)
    normed_half = jnp.concatenate([normed_own, swap(normed_own, "tensor", 2)], 0)
    normed_half, z1_side = lax.optimization_barrier((normed_half, z1_side))
    normed1 = jnp.concatenate([normed_half, swap(normed_half, "tensor", 1)], 0)
    scaled0 = (u0.astype(F32) * reordered(inv0, me)[:, None]).astype(BF16)

    x_pre1 = dot(after(normed1, out1_near), x_rows[1]).astype(BF16)
    bcdt_pre1 = dot(normed1, bcdt_rows[1])
    gate_pre1 = dot(normed1, z_rows[1]).astype(BF16)
    u1, y1, sq, kept1 = scan_fwd(me_row, x_pre1, bcdt_pre1, gate_pre1, side, weights[1])
    scaled_grad1 = dot(cotangent_low, out_rows[1])
    cross = restored(jnp.sum(scaled_grad1 * u1.astype(F32), -1), me)
    scaled_grad1 = scaled_grad1.astype(BF16)
    both = tensor_sum(jnp.stack([sq[0], cross]))
    mixed_sent = dot_t(u1[half:], out_rows[1]).astype(BF16)
    mixed_mine = dot_t(u1[:half], out_rows[1])
    mixed_mine = mixed_mine + swap(mixed_sent, "tensor", 1).astype(F32)
    both = after(both, mixed_sent, mixed_mine)
    mixed_got = swap(mixed_mine[quarter:].astype(BF16), "tensor", 2)
    inv1 = lax.rsqrt(both[0] / INNER + EPSILON)

    columns = jnp.stack([inv1, inv1 * inv1 * inv1 * both[1] / INNER], 1)
    g_gate1, g_y, d_gain1 = gate_bwd(
        me_row, scaled_grad1, y1, gate_pre1, columns, gated_gain[1][None]
    )
    z_sent = sent_half(normed1, g_gate1)
    z_got = swap(z_sent, "dp", 1)
    g_y = after(g_y, z_sent)
    g_x1, g_bc1, g_dt1, acc_x1, acc_bc1 = scan_bwd(
        me_row, g_y, x_pre1, bcdt_pre1, kept1, side, weights[1]
    )
    g_x1, z_got, mixed_got = lax.optimization_barrier((g_x1, z_got, mixed_got))

    def grad_rows(rows, g_gate, g_x, g_bcdt, layer):
        return (
            dot_t(g_gate[rows], z_rows[layer])
            + dot_t(g_x[rows], x_rows[layer])
            + dot_t(g_bcdt[rows], bcdt_rows[layer])
        )

    g_bcdt = jnp.concatenate([g_bc1, g_dt1], 1)
    sent = grad_rows(slice(half, length), g_gate1, g_x1, g_bcdt, 1).astype(BF16)
    cotangent_now = after(cotangent_low, sent)
    scaled1 = (u1.astype(F32) * reordered(inv1, me)[:, None]).astype(BF16)
    out_sent = sent_half(cotangent_now, scaled1)
    out_got = swap(out_sent, "dp", 1)
    own = grad_rows(slice(0, half), after(g_gate1, out_sent), g_x1, g_bcdt, 1)
    mine = own + swap(sent, "tensor", 1).astype(F32)
    away = mine[quarter:].astype(BF16)
    got = swap(away, "tensor", 2)
    normed_now = after(normed1, away)
    z_kept, z_next = scatter_first(grad_half(normed_now, g_gate1, 0), z_got)
    z_near = swap(z_next, "dp", near_mask)
    normed_now = after(normed_now, z_next)
    x_sent = sent_half(normed_now, g_x1)
    x_kept_half = grad_half(normed_now, g_x1, 0)
    out_kept_half = grad_half(after(cotangent_now, away), scaled1, 0)
    mixed_total = mixed_mine[:quarter] + mixed_got.astype(F32)
    last = stream1 + own_quarter(inv1, me)[:, None] * mixed_total
    mixed_own = dot_t(last.astype(BF16), order).astype(BF16)
    got, mine, out_got, z_near, x_sent, out_kept_half, x_kept_half, mixed_own = (
        lax.optimization_barrier(
            (got, mine, out_got, z_near, x_sent, out_kept_half, x_kept_half, mixed_own)
        )
    )
    x_got = swap(x_sent, "dp", 1)
    total = mine[:quarter] + got.astype(F32)
    rms = rms_of(stream1)
    normal = stream1 * rms
    grown = total * gains[1]
    grad_stream = cotangent_low[:quarter].astype(F32) + rms * (
        grown - normal * jnp.mean(grown * normal, -1, keepdims=True)
    )
    grad_own = grad_stream.astype(BF16)
    out_kept, out_next = scatter_first(out_kept_half, out_got)
    out_near = swap(out_next, "dp", near_mask)
    z_kept, z_next = scatter_first(z_kept, z_near)
    z_far = swap(z_next, "dp", masks[-3])
    total_now = after(total, grad_own)
    d_norm1 = jnp.sum(total_now * normal, 0)
    cross = jnp.sum(grad_own.astype(F32) * total0, -1)
    grad_half_rows = jnp.concatenate([grad_own, swap(grad_own, "tensor", 2)], 0)
    cross = jnp.concatenate([cross, swap(cross, "tensor", 2)], 0)
    grad_half_rows, cross, z_far, out_near = lax.optimization_barrier(
        (grad_half_rows, cross, z_far, out_near)
    )
    grad0 = jnp.concatenate([grad_half_rows, swap(grad_half_rows, "tensor", 1)], 0)
    cross = restored(jnp.concatenate([cross, swap(cross, "tensor", 1)], 0), me)
    out_kept, out_next = scatter_first(out_kept, out_near)
    out_far = swap(out_next, "dp", masks[-3])

    grad0 = lax.optimization_barrier(grad0)
    out_sent0 = sent_half(grad0, scaled0)
    out_got0 = swap(out_sent0, "dp", 1)
    scaled_grad0 = dot(after(grad0, out_sent0), out_rows[0]).astype(BF16)
    columns = jnp.stack([inv0, inv0 * inv0 * inv0 * cross / INNER], 1)
    g_gate0, g_y, d_gain0 = gate_bwd(
        me_row, scaled_grad0, y0, gate_pre0, columns, gated_gain[0][None]
    )
    z_sent0 = sent_half(normed0, g_gate0)
    z_got0 = swap(z_sent0, "dp", 1)
    g_y, z_sent0, x_got, out_far = lax.optimization_barrier((g_y, z_sent0, x_got, out_far))
    x_kept, x_next = scatter_first(x_kept_half, x_got)
    x_near = swap(x_next, "dp", near_mask)
    g_y = after(g_y, x_next)
    mixed = lax.all_gather(after(mixed_own, grad0), "tensor", axis=0).reshape(length, features)
    away1 = swap(after(columns_of(g_bc1, 1 - far), grad0), "tensor", 2)
    g_x0, g_bc0, g_dt0, acc_x0, acc_bc0 = scan_bwd(
        me_row, g_y, x_pre0, bcdt_pre0, kept0, side, weights[0]
    )
    away0 = swap(columns_of(g_bc0, 1 - far), "tensor", 2)
    g_x0, away1, x_near, out_got0 = lax.optimization_barrier((g_x0, away1, x_near, out_got0))
    x_sent0 = sent_half(normed0, g_x0)
    x_got0 = swap(x_sent0, "dp", 1)
    g_x0 = after(g_x0, x_sent0)
    g_bcdt = jnp.concatenate([g_bc0, g_dt0], 1)
    sent = grad_rows(slice(half, length), g_gate0, g_x0, g_bcdt, 0).astype(BF16)
    out_kept_half0 = grad_half(after(grad0, sent), scaled0, 0)
    out_kept0, out_next0 = scatter_first(out_kept_half0, out_got0)
    out_near0 = swap(out_next0, "dp", near_mask)
    own = grad_rows(slice(0, half), after(g_gate0, out_next0), g_x0, g_bcdt, 0)
    mine = own + swap(sent, "tensor", 1).astype(F32)
    away = mine[quarter:].astype(BF16)
    got = swap(away, "tensor", 2)
    normed_now, z_got0, x_near, away0, _ = lax.optimization_barrier(
        (normed0, z_got0, x_near, away0, away)
    )
    z_kept0, z_next0 = scatter_first(grad_half(normed_now, g_gate0, 0), z_got0)
    z_near0 = swap(z_next0, "dp", near_mask)
    normed_now = after(normed_now, z_next0)
    x_kept, x_next = scatter_first(x_kept, x_near)
    x_kept_half0 = grad_half(normed_now, g_x0, 0)
    x_kept_half0, out_near0, x_next = lax.optimization_barrier((x_kept_half0, out_near0, x_next))
    x_far = swap(x_next, "dp", masks[-3])
    out_kept0, out_next0 = scatter_first(out_kept0, out_near0)
    out_far0 = swap(out_next0, "dp", masks[-3])
    got, mine, out_next0 = lax.optimization_barrier((got, mine, out_next0))
    total = mine[:quarter] + got.astype(F32)
    rms = rms_of(stream0)
    normal = stream0 * rms
    grown = total * gains[0]
    grad_stream = grad_stream + rms * (
        grown - normal * jnp.mean(grown * normal, -1, keepdims=True)
    )
    d_hidden = dot_t(grad_stream.astype(BF16), order).astype(BF16)
    x_got0, z_near0, _ = lax.optimization_barrier((x_got0, z_near0, d_hidden))
    x_kept0, x_next0 = scatter_first(x_kept_half0, x_got0)
    x_near0 = swap(x_next0, "dp", near_mask)
    x_next0_first = x_next0
    z_kept0, z_next0 = scatter_first(z_kept0, z_near0)
    z_far0 = swap(z_next0, "dp", masks[-3])
    d_hidden = jnp.concatenate([d_hidden, swap(d_hidden, "tensor", 2)], 0)
    d_half = d_hidden
    d_norm0 = jnp.sum(after(total, d_half) * normal, 0)
    d_hidden = jnp.concatenate([d_hidden, swap(d_hidden, "tensor", 1)], 0)
    out_kept, x_kept, z_kept, out_kept0, z_kept0, _ = lax.optimization_barrier(
        (out_kept, x_kept, z_kept, out_kept0, z_kept0, d_half)
    )
    d_hidden = restored(d_hidden, me).astype(F32)

    def finished(kept, sent):
        for mask in reversed(masks[:-3]):
            kept, sent = scatter_first(kept, sent)
            sent = swap(sent, "dp", mask)
        return kept + sent.astype(F32)

    x_kept0, x_next0 = scatter_first(x_kept0, x_near0)
    d_out1 = finished(out_kept, out_far)
    d_x1 = finished(x_kept, x_far)
    d_z1 = finished(z_kept, z_far)
    d_out0 = finished(out_kept0, out_far0)
    d_z0 = finished(z_kept0, z_far0)
    d_x0 = finished(x_kept0, swap(x_next0, "dp", masks[-3]))

    near_cols = jnp.concatenate([columns_of(v, far) for v in (g_bc0, g_bc1)], 1)
    near_cols = after(near_cols, x_next0_first)
    away_cols = jnp.concatenate([away0, away1], 1)
    bc_sum = near_cols.astype(F32) + turned_over(away_cols, quarter).astype(F32)
    across_sum = swap(bc_sum.astype(BF16), "tensor", 1)
    bc_sum = bc_sum + turned_over(across_sum, half).astype(F32)
    small_sent, small_kept = [], []
    for layer, (rows, g_dt) in enumerate(((normed0, g_dt0), (normed1, g_dt1))):
        summed = bc_sum[:, layer * STATE : (layer + 1) * STATE]
        rolled = jnp.roll(summed, STATE // 2, 1)
        own_cols = jnp.where(core == 0, summed, rolled)[:, : STATE // 2].astype(BF16)
        own_cols = jnp.concatenate([own_cols, g_dt[:, : STATE // 2]], 1)
        small_sent.append(sent_half(rows, own_cols))
        small_kept.append(grad_half(rows, own_cols, 0))
    small_sent = after(jnp.concatenate(small_sent, 1), x_got0)
    small_got = swap(small_sent, "dp", 1)
    small_kept, small_next = scatter_first(jnp.concatenate(small_kept, 1), small_got)
    d_small = scatter_rest(small_kept, small_next, masks)
    d_small = jnp.stack([d_small[:, layer * LANES : (layer + 1) * LANES] for layer in range(LAYERS)])
    found = jnp.array(offsets(masks), jnp.int32)
    norm_part = jnp.stack([d_norm0, d_norm1]).reshape(LAYERS, len(found), 1, height)
    here = (found ^ lax.axis_index("dp"))[:, None] == jnp.arange(len(found))[None]
    norm_part = jnp.sum(jnp.where(here[None, :, :, None], norm_part, 0.0), 1)
    shared = jnp.concatenate(
        [acc_bc0, acc_bc1, jnp.zeros((8, width - 4 * STATE), F32)], 1
    )
    shared = tensor_sum(jnp.concatenate([shared, norm_part.reshape(-1, width)], 0))
    gains_part = jnp.concatenate([d_gain0, d_gain1], 0)
    summed = dp_sum(jnp.concatenate([acc_x0, acc_x1, gains_part, shared], 0))
    acc = summed[:16].reshape(LAYERS, 8, width)
    shared = summed[16 + LAYERS :]
    bc_acc = jnp.stack([shared[:8, : 2 * STATE], shared[:8, 2 * STATE : 4 * STATE]])
    d_norm_gain = shared[8:].reshape(LAYERS, features)
    d_skips = acc[:, 5].reshape(LAYERS, heads, HEAD_DIM).sum(2)
    own_width = STATE // 2
    return (
        mixed,
        d_hidden,
        d_norm_gain,
        jnp.stack([d_z0, d_z1]),
        jnp.stack([d_x0, d_x1]),
        d_small[:, :, :own_width],
        d_small[:, :, own_width : own_width + heads],
        acc[:, :4],
        acc[:, 4],
        bc_acc[:, :4],
        bc_acc[:, 4],
        acc[:, 6, :heads],
        acc[:, 7, :heads] * -jnp.exp(a_log),
        d_skips,
        summed[16 : 16 + LAYERS],
        jnp.stack([d_out0, d_out1]),
    )


def solution(mesh):
    in_specs = (
        P("dp", None),
        P("dp"),
        P(),
        P(None, "dp", "tensor"),
        P(None, "dp", "tensor"),
        P(None, "dp", None),
        P(None, "dp", "tensor"),
        P(None, None, "tensor"),
        P(None, "tensor"),
        P(),
        P(),
        P(None, "tensor"),
        P(None, "tensor"),
        P(None, "tensor"),
        P(None, "tensor"),
        P(None, "dp", "tensor"),
        P("dp", None),
    )
    out_specs = (
        P("dp", None),
        P("dp", None),
        P(),
        P(None, "dp", "tensor"),
        P(None, "dp", "tensor"),
        P(None, "dp", "tensor"),
        P(None, "dp", "tensor"),
        P(None, None, "tensor"),
        P(None, "tensor"),
        P(),
        P(),
        P(None, "tensor"),
        P(None, "tensor"),
        P(None, "tensor"),
        P(None, "tensor"),
        P(None, "dp", "tensor"),
    )
    return jax.shard_map(
        on_device, mesh=mesh, in_specs=in_specs, out_specs=out_specs, check_vma=False
    )
```
